32 devices in a mesh: dp: 16 (over z, y, x), tensor: 2 (over core).
Axes of the slice: x: 2, y: 2, z: 4, core: 2. Of those that a mesh axis runs over, the one named last changes fastest.
Arguments:
- hidden_in: bfloat16 [8192, 1536], P(('dp', 'tensor')), may hold values from -6 to 6
- segment_ids: int32 [8192], P('dp'), may hold values from 0 to 31, as said below
- routes: int32 [8192, 4], P('dp'), may hold values from 0 to 7, all different within a row
- slot_order: int32 [16, 2048], P('dp'), may hold values from 0 to 2047, each once within a row
- gain_attn: bfloat16 [1536], P('dp'), may hold values from 0.099609375 to 1.8984375
- w_query: bfloat16 [1536, 1536], P('dp', 'tensor'), may hold values from -0.3125 to 0.3125
- w_key: bfloat16 [1536, 256], P('dp', 'tensor'), may hold values from -0.3125 to 0.3125
- w_value: bfloat16 [1536, 256], P('dp', 'tensor'), may hold values from -0.15625 to 0.15625
- w_out: bfloat16 [1536, 1536], P('tensor', 'dp'), may hold values from -0.625 to 0.625
- gain_ffn: bfloat16 [1536], P('dp'), may hold values from 0.099609375 to 1.8984375
- w_router: bfloat16 [1536, 8], P('dp'), may hold values from -0.078125 to 0.078125
- w_gate: bfloat16 [8, 1536, 768], P(None, 'dp', 'tensor'), may hold values from -0.15625 to 0.15625
- w_up: bfloat16 [8, 1536, 768], P(None, 'dp', 'tensor'), may hold values from -0.15625 to 0.15625
- w_down: bfloat16 [8, 768, 1536], P(None, 'tensor', 'dp'), may hold values from -0.4375 to 0.4375
- grad_out: bfloat16 [8192, 1536], P(('dp', 'tensor')), may hold values from -6 to 6
Outputs:
- layer_out: float32 [8192, 1536], P(('dp', 'tensor'))
- grad_in: float32 [8192, 1536], P(('dp', 'tensor'))
- grad_gain_attn: float32 [1536], P('dp')
- grad_w_query: float32 [1536, 1536], P('dp', 'tensor')
- grad_w_key: float32 [1536, 256], P('dp', 'tensor')
- grad_w_value: float32 [1536, 256], P('dp', 'tensor')
- grad_w_out: float32 [1536, 1536], P('tensor', 'dp')
- grad_gain_ffn: float32 [1536], P('dp')
- grad_w_router: float32 [1536, 8], P('dp')
- grad_w_gate: float32 [8, 1536, 768], P(None, 'dp', 'tensor')
- grad_w_up: float32 [8, 1536, 768], P(None, 'dp', 'tensor')
- grad_w_down: float32 [8, 768, 1536], P(None, 'tensor', 'dp')
The draws below stay inside these ranges and needn't reach their ends.
Inputs may be any that keep to these rules, and one draw needn't show every extreme that they name: `segment_ids`: within each sequence of 512 tokens the ids start at 0, never fall and rise by at most one from token to token; documents never span two sequences.
All inputs are finite; a program needn't handle non-finite values.
Results may differ from the reference program's by a relative error of at most 0.023.
The reference program's roundings to bfloat16 on the way count: a program that leaves them out, or rounds other values in their place, can miss the bound.
Values may be sent and summed in bfloat16 or wider, within the bound.
No kernel may reach another device: no remote copies, remote signals or barrier semaphores. Data moves between devices by JAX's collectives and lax.ppermute only.
A program may use at most 256 MiB of HBM per device.

```python
import math
import jax
import jax.numpy as jnp
from jax import lax

D = 1536
HEADS = 12
KV = 2
HD = 128
H = 768
TOP = 4
E = 8
L = 512
GROUPS = 16
TOKENS = 8192
SLOTS = 2048
CAP = 288


def draw_segment_ids(key, part):
    key = jax.random.fold_in(key, 11)
    key_rate, key_bits, key_width = jax.random.split(key, 3)
    exponent = jax.random.randint(key_rate, (GROUPS, 1), 2, 8)
    rate = jnp.left_shift(jnp.ones_like(exponent), exponent)
    bits = jax.random.randint(key_bits, (GROUPS, L), 0, 1 << 20)
    starts = bits % rate == 0
    half_width = jax.random.randint(key_width, (GROUPS, 1), L // 8, L // 4 + 1)
    positions = jnp.arange(L, dtype=jnp.int32)[None, :]
    forbid = (positions > L // 2 - half_width) & (positions <= L // 2 + half_width)
    starts = starts & jnp.logical_not(forbid) | (positions == 0)
    first_rows = jnp.arange(GROUPS, dtype=jnp.int32)[:, None] == 0
    steady = first_rows & (positions < L // 4) & (positions % 4 == 0)
    starts = starts | steady
    ident = jnp.cumsum(starts.astype(jnp.int32), axis=1) - 1
    ident = jnp.minimum(ident, L // 16 - 1)
    return ident.reshape(-1).astype(jnp.int32)


def raised(entries, own_key, source, target, shards_of, factor):
    def block_of(axis_at):
        return (jnp.arange(entries.shape[axis_at]) // (entries.shape[axis_at] // shards_of)).reshape((-1,) + (1,) * (entries.ndim - 1 - axis_at))

    near = jax.random.permutation(own_key, shards_of)[block_of(target)]
    second = (block_of(target) + shards_of // 2) % shards_of
    return jnp.where((block_of(source) == near) | (block_of(source) == second), factor * entries, entries)


def block_levels(own_key, dims, pieces, smallest, high):
    level = 1.0
    for axis_at, shards_of in pieces:
        steps = jax.random.uniform(jax.random.fold_in(jax.random.fold_in(own_key, 6), axis_at), (shards_of,), jnp.float32, smallest / len(pieces), high / len(pieces))
        level = level * jnp.repeat(jnp.exp(steps), dims[axis_at] // shards_of).reshape((-1,) + (1,) * (len(dims) - 1 - axis_at))
    return level


def picks_of(key, rows, number_of, top, lift):
    sequence = jax.random.permutation(jax.random.fold_in(key, 1), number_of)
    pull = sequence
    for power in range(3):
        pull = pull * pull // number_of
    pull = pull * lift // number_of
    tickets = jax.random.randint(jax.random.fold_in(key, 2), (rows, number_of), 0, 4096) + pull
    sure = jax.random.permutation(jax.random.fold_in(key, 3), rows)[jnp.arange(number_of) % rows]
    tickets = jnp.where(jnp.arange(rows)[:, None] == sure[None, :], 1 << 14, tickets)
    score = tickets * number_of + jnp.arange(number_of)
    return lax.top_k(score.astype(jnp.int32), top)[1].astype(jnp.int32)


def noise(key, dims, deviation, most, cuts=(), kind=jnp.bfloat16):
    values = jax.random.normal(key, dims, jnp.float32) * deviation
    if len(cuts) > 0:
        values = block_levels(key, dims, cuts, -0.22, 0.18) * values
    return jnp.clip(values, min=-most, max=most).astype(kind)


def gaussian_with(own_key, dims, width, reach, cuts, heavy, held_as=jnp.bfloat16):
    values = width * jax.random.normal(own_key, dims, jnp.float32)
    if cuts:
        values = values * block_levels(own_key, dims, cuts, -0.22, 0.18)
    return jnp.clip(raised(values, jax.random.fold_in(own_key, 3), *heavy), -reach, reach).astype(held_as)


def setup_inputs(seed: int = 0) -> dict:
    key_list = jax.random.split(jax.random.key(seed), 16)
    hidden_in = noise(key_list[0], (TOKENS, D), 1.0, 6.0, ((0, 32),))
    segment_ids = draw_segment_ids(jax.random.fold_in(key_list[15], 71), 0)
    routes = picks_of(key_list[2], TOKENS, E, TOP, 4096)
    slot_order = jax.vmap(lambda own: jax.random.permutation(own, SLOTS))(jax.random.split(key_list[3], GROUPS)).reshape((GROUPS, SLOTS)).astype(jnp.int32)
    gain_attn = jnp.clip(1.0 + 0.18 * jax.random.normal(key_list[4], (D,), jnp.float32), 0.099609375, 1.8984375).astype(jnp.bfloat16)
    w_query = noise(key_list[5], (D, HEADS * HD), (D // 4) ** -0.5, 0.3125, ((0, 16), (1, 2)))
    w_key = noise(key_list[6], (D, KV * HD), (D // 4) ** -0.5, 0.3125, ((0, 16), (1, 2)))
    w_value = noise(key_list[7], (D, KV * HD), D ** -0.5, 0.15625, ((0, 16), (1, 2)))
    w_out = noise(key_list[8], (HEADS * HD, D), (HEADS * HD // 16) ** -0.5, 0.625, ((0, 2), (1, 16)))
    gain_ffn = jnp.clip(1.0 + 0.18 * jax.random.normal(key_list[9], (D,), jnp.float32), 0.099609375, 1.8984375).astype(jnp.bfloat16)
    w_router = noise(key_list[10], (D, E), (4 * D) ** -0.5, 0.078125, ((0, 16),))
    w_gate = noise(key_list[11], (E, D, H), D ** -0.5, 0.15625, ((1, 16), (2, 2)))
    w_up = noise(key_list[12], (E, D, H), D ** -0.5, 0.15625, ((1, 16), (2, 2)))
    w_down = noise(key_list[13], (E, H, D), (H // 4) ** -0.5, 0.4375, ((1, 2), (2, 16)))
    grad_out = gaussian_with(key_list[14], (TOKENS, D), 1.0, 6.0, ((0, 32),), (0, 1, 32, 2.75))
    return dict(hidden_in=hidden_in, segment_ids=segment_ids, routes=routes, slot_order=slot_order, gain_attn=gain_attn, w_query=w_query, w_key=w_key, w_value=w_value, w_out=w_out, gain_ffn=gain_ffn, w_router=w_router, w_gate=w_gate, w_up=w_up, w_down=w_down, grad_out=grad_out)


@jax.custom_vjp
def low(v):
    return lax.optimization_barrier(v.astype(jnp.bfloat16)).astype(jnp.float32)

@jax.custom_vjp
def low_back(v):
    return v

def low_keep(v):
    return (low(v), None)

def low_pass(kept, grad):
    return (grad,)

def back_keep(v):
    return (v, None)

def back_low(kept, grad):
    return (low(grad),)
low.defvjp(low_keep, low_pass)
low_back.defvjp(back_keep, back_low)
epsilon = 1e-06
highest = lax.Precision.HIGHEST

def product(left, right):
    return jnp.dot(left, right, precision=highest, preferred_element_type=jnp.float32)

def rms_scale(values):
    return values * lax.rsqrt(lax.optimization_barrier(jnp.mean(values * values, axis=-1, keepdims=True)) + epsilon)

def rope_tables(length, size):
    inverse = 10000.0 ** (-jnp.arange(size // 2, dtype=jnp.float32) / (size // 2))
    angle = jnp.arange(length, dtype=jnp.float32)[:, None] * inverse[None, :]
    return (jnp.cos(angle), jnp.sin(angle))

def rotate(values, cosine, sine_table):
    half_size = values.shape[-1] // 2
    first_half = values[..., :half_size]
    second = values[..., half_size:]
    cos_wide = cosine[:, None, :]
    sin_wide = sine_table[:, None, :]
    return jnp.concatenate([first_half * cos_wide - second * sin_wide, second * cos_wide + first_half * sin_wide], axis=-1)

def queue_slots(route, order_row, experts, capacity):
    length, top_count = route.shape
    slot_count = length * top_count
    flat_routes = route.reshape(-1)
    inverse = jnp.zeros((slot_count,), jnp.int32).at[order_row].set(jnp.arange(slot_count, dtype=jnp.int32))
    ranked = flat_routes[inverse]
    onehot = (ranked[:, None] == jnp.arange(experts, dtype=jnp.int32)[None, :]).astype(jnp.int32)
    before = jnp.cumsum(onehot, axis=0) - onehot
    ranked_pos = lax.optimization_barrier(jnp.sum(before * onehot, axis=1))
    position = ranked_pos[order_row]
    placing = jnp.where(position < capacity, flat_routes * capacity + position, experts * capacity).astype(jnp.int32)
    token_of = jnp.full((experts * capacity + 1,), length, jnp.int32).at[placing].set((jnp.arange(slot_count, dtype=jnp.int32) // top_count).astype(jnp.int32))
    return (placing, token_of[:experts * capacity])

def group_layer(hidden, segment_row, route, order_row, gain_a, query_w, key_w, value_w, out_w, gain_f, router_w, gate_w, upper_w, down_w):
    cosine, sine_table = rope_tables(L, HD)
    normed = low(rms_scale(hidden) * gain_a)
    queries = low_back(product(normed, query_w)).reshape(L, HEADS, HD)
    keys_raw = low_back(product(normed, key_w)).reshape(L, KV, HD)
    values_all = low(low_back(product(normed, value_w))).reshape(L, KV, HD)
    queries = low(rotate(queries, cosine, sine_table))
    keys_all = low(rotate(keys_raw, cosine, sine_table))
    per_group = HEADS // KV
    keys_wide = jnp.repeat(keys_all, per_group, axis=1)
    values_wide = jnp.repeat(values_all, per_group, axis=1)
    scale = 1.0 / math.sqrt(HD)
    scores = low_back(jnp.einsum('qhd,khd->hqk', queries, keys_wide, precision=highest) * scale)
    positions = jnp.arange(L, dtype=jnp.int32)
    allowed = (segment_row[:, None] == segment_row[None, :]) & (positions[None, :] <= positions[:, None])
    scores = jnp.where(allowed[None], scores, -1e+30)
    probabilities = low(jax.nn.softmax(scores, axis=-1))
    mixed = jnp.einsum('hqk,khd->qhd', probabilities, values_wide, precision=highest).reshape(L, HEADS * HD)
    mixed = low(low_back(mixed))
    attn = low_back(product(mixed, out_w))
    middle = hidden + attn
    normed2 = low(rms_scale(middle) * gain_f)
    logits = product(normed2, router_w)
    chosen = jnp.take_along_axis(logits, route, axis=1)
    gate_weights = jax.nn.softmax(chosen, axis=-1)
    placing, token_of = queue_slots(route, order_row, E, CAP)
    padded = jnp.concatenate([normed2, jnp.zeros((1, D), normed2.dtype)], axis=0)
    expert_in = padded[token_of].reshape(E, CAP, D)
    gate_pre = low_back(jnp.einsum('ecd,edh->ech', expert_in, gate_w, precision=highest))
    up_pre = low_back(jnp.einsum('ecd,edh->ech', expert_in, upper_w, precision=highest))
    activated = low(jax.nn.gelu(gate_pre) * up_pre)
    expert_out = low_back(jnp.einsum('ech,ehd->ecd', activated, down_w, precision=highest)).reshape(E * CAP, D)
    out_padded = jnp.concatenate([expert_out, jnp.zeros((1, D), expert_out.dtype)], axis=0)
    picked = out_padded[placing].reshape(L, TOP, D)
    branch = low_back(lax.optimization_barrier(jnp.sum(gate_weights[:, :, None] * picked, axis=1)))
    return middle + branch

def reference(hidden_in, segment_ids, routes, slot_order, gain_attn, w_query, w_key, w_value, w_out, gain_ffn, w_router, w_gate, w_up, w_down, grad_out):
    weights = (gain_attn.astype(jnp.float32), w_query.astype(jnp.float32), w_key.astype(jnp.float32), w_value.astype(jnp.float32), w_out.astype(jnp.float32), gain_ffn.astype(jnp.float32), w_router.astype(jnp.float32), w_gate.astype(jnp.float32), w_up.astype(jnp.float32), w_down.astype(jnp.float32))
    grouped = hidden_in.astype(jnp.float32).reshape(GROUPS, L, D)
    segment_rows = segment_ids.reshape(GROUPS, L)
    route_rows = routes.reshape(GROUPS, L, TOP)

    def whole_layer(inputs, params):

        def one_group(group_item):
            return group_layer(group_item[0], group_item[1], group_item[2], group_item[3], *params)
        return lax.map(jax.checkpoint(one_group), (inputs, segment_rows, route_rows, slot_order))
    result, pullback = jax.vjp(whole_layer, grouped, weights)
    grad_inputs, grad_params = pullback(grad_out.astype(jnp.float32).reshape(GROUPS, L, D))
    return (result.reshape(TOKENS, D), grad_inputs.reshape(TOKENS, D), grad_params[0], grad_params[1], grad_params[2], grad_params[3], grad_params[4], grad_params[5], grad_params[6], grad_params[7], grad_params[8], grad_params[9])
```

```python
import functools
import math

import jax
import jax.numpy as jnp
from jax import lax
from jax.experimental import pallas as pl
from jax.experimental.pallas import tpu as pltpu
from jax.sharding import PartitionSpec as P

HD = 128
EXTRA = 128
CUBE = 8
epsilon = 1e-06
highest = lax.Precision.HIGHEST
f32 = jnp.float32
bf16 = jnp.bfloat16
NN = (((1,), (0,)), ((), ()))
NT = (((1,), (1,)), ((), ()))


def rms_parts(values):
    inverse_root = lax.rsqrt(jnp.mean(values * values, axis=-1, keepdims=True) + epsilon)
    return (values * inverse_root, inverse_root)


def norm_backward(grad_normed, scaled, inverse_root, gain):
    grad_scaled = grad_normed * gain
    inner = jnp.mean(grad_scaled * scaled, axis=-1, keepdims=True)
    return inverse_root * (grad_scaled - scaled * inner)


def rope_tables(length, size):
    inverse = 10000.0 ** (-jnp.arange(size // 2, dtype=f32) / (size // 2))
    angle = jnp.arange(length, dtype=f32)[:, None] * inverse[None, :]
    return (jnp.cos(angle), jnp.sin(angle))


def rotate(values, cosine, sine_table):
    half_size = values.shape[-1] // 2
    first_half = values[..., :half_size]
    second = values[..., half_size:]
    cos_wide = cosine[:, None, :]
    sin_wide = sine_table[:, None, :]
    return jnp.concatenate(
        [first_half * cos_wide - second * sin_wide, second * cos_wide + first_half * sin_wide],
        axis=-1,
    )


def swap(values, bit, count):
    return lax.ppermute(values, "dp", [(i, i ^ bit) for i in range(count)])


def swap_core(values):
    return lax.ppermute(values, "tensor", [(0, 1), (1, 0)])


def thirds(rows):
    unit = 16 if rows % 16 == 0 and rows >= 48 else 1
    part = rows // unit // 3 * unit
    return ((0, rows - 2 * part), (rows - 2 * part, rows - part), (rows - part, rows))


def cut(values, span, axis):
    return lax.slice_in_dim(values, span[0], span[1], axis=axis)


def cube_gather(own, count, axis):
    got = {0: own}
    for bit in (1, 2, 4):
        got[bit] = swap(own, bit, count)
    got[3] = swap(got[2], 1, count)
    got[6] = swap(got[4], 2, count)
    got[5] = swap(got[1], 4, count)
    spans = thirds(own.shape[axis])
    got[7] = (
        swap(cut(got[6], spans[0], axis), 1, count),
        swap(cut(got[5], spans[1], axis), 2, count),
        swap(cut(got[3], spans[2], axis), 4, count),
    )
    return got


def add_round(left, right):
    return (left.astype(f32) + right.astype(f32)).astype(bf16)


def cube_sum(parts, count, axis):
    spans = thirds(parts[0].shape[axis])
    first = swap(cut(parts[7], spans[0], axis), 1, count)
    second = swap(cut(parts[7], spans[1], axis), 2, count)
    third = swap(cut(parts[7], spans[2], axis), 4, count)

    def patched(whole, extra, at):
        pieces = [cut(whole, span, axis) for span in spans]
        pieces[at] = add_round(pieces[at], extra)
        return jnp.concatenate(pieces, axis=axis)

    got2 = swap(patched(parts[3], third, 2), 1, count)
    got4 = swap(patched(parts[6], first, 0), 2, count)
    got1 = swap(patched(parts[5], second, 1), 4, count)
    last = (
        swap(add_round(parts[1], got1), 1, count),
        swap(add_round(parts[2], got2), 2, count),
        swap(add_round(parts[4], got4), 4, count),
    )
    return (
        parts[0].astype(f32) + last[0].astype(f32) + last[1].astype(f32) + last[2].astype(f32)
    )


def outer_bits(count):
    bits, bit = [], CUBE
    while bit < count:
        bits.append(bit)
        bit *= 2
    return bits


def outer_gather(own, count):
    pieces = [own[None]]
    for bit in outer_bits(count):
        pieces.append(swap(jnp.concatenate(pieces, axis=0), bit, count))
    return pieces


def place_kernel(copies, me_ref, *refs):
    out, sems = refs[-2], refs[-1]
    started = []
    for number, (source, entry, start, rows, offset, block) in enumerate(copies):
        target = pl.multiple_of((me_ref[0] ^ offset) * block + start, 16)
        copy = pltpu.make_async_copy(
            refs[source].at[entry], out.at[pl.ds(target, rows)], sems.at[number]
        )
        copy.start()
        started.append(copy)
    for copy in started:
        copy.wait()


def gather_rows(shard, me, count):
    block, width = shard.shape
    own = jnp.concatenate(outer_gather(shard, count), axis=0)
    got = cube_gather(own, count, 1)
    outer = own.shape[0]
    if block % 48:
        got[7] = jnp.concatenate(got[7], axis=1)
        stacked = jnp.stack([got[b] for b in range(CUBE)], axis=1)
        order = jnp.arange(count) ^ me
        return stacked.reshape(count, block, width)[order].reshape(count * block, width)
    sources, copies = [], []
    for b in range(CUBE):
        spans = thirds(block) if b == 7 else ((0, block),)
        for span, piece in zip(spans, got[b] if b == 7 else (got[b],)):
            for j in range(outer):
                copies.append((len(sources), j, span[0], span[1] - span[0], 8 * j + b, block))
            sources.append(piece)
    return pl.pallas_call(
        functools.partial(place_kernel, copies),
        out_shape=jax.ShapeDtypeStruct((count * block, width), shard.dtype),
        in_specs=[pl.BlockSpec(memory_space=pltpu.SMEM)]
        + [pl.BlockSpec(memory_space=pl.ANY)] * len(sources),
        out_specs=pl.BlockSpec(memory_space=pltpu.VMEM),
        scratch_shapes=[pltpu.SemaphoreType.DMA((len(copies),))],
        compiler_params=pltpu.CompilerParams(vmem_limit_bytes=24 * 1024 * 1024),
        name="place_rows",
    )(me.reshape(1), *sources)


def scatter_rows(whole, me, count):
    block = whole.shape[0] // count
    outer = count // CUBE
    offsets = jnp.arange(outer)[None, :] * CUBE + jnp.arange(CUBE)[:, None]
    parts = whole.astype(bf16).reshape(count, block, -1)[(offsets ^ me).reshape(-1)]
    parts = parts.reshape(CUBE, outer, block, -1)
    total = cube_sum([parts[b] for b in range(CUBE)], count, 1)
    for bit in reversed(outer_bits(count)):
        half = total.shape[0] // 2
        total = total[:half] + swap(total[half:].astype(bf16), bit, count).astype(f32)
    return total[0]


def gelu_parts(value):
    square = value * value
    inner = value * (0.7978845608028654 + 0.035677408136300125 * square)
    tanh = jnp.tanh(inner)
    half = 0.5 + 0.5 * tanh
    slope = half + 0.5 * value * (1.0 - tanh * tanh) * (
        0.7978845608028654 + 3.0 * 0.035677408136300125 * square
    )
    return value * half, slope


def moe_kernel(copies, hidden, me_ref, x_ref, g_ref, router_ref, *refs):
    count = len(set(c[0] for c in copies))
    sources = refs[:count]
    (branch_ref, gradn_ref, act_own, act_other, gp_own, gp_other, geo_ref) = refs[count : count + 7]
    weights, sems = refs[count + 7 :]

    @pl.when(pl.program_id(0) == 0)
    def _():
        started = []
        for number, (source, entry, rows, offset, from_col, to_col, cols) in enumerate(copies):
            row = pl.multiple_of(((me_ref[0] // CUBE) ^ offset) * rows, 16)
            copy = pltpu.make_async_copy(
                sources[source].at[entry, :, pl.ds(from_col, cols)],
                weights.at[pl.ds(row, rows), pl.ds(to_col, cols)],
                sems.at[number],
            )
            copy.start()
            started.append(copy)
        for copy in started:
            copy.wait()

    whole = 2 * hidden
    expert = me_ref[0] % CUBE
    x = x_ref[0]
    code = g_ref[0, :, x.shape[1] :].astype(f32)
    lanes = lax.broadcasted_iota(jnp.int32, code.shape, 1)
    logits = lax.dot_general(x, router_ref[...], NN, preferred_element_type=f32)
    routed = code > 0.5
    logits = jnp.where(routed, logits, -1e30)
    expo = jnp.where(routed, jnp.exp(logits - jnp.max(logits, axis=1, keepdims=True)), 0.0)
    gates = expo / jnp.sum(expo, axis=1, keepdims=True)
    kept = (lanes == expert) & (code > 1.5)
    gate = jnp.sum(jnp.where(kept, gates, 0.0), axis=1, keepdims=True)

    pre = lax.dot_general(x, weights[:, : 2 * whole], NN, preferred_element_type=f32)
    gate_pre, up_pre = pre[:, :whole], pre[:, whole:]
    gelu, slope = gelu_parts(gate_pre)
    act = (gelu * up_pre).astype(bf16)
    act_own[0] = act[:, :hidden]
    act_other[0] = act[:, hidden:]
    down = weights[:, 2 * whole :]
    expert_out = lax.dot_general(act, down, NT, preferred_element_type=f32)
    branch_ref[0] = (gate * expert_out).astype(bf16)
    g = g_ref[0, :, : x.shape[1]].astype(f32)
    grad_gate = jnp.sum(g * expert_out, axis=1, keepdims=True)
    gradn_ref[0, :, x.shape[1] :] = jnp.where(kept, grad_gate, 0.0).astype(bf16)
    geo = (gate * g).astype(bf16)
    geo_ref[0] = geo
    grad_act = lax.dot_general(geo, down, NN, preferred_element_type=f32)
    grad_gate_pre = (grad_act * up_pre * slope).astype(bf16)
    grad_up_pre = (grad_act * gelu).astype(bf16)
    gp_own[0, :, :hidden] = grad_gate_pre[:, :hidden]
    gp_own[0, :, hidden:] = grad_up_pre[:, :hidden]
    gp_other[0, :, :hidden] = grad_gate_pre[:, hidden:]
    gp_other[0, :, hidden:] = grad_up_pre[:, hidden:]
    grad_in = lax.dot_general(
        grad_gate_pre, weights[:, :whole], NT, preferred_element_type=f32
    ) + lax.dot_general(
        grad_up_pre, weights[:, whole : 2 * whole], NT, preferred_element_type=f32
    )
    gradn_ref[0, :, : x.shape[1]] = grad_in.astype(bf16)


def moe(me, x, g, router, pieces, hidden):
    blocks, rows, width = x.shape
    copies = []
    for source, (array, first, side) in enumerate(pieces):
        for entry in range(array.shape[0]):
            for kind in range(3):
                copies.append(
                    (
                        source,
                        entry,
                        array.shape[1],
                        first + entry,
                        kind * hidden,
                        (2 * kind + side) * hidden,
                        hidden,
                    )
                )

    def block(cols):
        return pl.BlockSpec((1, rows, cols), lambda b, me: (b, 0, 0))

    def out(cols):
        return jax.ShapeDtypeStruct((blocks, rows, cols), bf16)

    widths = (width, width + EXTRA, hidden, hidden, 2 * hidden, 2 * hidden, width)
    flops = 2 * blocks * rows * width * hidden * 12
    return pl.pallas_call(
        functools.partial(moe_kernel, copies, hidden),
        out_shape=[out(w) for w in widths],
        grid_spec=pltpu.PrefetchScalarGridSpec(
            num_scalar_prefetch=1,
            grid=(blocks,),
            in_specs=[
                block(width),
                block(width + EXTRA),
                pl.BlockSpec((width, EXTRA), lambda b, me: (0, 0)),
            ]
            + [pl.BlockSpec(memory_space=pl.ANY)] * len(pieces),
            out_specs=[block(w) for w in widths],
            scratch_shapes=[
                pltpu.VMEM((width, 6 * hidden), bf16),
                pltpu.SemaphoreType.DMA((len(copies),)),
            ],
        ),
        compiler_params=pltpu.CompilerParams(vmem_limit_bytes=60 * 1024 * 1024),
        cost_estimate=pl.CostEstimate(flops=flops, bytes_accessed=50_000_000, transcendentals=0),
        name="experts",
    )(me.reshape(1), x, g, router, *[p[0] for p in pieces])


def per_device(
    count,
    hidden_in,
    segment_ids,
    routes,
    slot_order,
    gain_attn,
    w_query,
    w_key,
    w_value,
    w_out,
    gain_ffn,
    w_router,
    w_gate,
    w_up,
    w_down,
    grad_out,
):
    tok_rows, width = hidden_in.shape
    seq_len = segment_ids.shape[0]
    top_count = routes.shape[1]
    experts, block, hidden = w_gate.shape
    capacity = 9 * seq_len * top_count // (8 * experts)
    me = lax.axis_index("dp").astype(jnp.int32)
    core = lax.axis_index("tensor").astype(jnp.int32)
    groups = [list(range(at, at + CUBE)) for at in range(0, count, CUBE)]

    def both_halves(mine):
        other = swap_core(mine)
        return jnp.where(
            core == 0,
            jnp.concatenate([mine, other], axis=0),
            jnp.concatenate([other, mine], axis=0),
        )

    expert_shard = jnp.concatenate([w_gate, w_up, jnp.swapaxes(w_down, 1, 2)], axis=2)
    expert_rows = lax.all_to_all(
        expert_shard.reshape(experts * block, 3 * hidden),
        "dp",
        0,
        0,
        tiled=True,
        axis_index_groups=groups,
    )

    small = jnp.concatenate([gain_attn[:, None], gain_ffn[:, None], w_router], axis=1)
    small = jnp.pad(small, ((0, 0), (0, EXTRA - small.shape[1])))
    shard_qkv = jnp.concatenate([w_query, w_key, w_value, small], axis=1)
    full_qkv = gather_rows(shard_qkv, me, count)
    out_wt = gather_rows(w_out.T, me, count)
    heads_cols, kv_cols = w_query.shape[1], w_key.shape[1]
    qkv_cols = heads_cols + 2 * kv_cols
    query_w = full_qkv[:, :heads_cols]
    key_w = full_qkv[:, heads_cols : heads_cols + kv_cols]
    value_w = full_qkv[:, heads_cols + kv_cols : qkv_cols]
    gain_af = full_qkv[:, qkv_cols].astype(f32)
    gain_ff = full_qkv[:, qkv_cols + 1].astype(f32)
    router_w = full_qkv[:, qkv_cols + 2 : qkv_cols + 2 + experts]
    router_pad = jnp.pad(router_w, ((0, 0), (0, EXTRA - experts)))

    order = jnp.min(
        jnp.where(
            routes[:, :, None] == jnp.arange(experts, dtype=jnp.int32),
            slot_order[0].reshape(seq_len, top_count)[:, :, None],
            seq_len * top_count,
        ),
        axis=1,
    )
    order_own = lax.dynamic_slice_in_dim(order, core * tok_rows, tok_rows, 0)
    ahead = jnp.sum((order[None, :, :] < order_own[:, None, :]).astype(jnp.int32), axis=1)
    routed_own = order_own < seq_len * top_count
    kept_own = routed_own & (ahead < capacity)
    code_own = routed_own.astype(bf16) + kept_own.astype(bf16)
    code_own = jnp.pad(code_own, ((0, 0), (0, EXTRA - experts)))

    hidden_full = both_halves(hidden_in).astype(f32)
    scaled_full, _ = rms_parts(hidden_full)
    scaled_in, root_in = rms_parts(hidden_in.astype(f32))
    normed = (scaled_full * gain_af).astype(bf16)
    head_count = heads_cols // HD
    kv_local = kv_cols // HD
    per_group = head_count // kv_local
    cosine, sine_table = rope_tables(seq_len, HD)
    qkv = jnp.dot(normed, full_qkv[:, :qkv_cols], preferred_element_type=f32)
    query_f = qkv[:, :heads_cols].reshape(seq_len, head_count, HD)
    key_f = qkv[:, heads_cols : heads_cols + kv_cols].reshape(seq_len, kv_local, HD)
    value_r = qkv[:, heads_cols + kv_cols :].astype(bf16).reshape(seq_len, kv_local, HD)
    query_r = rotate(query_f, cosine, sine_table).astype(bf16)
    key_r = rotate(key_f, cosine, sine_table).astype(bf16)
    query_g = query_r.reshape(seq_len, kv_local, per_group, HD)
    scale = 1.0 / math.sqrt(HD)
    positions = jnp.arange(seq_len, dtype=jnp.int32)

    def block_scores():
        raw = jnp.einsum("qgrd,kgd->grqk", query_g, key_r, preferred_element_type=f32) * scale
        allowed = (segment_ids[:, None] == segment_ids[None, :]) & (
            positions[None, :] <= positions[:, None]
        )
        return jnp.where(allowed[None, None], raw, -1e30)

    masked = block_scores()
    peak = jnp.max(masked, axis=-1, keepdims=True)
    expo_vals = jnp.exp(masked - peak)
    total = jnp.sum(expo_vals, axis=-1, keepdims=True)
    probabilities = (expo_vals / total).astype(bf16)
    mixed_block = jnp.einsum("grqk,kgd->qgrd", probabilities, value_r, preferred_element_type=f32)
    mixed = mixed_block.reshape(seq_len, head_count * HD).astype(bf16)
    lse = peak + jnp.log(total)
    attn_part = jnp.einsum("qc,dc->qd", mixed, out_wt, preferred_element_type=f32)

    def sum_cores(part):
        mine = lax.dynamic_slice_in_dim(part, core * tok_rows, tok_rows, 0)
        other = lax.dynamic_slice_in_dim(part, (1 - core) * tok_rows, tok_rows, 0)
        return mine + swap_core(other.astype(bf16)).astype(f32)

    middle = hidden_in.astype(f32) + sum_cores(attn_part)
    scaled_mid, root_mid = rms_parts(middle)
    normed2 = (scaled_mid * gain_ff).astype(bf16)

    def stacked(got):
        return jnp.stack([got[b] for b in range(7)] + [jnp.concatenate(got[7], axis=0)], axis=0)

    grads_cube = stacked(
        cube_gather(jnp.concatenate([grad_out, code_own], axis=1), count, 0)
    )
    normed_cube = stacked(cube_gather(normed2, count, 0))
    pieces, first = [], 0
    for array in outer_gather(expert_rows, count):
        pieces.append((array, first, 0))
        pieces.append((swap_core(array), first, 1))
        first += array.shape[0]
    branch, gradn, act_own, act_other, gp_own, gp_other, geo = moe(
        me, normed_cube, grads_cube, router_pad, pieces, hidden
    )
    gradn_sum = cube_sum([gradn[b] for b in range(CUBE)], count, 0)
    branch_sum = cube_sum([branch[b] for b in range(CUBE)], count, 0)
    layer_out = middle + branch_sum

    def flat(values):
        return values.reshape(-1, values.shape[-1])

    def weight_grads(gp, act):
        return jnp.concatenate(
            [
                jnp.einsum("td,th->dh", flat(normed_cube), flat(gp), preferred_element_type=f32),
                jnp.einsum("td,th->dh", flat(geo), flat(act), preferred_element_type=f32),
            ],
            axis=1,
        ).astype(bf16)

    expert_grads = weight_grads(gp_own, act_own).astype(f32) + swap_core(
        weight_grads(gp_other, act_other)
    ).astype(f32)
    for bit in reversed(outer_bits(count)):
        half = expert_grads.shape[0] // 2
        high = (me // bit) % 2
        keep = lax.dynamic_slice_in_dim(expert_grads, high * half, half, 0)
        send = lax.dynamic_slice_in_dim(expert_grads, (1 - high) * half, half, 0)
        expert_grads = keep + swap(send.astype(bf16), bit, count).astype(f32)
    expert_grads = (
        lax.all_to_all(
            expert_grads.astype(bf16), "dp", 0, 0, tiled=True, axis_index_groups=groups
        )
        .reshape(experts, block, 3 * hidden)
        .astype(f32)
    )
    grad_gate_w = expert_grads[:, :, :hidden]
    grad_up_w = expert_grads[:, :, hidden : 2 * hidden]
    grad_down_w = jnp.swapaxes(expert_grads[:, :, 2 * hidden :], 1, 2)

    logits = jnp.dot(normed2, router_w, preferred_element_type=f32)
    logits = jnp.where(routed_own, logits, -1e30)
    expo = jnp.where(routed_own, jnp.exp(logits - jnp.max(logits, axis=1, keepdims=True)), 0.0)
    gates = expo / jnp.sum(expo, axis=1, keepdims=True)
    grad_gates = gradn_sum[:, width : width + experts]
    grad_logits = gates * (grad_gates - jnp.sum(gates * grad_gates, axis=1, keepdims=True))
    grad_normed2 = gradn_sum[:, :width] + jnp.einsum(
        "te,de->td", grad_logits, router_w.astype(f32), precision=highest
    )
    grad_router = jnp.einsum("td,te->de", normed2.astype(f32), grad_logits, precision=highest)
    grad_gain_f = jnp.sum(grad_normed2 * scaled_mid, axis=0)
    grad_middle = grad_out.astype(f32) + norm_backward(
        grad_normed2, scaled_mid, root_mid, gain_ff
    )

    grad_mid_full = both_halves(grad_middle.astype(bf16))
    grad_out_wt = jnp.einsum("qd,qc->dc", grad_mid_full, mixed, preferred_element_type=f32)
    small_f = jnp.concatenate([grad_gain_f[:, None], grad_router], axis=1)
    small_f = jnp.pad(small_f, ((0, 0), (0, EXTRA - small_f.shape[1]))).astype(bf16)
    small_f = small_f.astype(f32) + swap_core(small_f).astype(f32)
    out_grads = scatter_rows(
        jnp.concatenate([grad_out_wt, small_f], axis=1).astype(bf16), me, count
    )
    grad_mixed = jnp.dot(grad_mid_full, out_wt, preferred_element_type=f32)
    grad_mixed = grad_mixed.astype(bf16).reshape(seq_len, kv_local, per_group, HD)
    probs_float = jnp.exp(block_scores() - lse)
    probs_r = probs_float.astype(bf16)
    grad_probs = jnp.einsum("qgrd,kgd->grqk", grad_mixed, value_r, preferred_element_type=f32)
    inner = jnp.sum(grad_probs * probs_float, axis=-1, keepdims=True)
    grad_scores = (probs_float * (grad_probs - inner)).astype(bf16)
    grad_query = (
        jnp.einsum("grqk,kgd->qgrd", grad_scores, key_r, preferred_element_type=f32) * scale
    )
    grad_key = (
        jnp.einsum("grqk,qgrd->kgd", grad_scores, query_g, preferred_element_type=f32) * scale
    )
    grad_value = jnp.einsum("grqk,qgrd->kgd", probs_r, grad_mixed, preferred_element_type=f32)
    grad_query = rotate(grad_query.reshape(seq_len, head_count, HD), cosine, -sine_table)
    grad_key = rotate(grad_key, cosine, -sine_table)
    grad_qkv = jnp.concatenate(
        [
            grad_query.astype(bf16).reshape(seq_len, heads_cols),
            grad_key.astype(bf16).reshape(seq_len, kv_cols),
            grad_value.astype(bf16).reshape(seq_len, kv_cols),
        ],
        axis=1,
    )
    grad_qkv_w = jnp.einsum("qd,qc->dc", normed, grad_qkv, preferred_element_type=f32)
    grad_normed_part = jnp.einsum(
        "qc,dc->qd", grad_qkv, full_qkv[:, :qkv_cols], preferred_element_type=f32
    )
    grad_gain_a = jnp.sum(grad_normed_part * scaled_full, axis=0)
    grad_gain_a = grad_gain_a + swap_core(grad_gain_a)
    small_a = jnp.pad(grad_gain_a[:, None], ((0, 0), (0, EXTRA - 1)))
    qkv_grads = scatter_rows(
        jnp.concatenate([grad_qkv_w, small_a], axis=1).astype(bf16), me, count
    )
    grad_normed = sum_cores(grad_normed_part)
    grad_in = grad_middle + norm_backward(grad_normed, scaled_in, root_in, gain_af)
    return (
        layer_out,
        grad_in,
        qkv_grads[:, qkv_cols],
        qkv_grads[:, :heads_cols],
        qkv_grads[:, heads_cols : heads_cols + kv_cols],
        qkv_grads[:, heads_cols + kv_cols : qkv_cols],
        out_grads[:, :heads_cols].T,
        out_grads[:, heads_cols],
        out_grads[:, heads_cols + 1 : heads_cols + 1 + experts],
        grad_gate_w,
        grad_up_w,
        grad_down_w,
    )


def solution(mesh):
    return jax.shard_map(
        functools.partial(per_device, mesh.shape["dp"]),
        mesh=mesh,
        in_specs=(
            P(("dp", "tensor"), None),
            P("dp"),
            P("dp", None),
            P("dp", None),
            P("dp"),
            P("dp", "tensor"),
            P("dp", "tensor"),
            P("dp", "tensor"),
            P("tensor", "dp"),
            P("dp"),
            P("dp", None),
            P(None, "dp", "tensor"),
            P(None, "dp", "tensor"),
            P(None, "tensor", "dp"),
            P(("dp", "tensor"), None),
        ),
        out_specs=(
            P(("dp", "tensor"), None),
            P(("dp", "tensor"), None),
            P("dp"),
            P("dp", "tensor"),
            P("dp", "tensor"),
            P("dp", "tensor"),
            P("tensor", "dp"),
            P("dp"),
            P("dp", None),
            P(None, "dp", "tensor"),
            P(None, "dp", "tensor"),
            P(None, "tensor", "dp"),
        ),
        check_vma=False,
    )
```

```python
import functools
import math

import jax
import jax.numpy as jnp
from jax import lax
from jax.experimental import pallas as pl
from jax.experimental.pallas import tpu as pltpu
from jax.sharding import PartitionSpec as P

HD = 128
EXTRA = 128
GAIN_A, GAIN_F = 8, 9
CUBE = 8
BRIEF = pl.CostEstimate(flops=0, bytes_accessed=3_000_000, transcendentals=0)
epsilon = 1e-06
highest = lax.Precision.HIGHEST
f32 = jnp.float32
bf16 = jnp.bfloat16
NN = (((1,), (0,)), ((), ()))
NT = (((1,), (1,)), ((), ()))
TN = (((0,), (0,)), ((), ()))


def rms_parts(values):
    inverse_root = lax.rsqrt(jnp.mean(values * values, axis=-1, keepdims=True) + epsilon)
    return (values * inverse_root, inverse_root)


def norm_backward(grad_normed, scaled, inverse_root, gain):
    grad_scaled = grad_normed * gain
    inner = jnp.mean(grad_scaled * scaled, axis=-1, keepdims=True)
    return inverse_root * (grad_scaled - scaled * inner)


def rope_tables(length, size):
    inverse = 10000.0 ** (-jnp.arange(size // 2, dtype=f32) / (size // 2))
    angle = jnp.arange(length, dtype=f32)[:, None] * inverse[None, :]
    return (jnp.cos(angle), jnp.sin(angle))


def swap(values, bit, count):
    return lax.ppermute(values, "dp", [(i, i ^ bit) for i in range(count)])


def swap_core(values):
    return lax.ppermute(values, "tensor", [(0, 1), (1, 0)])


def gate(values, *events):
    values = list(values)
    flat = jax.tree.leaves(events)
    return pl.pallas_call(
        lambda *refs: None,
        out_shape=[jax.ShapeDtypeStruct(v.shape, v.dtype) for v in values],
        in_specs=[pl.BlockSpec(memory_space=pl.ANY)] * (len(values) + len(flat)),
        out_specs=[pl.BlockSpec(memory_space=pl.ANY)] * len(values),
        input_output_aliases={i: i for i in range(len(values))},
        compiler_params=pltpu.CompilerParams(vmem_limit_bytes=60 * 1024 * 1024),
        cost_estimate=BRIEF,
        name="gate",
    )(*values, *flat)


def gate_dict(got, keys, *events):
    return got | dict(zip(keys, gate([got[k] for k in keys], *events)))


def halves(rows):
    part = rows // 2
    return ((0, part), (part, rows))


def cut(values, span, axis):
    return lax.slice_in_dim(values, span[0], span[1], axis=axis)


NEAR, FAR, LAST = (1, 2, 4), (3, 6, 5), (7, 8)


def add_round(left, right):
    return (left.astype(f32) + right.astype(f32)).astype(bf16)


def sum_last(parts, count):
    return {7: swap(parts[7], 1, count), 8: swap(parts[8], 2, count)}


def patch_kernel(first, second, low, high, first_out, second_out):
    first_out[...] = (first[...].astype(f32) + low[...].astype(f32)).astype(bf16)
    second_out[...] = (second[...].astype(f32) + high[...].astype(f32)).astype(bf16)


def patch(first, second, low, high):
    shape = first.shape
    half = low.shape
    if half[-2] % 16:
        return (
            jnp.concatenate([add_round(first[..., : half[-2], :], low), first[..., half[-2] :, :]], -2),
            jnp.concatenate([second[..., : half[-2], :], add_round(second[..., half[-2] :, :], high)], -2),
        )
    lead = (0,) * (len(shape) - 2)
    top = pl.BlockSpec(half, lambda i: lead + (0, 0))
    bottom = pl.BlockSpec(half, lambda i: lead + (1, 0))
    return pl.pallas_call(
        patch_kernel,
        grid=(1,),
        out_shape=[jax.ShapeDtypeStruct(shape, bf16)] * 2,
        in_specs=[top, bottom, top, top],
        out_specs=[top, bottom],
        input_output_aliases={0: 0, 1: 1},
        compiler_params=pltpu.CompilerParams(vmem_limit_bytes=60 * 1024 * 1024),
        cost_estimate=BRIEF,
        name="patch",
    )(first, second, low, high)


def far_terms(parts, got):
    return patch(parts[6], parts[5], got[7], got[8])


def sum_far(parts, terms, count):
    first, second = terms
    return {4: swap(first, 2, count), 1: swap(second, 4, count), 2: swap(parts[3], 1, count)}


def terms_kernel(*refs):
    for k in range(3):
        refs[6 + k][...] = (refs[k][...].astype(f32) + refs[3 + k][...].astype(f32)).astype(bf16)


def near_terms(parts, got):
    args = [parts[bit] for bit in NEAR] + [got[bit] for bit in NEAR]
    shape = parts[1].shape
    grid = 4 if shape[-2] % 64 == 0 else 1
    block = shape[:-2] + (shape[-2] // grid, shape[-1])
    lead = (0,) * (len(shape) - 2)
    spec = pl.BlockSpec(block, lambda i: lead + (i, 0))
    outs = pl.pallas_call(
        terms_kernel,
        grid=(grid,),
        out_shape=[jax.ShapeDtypeStruct(shape, bf16)] * 3,
        in_specs=[spec] * 6,
        out_specs=[spec] * 3,
        compiler_params=pltpu.CompilerParams(vmem_limit_bytes=60 * 1024 * 1024),
        cost_estimate=BRIEF,
        name="terms",
    )(*args)
    return dict(zip(NEAR, outs))


def sum_near(terms, count):
    return {bit: swap(terms[bit], bit, count) for bit in NEAR}


def sum_own(parts, got):
    return parts[0].astype(f32) + (
        got[1].astype(f32) + (got[2].astype(f32) + got[4].astype(f32))
    )


def outer_bits(count):
    bits, bit = [], CUBE
    while bit < count:
        bits.append(bit)
        bit *= 2
    return bits


def outer_gather(own, count):
    pieces = [own[None]]
    for bit in outer_bits(count):
        pieces.append(swap(jnp.concatenate(pieces, axis=0), bit, count))
    return pieces


def outer_pair(shard, count):
    return jnp.concatenate(outer_gather(shard, count), axis=0)


def piece_copies(got, block, me, count):
    if block % 32:
        stacked = jnp.stack(
            [got[b] for b in range(7)] + [jnp.concatenate([got[b] for b in LAST], axis=1)],
            axis=1,
        )
        whole = stacked.reshape(count, block, -1)[jnp.arange(count) ^ me]
        return [whole.reshape(1, count * block, -1)], [(0, 0, 0, count * block, None, block)]
    sources, copies = [], []
    spans = [(0, block)] * 7 + list(halves(block))
    for b, span in enumerate(spans):
        for j in range(got[b].shape[0]):
            copies.append((b, j, span[0], span[1] - span[0], 8 * j + min(b, 7), block))
        sources.append(got[b])
    return sources, copies


def lay_rows(copies, sources, targets, sems, me):
    started = []
    for number, (source, entry, start, rows, offset, block) in enumerate(copies):
        row = 0 if offset is None else pl.multiple_of((me ^ offset) * block + start, 16)
        column = 0
        for k, target in enumerate(targets):
            cols = target.shape[1]
            copy = pltpu.make_async_copy(
                sources[source].at[entry, :, pl.ds(column, cols)],
                target.at[pl.ds(row, rows)],
                sems.at[len(targets) * number + k],
            )
            copy.start()
            started.append(copy)
            column += cols
    for copy in started:
        copy.wait()


def part_order(block):
    return [(b, (0, block)) for b in range(7)] + [(7, span) for span in halves(block)]


def part_shapes(count, block, width):
    if block % 32:
        return [jax.ShapeDtypeStruct((count * block, width), bf16)]
    return [
        jax.ShapeDtypeStruct((count // CUBE, span[1] - span[0], width), bf16)
        for _, span in part_order(block)
    ]


def store_parts(whole, parts, me, block, at):
    cols = pl.ds(at, whole.shape[1])
    if len(parts) == 1:
        parts[0][:, cols] = whole[...].astype(bf16)
        return
    for part, (offset, span) in zip(parts, part_order(block)):
        for j in range(part.shape[0]):
            row = pl.multiple_of((me ^ (8 * j + offset)) * block + span[0], 16)
            part[j, :, cols] = whole[pl.ds(row, span[1] - span[0])].astype(bf16)


def spread_parts(parts, me, count):
    if len(parts) > 1:
        return dict(enumerate(parts))
    block = parts[0].shape[0] // count
    outer = jnp.arange(count // CUBE) * CUBE
    blocks = parts[0].reshape(count, block, -1)
    return {
        k: cut(blocks[(offset + outer) ^ me], span, 1)
        for k, (offset, span) in enumerate(part_order(block))
    }


def outer_sum(total, count):
    for bit in reversed(outer_bits(count)):
        half = total.shape[0] // 2
        total = total[:half] + swap(total[half:].astype(bf16), bit, count).astype(f32)
    return total[0]


def vmem_call(kernel, out_shapes, scratch, args, name, smem=(), flops=0):
    spaces = {0: pltpu.VMEM, 1: pltpu.SMEM, 2: pl.ANY}
    moved = sum(math.prod(o.shape) * o.dtype.itemsize for o in out_shapes)
    moved += sum(math.prod(a.shape) * a.dtype.itemsize for a, _ in args)
    return pl.pallas_call(
        kernel,
        out_shape=out_shapes,
        in_specs=[pl.BlockSpec(memory_space=spaces[space]) for _, space in args],
        out_specs=[pl.BlockSpec(memory_space=pltpu.VMEM)] * len(out_shapes),
        scratch_shapes=scratch,
        compiler_params=pltpu.CompilerParams(vmem_limit_bytes=60 * 1024 * 1024),
        cost_estimate=BRIEF,
        name=name,
    )(*[a for a, _ in args])


def turn(values, cosine, sine):
    return values * cosine + pltpu.roll(values, values.shape[1] // 2, 1) * sine


def masks(seg_col, seg_row, splits):
    out = []
    for low, high in splits:
        shape = (high - low, high)
        query_at = lax.broadcasted_iota(jnp.int32, shape, 0) + low
        key_at = lax.broadcasted_iota(jnp.int32, shape, 1)
        allowed = (seg_col[low:high] == seg_row[:, :high]) & (key_at <= query_at)
        out.append(jnp.where(allowed, 0.0, -1e30))
    return out


def row_splits(length):
    return [(at, at + length // 2) for at in (0, length // 2)]


def attend_kernel(
    copies, sizes, at_ref, own_ref, other_ref, seg_col, seg_row, cos_ref, sin_ref, *refs
):
    heads, kv_heads, sources = sizes
    pieces = refs[:sources]
    hid, normed, qs, ks, vs, mixed, lse, weights, small, out_weights, gains = refs[sources:-3]
    own, other, sems = refs[-3:]
    me, core = at_ref[0], at_ref[1]
    rows = own_ref.shape[0]
    length = 2 * rows
    hid[pl.ds(pl.multiple_of(core * rows, rows), rows)] = own_ref[...]
    hid[pl.ds(pl.multiple_of((1 - core) * rows, rows), rows)] = other_ref[...]
    lay_rows(copies, pieces, (weights, small, out_weights), sems, me)
    gains[...] = jnp.transpose(small[...].astype(f32))[: gains.shape[0]]
    value = hid[...].astype(f32)
    root = lax.rsqrt(jnp.mean(value * value, axis=1, keepdims=True) + epsilon)
    normed[...] = (value * root * gains[GAIN_A : GAIN_A + 1]).astype(bf16)
    qkv = lax.dot_general(normed[...], weights[...], NN, preferred_element_type=f32)
    cosine, sine = cos_ref[...], sin_ref[...]
    for head in range(heads):
        at = slice(head * HD, (head + 1) * HD)
        qs[:, at] = turn(qkv[:, at], cosine, sine).astype(bf16)
    for head in range(kv_heads):
        at = slice(head * HD, (head + 1) * HD)
        ks[:, at] = turn(qkv[:, heads * HD :][:, at], cosine, sine).astype(bf16)
    vs[...] = qkv[:, (heads + kv_heads) * HD :].astype(bf16)
    splits = row_splits(length)
    scale = 1.0 / math.sqrt(HD)
    for (low, high), mask in zip(splits, masks(seg_col[...], seg_row[...], splits)):
        for head in range(heads):
            at = slice(head * HD, (head + 1) * HD)
            kv = head // (heads // kv_heads)
            kv = slice(kv * HD, (kv + 1) * HD)
            scores = lax.dot_general(
                qs[low:high, at], ks[:high, kv], NT, preferred_element_type=f32
            )
            scores = scores * scale + mask
            peak = jnp.max(scores, axis=1, keepdims=True)
            expo = jnp.exp(scores - peak)
            total = jnp.sum(expo, axis=1, keepdims=True)
            lse[low:high, head : head + 1] = peak + jnp.log(total)
            probs = (expo * (1.0 / total)).astype(bf16)
            mixed[low:high, at] = lax.dot_general(
                probs, vs[:high, kv], NN, preferred_element_type=f32
            ).astype(bf16)
    for target, half in ((other, 1 - core), (own, core)):
        part = mixed[pl.ds(pl.multiple_of(half * rows, rows), rows)]
        target[...] = lax.dot_general(
            part, out_weights[...], NT, preferred_element_type=f32
        ).astype(target.dtype)


def middle_kernel(hidden, own, other, gains, middle, normed):
    value = hidden[...].astype(f32) + own[...] + other[...].astype(f32)
    middle[...] = value
    root = lax.rsqrt(jnp.mean(value * value, axis=1, keepdims=True) + epsilon)
    normed[...] = (value * root * gains[GAIN_F : GAIN_F + 1]).astype(bf16)


def middle_back_kernel(
    middle, normed, grad_out, code, router, gains, own, *refs
):
    others, (grad_middle, grad_round, small) = refs[:-3], refs[-3:]
    width = middle.shape[1]
    total = own[...].astype(f32)
    for other in others:
        total += other[...].astype(f32)
    routed = code[...].astype(f32) > 0.5
    logits = lax.dot_general(normed[...], router[...], NN, preferred_element_type=f32)
    logits = jnp.where(routed, logits, -1e30)
    expo = jnp.where(routed, jnp.exp(logits - jnp.max(logits, axis=1, keepdims=True)), 0.0)
    gates = expo / jnp.sum(expo, axis=1, keepdims=True)
    grad_gates = total[:, width:]
    grad_logits = gates * (grad_gates - jnp.sum(gates * grad_gates, axis=1, keepdims=True))
    high = grad_logits.astype(bf16)
    low = (grad_logits - high.astype(f32)).astype(bf16)
    grad_normed = total[:, :width]
    router_grad = jnp.zeros(small.shape, f32)
    for part in (high, low):
        grad_normed += lax.dot_general(part, router[...], NT, preferred_element_type=f32)
        router_grad += lax.dot_general(normed[...], part, TN, preferred_element_type=f32)
    value = middle[...]
    root = lax.rsqrt(jnp.mean(value * value, axis=1, keepdims=True) + epsilon)
    scaled = value * root
    column = jnp.sum(grad_normed * scaled, axis=0, keepdims=True)
    column = jnp.transpose(jnp.broadcast_to(column, (EXTRA, width)))
    lanes = lax.broadcasted_iota(jnp.int32, small.shape, 1)
    small[...] = jnp.where(lanes == GAIN_F, column, router_grad)
    grad_scaled = grad_normed * gains[GAIN_F : GAIN_F + 1]
    inner = jnp.mean(grad_scaled * scaled, axis=1, keepdims=True)
    result = grad_out[...].astype(f32) + root * (grad_scaled - scaled * inner)
    grad_middle[...] = result
    grad_round[...] = result.astype(bf16)


def attend_back_kernel(
    block,
    sizes,
    at_ref,
    own_ref,
    other_ref,
    mixed,
    out_weights,
    small_ref,
    qs,
    ks,
    vs,
    lse,
    seg_col,
    seg_row,
    cos_ref,
    sin_ref,
    hid,
    normed,
    weights,
    *refs,
):
    heads, kv_heads = sizes
    own, other, parts = refs[0], refs[1], refs[2:-6]
    acc, small, grads, whole, grad_mixed, out_acc = refs[-6:]
    me, core = at_ref[0], at_ref[1]
    length, width = hid.shape
    rows = own.shape[0]
    cols = grads.shape[1]
    whole[pl.ds(pl.multiple_of(core * rows, rows), rows)] = own_ref[...]
    whole[pl.ds(pl.multiple_of((1 - core) * rows, rows), rows)] = other_ref[...]
    grad_mixed[...] = lax.dot_general(
        whole[...], out_weights[...], NN, preferred_element_type=f32
    ).astype(bf16)
    out_acc[...] = lax.dot_general(whole[...], mixed[...], TN, preferred_element_type=f32)
    store_parts(out_acc, parts, me, block, cols + EXTRA)
    cosine, sine = cos_ref[...], -sin_ref[...]
    splits = row_splits(length)
    scale = 1.0 / math.sqrt(HD)
    per_group = heads // kv_heads
    bias = masks(seg_col[...], seg_row[...], splits)
    for kv_head in range(kv_heads):
        kv = slice(kv_head * HD, (kv_head + 1) * HD)
        grad_key = jnp.zeros((length, HD), f32)
        grad_value = jnp.zeros((length, HD), f32)
        for (low, high), mask in zip(splits, bias):
            key_sum = jnp.zeros((high, HD), f32)
            value_sum = jnp.zeros((high, HD), f32)
            for head in range(kv_head * per_group, (kv_head + 1) * per_group):
                at = slice(head * HD, (head + 1) * HD)
                query, grad = qs[low:high, at], grad_mixed[low:high, at]
                scores = lax.dot_general(query, ks[:high, kv], NT, preferred_element_type=f32)
                probs = jnp.exp(scores * scale + mask - lse[low:high, head : head + 1])
                grad_probs = lax.dot_general(
                    grad, vs[:high, kv], NT, preferred_element_type=f32
                )
                inner = jnp.sum(grad_probs * probs, axis=1, keepdims=True)
                grad_scores = (probs * (grad_probs - inner)).astype(bf16)
                grad_query = lax.dot_general(
                    grad_scores, ks[:high, kv], NN, preferred_element_type=f32
                )
                grads[low:high, at] = turn(
                    grad_query * scale, cosine[low:high], sine[low:high]
                ).astype(bf16)
                key_sum += lax.dot_general(grad_scores, query, TN, preferred_element_type=f32)
                value_sum += lax.dot_general(
                    probs.astype(bf16), grad, TN, preferred_element_type=f32
                )
            if high < length:
                pad = jnp.zeros((length - high, HD), f32)
                key_sum = jnp.concatenate([key_sum, pad], axis=0)
                value_sum = jnp.concatenate([value_sum, pad], axis=0)
            grad_key += key_sum
            grad_value += value_sum
        at = (heads + kv_head) * HD
        grads[:, at : at + HD] = turn(grad_key * scale, cosine, sine).astype(bf16)
        at += kv_heads * HD
        grads[:, at : at + HD] = grad_value.astype(bf16)
    acc[...] = lax.dot_general(normed[...], grads[...], TN, preferred_element_type=f32)
    store_parts(acc, parts, me, block, 0)
    value = hid[...].astype(f32)
    root = lax.rsqrt(jnp.mean(value * value, axis=1, keepdims=True) + epsilon)
    column = jnp.zeros((1, width), f32)
    for target, half in ((other, 1 - core), (own, core)):
        at = pl.ds(pl.multiple_of(half * rows, rows), rows)
        part = lax.dot_general(grads[at], weights[...], NT, preferred_element_type=f32)
        target[...] = part.astype(target.dtype)
        half_value = hid[at].astype(f32)
        half_root = lax.rsqrt(jnp.mean(half_value * half_value, axis=1, keepdims=True) + epsilon)
        column += jnp.sum(part * (half_value * half_root), axis=0, keepdims=True)
    lanes = lax.broadcasted_iota(jnp.int32, small.shape, 1)
    column = jnp.transpose(jnp.broadcast_to(column, (EXTRA, width)))
    small[...] = jnp.where(lanes == GAIN_A, column, small_ref[...])
    store_parts(small, parts, me, block, cols)


def slots_kernel(parts, at_ref, order_col, order_row, own, other, code, *refs):
    picks, rows_out, whole = refs[: len(parts)], refs[-2], refs[-1]
    core = at_ref[1]
    rows = own.shape[0]
    width = own.shape[1]
    whole[pl.ds(pl.multiple_of(core * rows, rows), rows), :width] = own[...]
    whole[pl.ds(pl.multiple_of((1 - core) * rows, rows), rows), :width] = other[...]
    whole[:, width:] = code[...]
    none = order_row.shape[0] // 2 * order_row.shape[1]
    first = core * sum(parts)
    for expert in range(order_row.shape[0]):
        row = order_row[expert : expert + 1, :]
        ahead = (order_col[:, expert : expert + 1] < row).astype(f32)
        position = jnp.sum(ahead, axis=0, keepdims=True).astype(jnp.int32)
        position = jnp.where(row < none, position, -1)
        low = first
        for pick, count in zip(picks, parts):
            slot = lax.broadcasted_iota(jnp.int32, (count, row.shape[1]), 0) + low
            pick[expert * count : (expert + 1) * count, :] = (slot == position).astype(bf16)
            low = low + count
    low = 0
    for pick, count in zip(picks, parts):
        taken = lax.dot_general(pick[...], whole[...], NN, preferred_element_type=f32)
        rows_out[:, low : low + count] = taken.astype(bf16).reshape(
            order_row.shape[0], count, whole.shape[1]
        )
        low += count


def take_kernel(at_ref, own, other, *refs):
    count = (len(refs) - 1) // 2
    picks, outs, whole = refs[:count], refs[count:-1], refs[-1]
    core = at_ref[1]
    rows = own.shape[0]
    whole[pl.ds(pl.multiple_of(core * rows, rows), rows)] = own[...]
    whole[pl.ds(pl.multiple_of((1 - core) * rows, rows), rows)] = other[...]
    for pick, out in zip(picks, outs):
        out[...] = lax.dot_general(
            pick[...], whole[...], NN, preferred_element_type=f32
        ).astype(bf16)


def give_kernel(count, at_ref, *refs):
    picks, values, (own, other) = refs[:count], refs[count:-2], refs[-2:]
    rows = own.shape[0]
    if len(values) < count:
        whole, values, low = values[0][...], [], 0
        for pick in picks:
            each = pick.shape[0] // whole.shape[0]
            values.append(whole[:, low : low + each].reshape(pick.shape[0], whole.shape[2]))
            low += each
    for target, half in ((other, 1 - at_ref[1]), (own, at_ref[1])):
        columns = pl.ds(pl.multiple_of(half * rows, rows), rows)
        total = None
        for pick, value in zip(picks, values):
            part = lax.dot_general(
                pick[:, columns], value[...], TN, preferred_element_type=f32
            )
            total = part if total is None else total + part
        target[...] = total.astype(target.dtype)


def gelu_parts(value):
    square = value * value
    inner = value * (0.7978845608028654 + 0.035677408136300125 * square)
    tanh = jnp.tanh(inner)
    half = 0.5 + 0.5 * tanh
    slope = half + 0.5 * value * (1.0 - tanh * tanh) * (
        0.7978845608028654 + 3.0 * 0.035677408136300125 * square
    )
    return value * half, slope


def moe_kernel(plan, at_ref, router_ref, x_in, g_in, *refs):
    copies, hidden, blocks, outer, first, groups = plan
    weight_count = len(set(c[0] for c in copies))
    if first:
        refs = refs[1:]
    sources, outs, refs = refs[:weight_count], refs[weight_count:][:5], refs[weight_count + 5 :]
    weights, xs, gs = refs[:3]
    buffers = refs[3:8]
    weight_sems, in_sems, out_sems = refs[8:]
    branch, gradn, act_all, gp_all, geo_all = buffers
    _, rows, width = xs.shape
    whole = 2 * hidden
    expert = at_ref[0] % CUBE

    weight_copies = []
    block_rows = weights.shape[0] // outer
    for number, (source, entry, low, length, offset, from_col, to_col, cols) in enumerate(copies):
        row = pl.multiple_of(((at_ref[0] // CUBE) ^ offset) * block_rows + low, 16)
        weight_copies.append(
            pltpu.make_async_copy(
                sources[source].at[entry, :, pl.ds(from_col, cols)],
                weights.at[pl.ds(row, length), pl.ds(to_col, cols)],
                weight_sems.at[number],
            )
        )
    weight_order = sorted(range(len(copies)), key=lambda k: copies[k][5] // hidden)
    in_copies = []
    for block in range(blocks):
        span = pl.ds(block * rows, rows)
        for kind, (source, target) in enumerate(((x_in, xs), (g_in, gs))):
            held = (span,)
            if kind == 1:
                held = pl.ds(block * groups, groups), pl.ds(first, rows // groups)
            in_copies.append(
                pltpu.make_async_copy(
                    source.at[held], target.at[block], in_sems.at[2 * block + kind]
                )
            )
    in_copies[0].start()
    for k in weight_order:
        weight_copies[k].start()
    for copy in in_copies[1:]:
        copy.start()
    out_copies = []
    for block in range(blocks):
        in_copies[2 * block].wait()
        x = xs[block]
        logits = lax.dot_general(x, router_ref[...], NN, preferred_element_type=f32)
        if block == 0:
            for k in weight_order:
                if copies[k][5] < 2 * hidden:
                    weight_copies[k].wait()
        pre = lax.dot_general(x, weights[:, : 2 * whole], NN, preferred_element_type=f32)
        in_copies[2 * block + 1].wait()
        both = gs[block].reshape(rows, gs.shape[3])
        routed = both[:, width:].astype(f32) > 0.5
        lanes = lax.broadcasted_iota(jnp.int32, routed.shape, 1)
        logits = jnp.where(routed, logits, -1e30)
        expo = jnp.where(routed, jnp.exp(logits - jnp.max(logits, axis=1, keepdims=True)), 0.0)
        total = jnp.sum(expo, axis=1, keepdims=True)
        gate = jnp.sum(jnp.where(lanes == expert, expo, 0.0), axis=1, keepdims=True)
        gate = gate / jnp.where(total > 0.0, total, 1.0)

        gate_pre, up_pre = pre[:, :whole], pre[:, whole:]
        gelu, slope = gelu_parts(gate_pre)
        act = (gelu * up_pre).astype(bf16)
        act_all[block] = act
        if block == 0:
            for k in weight_order:
                if copies[k][5] == 2 * hidden:
                    weight_copies[k].wait()
        down = weights[:, 2 * whole :]
        expert_out = lax.dot_general(act, down, NT, preferred_element_type=f32)
        branch[block] = (gate * expert_out).astype(bf16).reshape(branch.shape[1:])
        g = both[:, :width].astype(f32)
        grad_gate = jnp.sum(g * expert_out, axis=1, keepdims=True)
        gradn[block, :, width:] = jnp.where(lanes == expert, grad_gate, 0.0).astype(bf16)
        geo = (gate * g).astype(bf16)
        geo_all[block] = geo
        grad_act = lax.dot_general(geo, down, NN, preferred_element_type=f32)
        grad_gate_pre = (grad_act * up_pre * slope).astype(bf16)
        grad_up_pre = (grad_act * gelu).astype(bf16)
        for side in range(2):
            cols = slice(side * hidden, (side + 1) * hidden)
            for kind, part in enumerate((grad_gate_pre, grad_up_pre)):
                at = (2 * side + kind) * hidden
                gp_all[block, :, at : at + hidden] = part[:, cols]
        grad_in = lax.dot_general(
            grad_gate_pre, weights[:, :whole], NT, preferred_element_type=f32
        ) + lax.dot_general(
            grad_up_pre, weights[:, whole : 2 * whole], NT, preferred_element_type=f32
        )
        gradn[block, :, :width] = grad_in.astype(bf16)
        for number, (source, target) in enumerate(zip(buffers, outs)):
            if number == 0:
                held = pl.ds(block * groups, groups), pl.ds(first, rows // groups)
            else:
                held = (pl.ds(block * rows, rows),)
            copy = pltpu.make_async_copy(
                source.at[block], target.at[held], out_sems.at[5 * block + number]
            )
            copy.start()
            out_copies.append(copy)
    for copy in out_copies:
        copy.wait()


def moe(at, x, g, router, pieces, hidden, outer, sequences, capacity, branch=None):
    copies = []
    for source, (array, first, low, side) in enumerate(pieces):
        for entry in range(array.shape[0]):
            for kind in range(3):
                copies.append(
                    (source, entry, low, array.shape[1], first + entry, kind * hidden)
                    + ((2 * kind + side) * hidden, hidden)
                )
    total, width = x.shape
    blocks = 2
    rows = total // blocks
    widths = (width, width + EXTRA, 2 * hidden, 4 * hidden, width)
    each = total // sequences
    first = 0 if branch is None else capacity - each
    args = [x, g] + ([] if branch is None else [branch]) + [p[0] for p in pieces]
    groups = sequences // blocks
    buffers = [(blocks, rows, w) for w in widths]
    buffers[0] = (blocks, groups, each, width)
    return pl.pallas_call(
        functools.partial(moe_kernel, (copies, hidden, blocks, outer, first, groups)),
        out_shape=[jax.ShapeDtypeStruct((sequences, capacity, width), bf16)]
        + [jax.ShapeDtypeStruct((total, w), bf16) for w in widths[1:]],
        in_specs=[pl.BlockSpec(memory_space=pltpu.SMEM), pl.BlockSpec(memory_space=pltpu.VMEM)]
        + [pl.BlockSpec(memory_space=pl.ANY)] * len(args),
        out_specs=[pl.BlockSpec(memory_space=pl.ANY)] * 5,
        scratch_shapes=[
            pltpu.VMEM((width, 6 * hidden), bf16),
            pltpu.VMEM((blocks, rows, width), bf16),
            pltpu.VMEM((blocks, groups, each, width + EXTRA), bf16),
        ]
        + [pltpu.VMEM(dims, bf16) for dims in buffers]
        + [
            pltpu.SemaphoreType.DMA((len(copies),)),
            pltpu.SemaphoreType.DMA((2 * blocks,)),
            pltpu.SemaphoreType.DMA((5 * blocks,)),
        ],
        input_output_aliases={} if branch is None else {4: 0},
        compiler_params=pltpu.CompilerParams(vmem_limit_bytes=60 * 1024 * 1024),
        cost_estimate=BRIEF,
        name="experts",
    )(at, router, *args)


def weight_grads_kernel(calls, pre, down, at_ref, *refs):
    kinds = int(pre) + int(down)
    pairs = []
    for _ in range(kinds):
        pairs.append((refs[:calls], refs[calls : 2 * calls]))
        refs = refs[2 * calls :]
    outs, buffers, sems = refs[: 2 * kinds], refs[2 * kinds : -1], refs[-1]
    cols = buffers[0].shape[1]
    columns = pl.ds(pl.multiple_of(at_ref[2] * cols, cols), cols)
    copies = []
    for number, (lefts, rights) in enumerate(pairs):
        row = 0
        for left, right in zip(lefts, rights):
            rows = pl.ds(row, left.shape[0])
            for source, target in (
                (left.at[:, columns], buffers[2 * number].at[rows]),
                (right, buffers[2 * number + 1].at[rows]),
            ):
                copies.append(pltpu.make_async_copy(source, target, sems.at[len(copies)]))
                copies[-1].start()
            row += left.shape[0]
    for number in range(kinds):
        for copy in copies[2 * calls * number : 2 * calls * (number + 1)]:
            copy.wait()
        total = lax.dot_general(
            buffers[2 * number][...],
            buffers[2 * number + 1][...],
            TN,
            preferred_element_type=f32,
        )
        width = total.shape[1]
        outs[2 * number][...] = total[:, : width // 2]
        outs[2 * number + 1][...] = total[:, width // 2 :].astype(bf16)


def weight_grads(at, half, pre, down):
    args, outs, scratch = [], [], []
    for pairs in (pre, down):
        if not pairs:
            continue
        args += [p[0] for p in pairs] + [p[1] for p in pairs]
        rows = sum(p[0].shape[0] for p in pairs)
        left, right = pairs[0][0].shape[1] // 2, pairs[0][1].shape[1]
        outs += [((left, right // 2), f32), ((left, right // 2), bf16)]
        scratch += [(rows, left), (rows, right)]
    return pl.pallas_call(
        functools.partial(weight_grads_kernel, len(pre or down), bool(pre), bool(down)),
        out_shape=[jax.ShapeDtypeStruct(dims, kind) for dims, kind in outs],
        in_specs=[pl.BlockSpec(memory_space=pltpu.SMEM)]
        + [pl.BlockSpec(memory_space=pl.ANY)] * len(args),
        out_specs=[pl.BlockSpec(memory_space=pltpu.VMEM)] * len(outs),
        scratch_shapes=[pltpu.VMEM(dims, bf16) for dims in scratch]
        + [pltpu.SemaphoreType.DMA((len(args),))],
        compiler_params=pltpu.CompilerParams(vmem_limit_bytes=60 * 1024 * 1024),
        cost_estimate=BRIEF,
        name="weight_grads",
    )(jnp.concatenate([at, half.reshape(1)]), *args)


def per_device(
    count,
    hidden_in,
    segment_ids,
    routes,
    slot_order,
    gain_attn,
    w_query,
    w_key,
    w_value,
    w_out,
    gain_ffn,
    w_router,
    w_gate,
    w_up,
    w_down,
    grad_out,
):
    tok_rows, width = hidden_in.shape
    seq_len = segment_ids.shape[0]
    top_count = routes.shape[1]
    experts, block, hidden = w_gate.shape
    capacity = 9 * seq_len * top_count // (8 * experts)
    me = lax.axis_index("dp").astype(jnp.int32)
    core = lax.axis_index("tensor").astype(jnp.int32)
    at = jnp.stack([me, core])
    groups = [list(range(first, first + CUBE)) for first in range(0, count, CUBE)]
    heads_cols, kv_cols = w_query.shape[1], w_key.shape[1]
    qkv_cols = heads_cols + 2 * kv_cols
    heads, kv_heads = heads_cols // HD, kv_cols // HD

    def shape(rows, cols, dtype=bf16):
        return jax.ShapeDtypeStruct((rows, cols), dtype)

    def near(own):
        return {0: own} | {bit: swap(own, bit, count) for bit in NEAR}

    def far(got):
        return got | {
            3: swap(got[2], 1, count),
            6: swap(got[4], 2, count),
            5: swap(got[1], 4, count),
        }

    def last(got, axis):
        spans = halves(got[0].shape[axis])
        return got | {
            7: swap(cut(got[6], spans[0], axis), 1, count),
            8: swap(cut(got[5], spans[1], axis), 2, count),
        }

    small = jnp.concatenate([w_router, gain_attn[:, None], gain_ffn[:, None]], axis=1)
    small = jnp.pad(small, ((0, 0), (0, EXTRA - small.shape[1])))
    pair = outer_pair(
        jnp.concatenate([w_query, w_key, w_value, small, w_out.T], axis=1), count
    )
    hidden_other = swap_core(hidden_in)

    expert_shard = jnp.concatenate([w_gate, w_up, jnp.swapaxes(w_down, 1, 2)], axis=2)
    expert_rows = lax.all_to_all(
        expert_shard.reshape(experts * block, 3 * hidden),
        "dp",
        0,
        0,
        tiled=True,
        axis_index_groups=groups,
    )

    order = jnp.min(
        jnp.where(
            routes[:, :, None] == jnp.arange(experts, dtype=jnp.int32),
            slot_order[0].reshape(seq_len, top_count)[:, :, None],
            seq_len * top_count,
        ),
        axis=1,
    )
    code = (order < seq_len * top_count).astype(bf16)
    code = jnp.pad(code, ((0, 0), (0, EXTRA - experts)))
    code_own = lax.dynamic_slice_in_dim(code, core * tok_rows, tok_rows, 0)
    first_part = (capacity // 4 + 15) // 16 * 16
    slot_parts = (first_part, capacity // 2 - first_part)
    grad_other = swap_core(grad_out)
    slots = vmem_call(
        functools.partial(slots_kernel, slot_parts),
        [shape(experts * part, seq_len) for part in slot_parts]
        + [jax.ShapeDtypeStruct((experts, sum(slot_parts), width + EXTRA), bf16)],
        [pltpu.VMEM((seq_len, width + EXTRA), bf16)],
        [(at, 1), (order, 0), (order.T, 0), (grad_out, 0), (grad_other, 0), (code, 0)],
        "slots",
    )
    picks, grad_rows = slots[:2], slots[2]

    def exchange(rows):
        return lax.all_to_all(rows, "dp", 0, 0, tiled=True, axis_index_groups=groups)

    cosine, sine_table = rope_tables(seq_len, HD)
    cosine = jnp.concatenate([cosine, cosine], axis=1)
    sine_table = jnp.concatenate([-sine_table, sine_table], axis=1)
    seg_col, seg_row = segment_ids[:, None], segment_ids[None, :]

    (pair,) = gate([pair], cosine, sine_table, hidden_other, grad_other)
    if count == 2 * CUBE:
        edges = [expert_rows.shape[0] * k // 48 // 16 * 16 for k in (0, 13, 26, 32, 48)]
    else:
        edges = [0] * 4 + [expert_rows.shape[0]]
    pieces = [(expert_rows[None], 0, 0, 0), (swap_core(expert_rows)[None], 0, 0, 1)]

    def outer_chunk(k, *events):
        low, high = edges[k], edges[k + 1]
        if high == low:
            return [], []
        (chunk,) = gate([cut(expert_rows, (low, high), 0)], *events)
        arrays, first, swapped = outer_gather(chunk, count)[1:], 1, []
        for array in arrays:
            swapped.append(swap_core(array))
            pieces.append((array, first, low, 0))
            pieces.append((swapped[-1], first, low, 1))
            first += array.shape[0]
        return arrays, swapped

    with jax.named_scope("weights_near"):
        got = near(pair)
    arrays, swapped = outer_chunk(0, pair)
    got = gate_dict(got, NEAR, grad_rows, arrays, pieces[1][0])
    with jax.named_scope("weights_far"):
        got = far(got)
    arrays, swapped_next = outer_chunk(1, got[1])
    got = gate_dict(got, FAR, arrays, swapped)
    with jax.named_scope("weights_last"):
        got = last(got, 1)
    arrays, swapped = outer_chunk(2, got[3])
    got = gate_dict(got, LAST, arrays, swapped_next)
    sources, copies = piece_copies(got, block, me, count)
    grad_rows, seg_col = gate([grad_rows, seg_col], got[7])
    with jax.named_scope("grads_rows"):
        grad_rows = exchange(grad_rows)
    attended = vmem_call(
        functools.partial(attend_kernel, copies, (heads, kv_heads, len(sources))),
        [
            shape(seq_len, width),
            shape(seq_len, width),
            shape(seq_len, heads_cols),
            shape(seq_len, kv_cols),
            shape(seq_len, kv_cols),
            shape(seq_len, heads_cols),
            shape(seq_len, HD, f32),
            shape(width, qkv_cols),
            shape(width, EXTRA),
            shape(width, heads_cols),
            shape(16, width, f32),
            shape(tok_rows, width, f32),
            shape(tok_rows, width),
        ],
        [pltpu.SemaphoreType.DMA((3 * len(copies),))],
        [(at, 1), (hidden_in, 0), (hidden_other, 0), (seg_col, 0), (seg_row, 0)]
        + [(cosine, 0), (sine_table, 0)]
        + [(piece, 2) for piece in sources],
        "attend",
        flops=2 * seq_len * (width * (qkv_cols + heads_cols) + heads_cols * seq_len),
    )
    hid, normed, qs, ks, vs, mixed, lse, full_qkv, router, out_wt, gains = attended[:-2]
    attn_own, attn_other = attended[-2:]
    middle, normed2 = vmem_call(
        middle_kernel,
        [shape(tok_rows, width, f32), shape(tok_rows, width)],
        [],
        [(hidden_in, 0), (attn_own, 0), (swap_core(attn_other), 0), (gains, 0)],
        "middle",
    )

    rows = vmem_call(
        take_kernel,
        [shape(experts * part, width) for part in slot_parts],
        [pltpu.VMEM((seq_len, width), bf16)],
        [(at, 1), (normed2, 0), (swap_core(normed2), 0)] + [(pick, 0) for pick in picks],
        "take",
    )
    rows = list(rows)
    rows[0], grad_rows = gate([rows[0], grad_rows], swapped)
    with jax.named_scope("tokens_rows"):
        x_first = exchange(rows[0])
    arrays, _ = outer_chunk(3, rows[0])
    x_first, rows_second = gate([x_first, rows[1]], arrays)
    with jax.named_scope("tokens_rows"):
        x_second = exchange(rows_second)

    def experts_on(x, g, router, branch=None):
        held = (CUBE, sum(slot_parts))
        return moe(at, x, g, router, pieces, hidden, count // CUBE, *held, branch)

    branch, gradn_first, *first = experts_on(x_first, grad_rows, router)
    with jax.named_scope("gradn_rows"):
        gradn_first = exchange(gradn_first)
    (second_router,) = gate([router], first[0])
    branch, gradn_second, *second = experts_on(x_second, grad_rows, second_router, branch)

    xs = (x_first, x_second)
    pre_pairs = [(x, call[1]) for x, call in zip(xs, (first, second))]
    down_pairs = [(call[2], call[0]) for call in (first, second)]
    bits = outer_bits(count)
    top = (me // bits[-1]) % 2 if bits else jnp.zeros((), jnp.int32)

    def part_grads(half, pre, down, event):
        half = gate([half.reshape(1)], event)[0]
        outs = weight_grads(at, half, pre, down)
        return [(outs[i], outs[i + 1]) for i in range(0, len(outs), 2)]

    def both_cores(pair):
        return pair[0] + swap_core(pair[1]).astype(f32)

    (send_down,) = part_grads(1 - top, [], down_pairs, second[0])
    (gradn_second,) = gate([gradn_second], send_down)
    event = gradn_second
    with jax.named_scope("gradn_rows"):
        gradn_second = exchange(gradn_second)
    with jax.named_scope("expert_scatter"):
        down_part = both_cores(send_down).astype(bf16)
    (send_pre,) = part_grads(1 - top, pre_pairs, [], event)
    keep_pre, keep_down = part_grads(top, pre_pairs, down_pairs, send_pre)
    with jax.named_scope("expert_scatter"):
        send_pre = both_cores(send_pre).astype(bf16)

        sent = jnp.concatenate([send_pre, down_part], axis=1)
        sent_got = swap(sent, bits[-1], count) if bits else sent

    def give(picks, values, name):
        own, other = vmem_call(
            functools.partial(give_kernel, len(picks)),
            [shape(tok_rows, values[0].shape[-1], f32), shape(tok_rows, values[0].shape[-1])],
            [],
            [(at, 1)] + [(pick, 0) for pick in picks] + [(value, 0) for value in values],
            name,
        )
        return own, swap_core(other)

    gradn_second, gradn_first = gate([gradn_second, gradn_first], keep_pre[0])
    gradn = list(give(picks, (gradn_first, gradn_second), "give_gradn"))

    grad_middle, grad_mid_r, small_f = vmem_call(
        middle_back_kernel,
        [shape(tok_rows, width, f32), shape(tok_rows, width), shape(width, EXTRA, f32)],
        [],
        [(middle, 0), (normed2, 0), (grad_out, 0), (code_own, 0), (router, 0), (gains, 0)]
        + [(array, 0) for array in gradn],
        "middle_back",
    )

    grad_mid_other = swap_core(grad_mid_r)
    (branch,) = gate([branch], gradn[0])
    with jax.named_scope("branch_rows"):
        branch = exchange(branch)
    normed_own, normed_other, *parts = vmem_call(
        functools.partial(attend_back_kernel, block, (heads, kv_heads)),
        [shape(tok_rows, width, f32), shape(tok_rows, width)]
        + part_shapes(count, block, qkv_cols + EXTRA + heads_cols),
        [
            pltpu.VMEM((width, qkv_cols), f32),
            pltpu.VMEM((width, EXTRA), f32),
            pltpu.VMEM((seq_len, qkv_cols), bf16),
            pltpu.VMEM((seq_len, width), bf16),
            pltpu.VMEM((seq_len, heads_cols), bf16),
            pltpu.VMEM((width, heads_cols), f32),
        ],
        [(at, 1), (grad_mid_r, 0), (grad_mid_other, 0), (mixed, 0), (out_wt, 0)]
        + [(small_f, 0), (qs, 0), (ks, 0), (vs, 0), (lse, 0), (seg_col, 0)]
        + [(seg_row, 0), (cosine, 0), (sine_table, 0), (hid, 0), (normed, 0), (full_qkv, 0)],
        "attend_back",
        flops=4 * seq_len * (width * (qkv_cols + heads_cols) + 2 * heads_cols * seq_len),
    )
    parts = spread_parts(parts, me, count)

    parts = gate_dict(parts, (3,) + LAST)
    with jax.named_scope("attn_last"):
        got = sum_last(parts, count)
    grad_normed = normed_own + swap_core(normed_other).astype(f32)
    gated = gate([got[7], got[8], parts[3]])
    got, parts[3] = dict(zip(LAST, gated)), gated[2]
    with jax.named_scope("attn_far"):
        terms = far_terms(parts, got)
        attn_far = sum_far(parts, terms, count)
    with jax.named_scope("expert_scatter"):
        (sent_got,) = gate([sent_got], terms)
        keep = jnp.concatenate([both_cores(keep_pre), both_cores(keep_down)], axis=1)
        total = keep + sent_got.astype(f32) if bits else jnp.concatenate([keep, sent_got], axis=0)
        for bit in reversed(bits[:-1]):
            half = total.shape[0] // 2
            high = (me // bit) % 2
            mine = lax.dynamic_slice_in_dim(total, high * half, half, 0)
            other = lax.dynamic_slice_in_dim(total, (1 - high) * half, half, 0)
            total = mine + swap(other.astype(bf16), bit, count).astype(f32)
        total = total.astype(bf16)
    gated = gate([attn_far[k] for k in NEAR] + [total, branch])
    attn_far, total, branch = dict(zip(NEAR, gated)), gated[3], gated[4]
    with jax.named_scope("attn_near"):
        attn_near = sum_near(near_terms(parts, attn_far), count)
    with jax.named_scope("expert_scatter"):
        total = exchange(total)
    gated = gate([attn_near[k] for k in NEAR] + [branch])
    attn_near, branch = dict(zip(NEAR, gated)), gated[3]
    with jax.named_scope("attn_outer"):
        attn_grads = outer_sum(sum_own(parts, attn_near), count)
    branch_own, branch_other = give(picks, (branch,), "give_branch")
    layer_out = middle + branch_own + branch_other.astype(f32)

    expert_grads = total.reshape(experts, block, 3 * hidden).astype(f32)
    grad_gate_w = expert_grads[:, :, :hidden]
    grad_up_w = expert_grads[:, :, hidden : 2 * hidden]
    grad_down_w = jnp.swapaxes(expert_grads[:, :, 2 * hidden :], 1, 2)
    scaled_in, root_in = rms_parts(hidden_in.astype(f32))
    grad_in = grad_middle + norm_backward(grad_normed, scaled_in, root_in, gains[GAIN_A])
    smalls = attn_grads[:, qkv_cols : qkv_cols + EXTRA]
    smalls = smalls + swap_core(smalls)
    return (
        layer_out,
        grad_in,
        smalls[:, GAIN_A],
        attn_grads[:, :heads_cols],
        attn_grads[:, heads_cols : heads_cols + kv_cols],
        attn_grads[:, heads_cols + kv_cols : qkv_cols],
        attn_grads[:, qkv_cols + EXTRA :].T,
        smalls[:, GAIN_F],
        smalls[:, :experts],
        grad_gate_w,
        grad_up_w,
        grad_down_w,
    )


def solution(mesh):
    return jax.shard_map(
        functools.partial(per_device, mesh.shape["dp"]),
        mesh=mesh,
        in_specs=(
            P(("dp", "tensor"), None),
            P("dp"),
            P("dp", None),
            P("dp", None),
            P("dp"),
            P("dp", "tensor"),
            P("dp", "tensor"),
            P("dp", "tensor"),
            P("tensor", "dp"),
            P("dp"),
            P("dp", None),
            P(None, "dp", "tensor"),
            P(None, "dp", "tensor"),
            P(None, "tensor", "dp"),
            P(("dp", "tensor"), None),
        ),
        out_specs=(
            P(("dp", "tensor"), None),
            P(("dp", "tensor"), None),
            P("dp"),
            P("dp", "tensor"),
            P("dp", "tensor"),
            P("dp", "tensor"),
            P("tensor", "dp"),
            P("dp"),
            P("dp", None),
            P(None, "dp", "tensor"),
            P(None, "dp", "tensor"),
            P(None, "tensor", "dp"),
        ),
        check_vma=False,
    )
```

```python
import functools
import math

import jax
import jax.numpy as jnp
from jax import lax
from jax.experimental import pallas as pl
from jax.experimental.pallas import tpu as pltpu
from jax.sharding import PartitionSpec as P

HD = 128
EXTRA = 128
GAIN_A, GAIN_F = 8, 9
CUBE = 8
BRIEF = pl.CostEstimate(flops=0, bytes_accessed=3_000_000, transcendentals=0)
LIGHT = ("attend", "middle", "take", "give_gradn", "middle_back", "attend_back")
FREE = pl.CostEstimate(flops=0, bytes_accessed=0, transcendentals=0)
epsilon = 1e-06
highest = lax.Precision.HIGHEST
f32 = jnp.float32
bf16 = jnp.bfloat16
NN = (((1,), (0,)), ((), ()))
NT = (((1,), (1,)), ((), ()))
TN = (((0,), (0,)), ((), ()))


def rms_parts(values):
    inverse_root = lax.rsqrt(jnp.mean(values * values, axis=-1, keepdims=True) + epsilon)
    return (values * inverse_root, inverse_root)


def norm_backward(grad_normed, scaled, inverse_root, gain):
    grad_scaled = grad_normed * gain
    inner = jnp.mean(grad_scaled * scaled, axis=-1, keepdims=True)
    return inverse_root * (grad_scaled - scaled * inner)


def rope_tables(length, size):
    inverse = 10000.0 ** (-jnp.arange(size // 2, dtype=f32) / (size // 2))
    angle = jnp.arange(length, dtype=f32)[:, None] * inverse[None, :]
    return (jnp.cos(angle), jnp.sin(angle))


def swap(values, bit, count):
    return lax.ppermute(values, "dp", [(i, i ^ bit) for i in range(count)])


def swap_core(values):
    return lax.ppermute(values, "tensor", [(0, 1), (1, 0)])


def gate(values, *events):
    values = list(values)
    flat = jax.tree.leaves(events)
    return pl.pallas_call(
        lambda *refs: None,
        out_shape=[jax.ShapeDtypeStruct(v.shape, v.dtype) for v in values],
        in_specs=[pl.BlockSpec(memory_space=pl.ANY)] * (len(values) + len(flat)),
        out_specs=[pl.BlockSpec(memory_space=pl.ANY)] * len(values),
        input_output_aliases={i: i for i in range(len(values))},
        compiler_params=pltpu.CompilerParams(vmem_limit_bytes=60 * 1024 * 1024),
        cost_estimate=BRIEF,
        name="gate",
    )(*values, *flat)


def gate_dict(got, keys, *events):
    return got | dict(zip(keys, gate([got[k] for k in keys], *events)))


def halves(rows):
    part = rows // 2
    return ((0, part), (part, rows))


def cut(values, span, axis):
    return lax.slice_in_dim(values, span[0], span[1], axis=axis)


NEAR, FAR, LAST = (1, 2, 4), (3, 9, 6, 5), (7, 8)


def add_round(left, right):
    return (left.astype(f32) + right.astype(f32)).astype(bf16)


def sum_last(parts, count):
    return {7: swap(parts[7], 1, count), 8: swap(parts[8], 2, count)}


def patch_kernel(first, second, low, high, first_out, second_out):
    first_out[...] = (first[...].astype(f32) + low[...].astype(f32)).astype(bf16)
    second_out[...] = (second[...].astype(f32) + high[...].astype(f32)).astype(bf16)


def patch(first, second, low, high):
    shape = first.shape
    half = low.shape
    if half[1] % 16:
        return (
            jnp.concatenate([add_round(first[: half[0]], low), first[half[0] :]], axis=0),
            jnp.concatenate([second[: half[0]], add_round(second[half[0] :], high)], axis=0),
        )
    top = pl.BlockSpec(half, lambda i: (0, 0, 0))
    bottom = pl.BlockSpec(half, lambda i: (1, 0, 0))
    return pl.pallas_call(
        patch_kernel,
        grid=(1,),
        out_shape=[jax.ShapeDtypeStruct(shape, bf16)] * 2,
        in_specs=[top, bottom, top, top],
        out_specs=[top, bottom],
        input_output_aliases={0: 0, 1: 1},
        compiler_params=pltpu.CompilerParams(vmem_limit_bytes=60 * 1024 * 1024),
        cost_estimate=FREE,
        name="patch",
    )(first, second, low, high)


def far_terms(parts, got):
    return patch(parts[6], parts[5], got[7], got[8])


def sum_far(parts, terms, count):
    first, second = terms
    return {4: swap(first, 2, count), 1: swap(second, 4, count), 2: swap(parts[3], 1, count)}


def terms_kernel(*refs):
    for k in range(3):
        refs[6 + k][...] = (refs[k][...].astype(f32) + refs[3 + k][...].astype(f32)).astype(bf16)


def near_terms(parts, got):
    args = [parts[bit] for bit in NEAR] + [got[bit] for bit in NEAR]
    shape = parts[1].shape
    grid = 4 if shape[-2] % 64 == 0 else 1
    block = shape[:-2] + (shape[-2] // grid, shape[-1])
    lead = (0,) * (len(shape) - 2)
    spec = pl.BlockSpec(block, lambda i: lead + (i, 0))
    outs = pl.pallas_call(
        terms_kernel,
        grid=(grid,),
        out_shape=[jax.ShapeDtypeStruct(shape, bf16)] * 3,
        in_specs=[spec] * 6,
        out_specs=[spec] * 3,
        compiler_params=pltpu.CompilerParams(vmem_limit_bytes=60 * 1024 * 1024),
        cost_estimate=FREE,
        name="terms",
    )(*args)
    return dict(zip(NEAR, outs))


def sum_near(terms, count):
    return {bit: swap(terms[bit], bit, count) for bit in NEAR}


def sum_own(parts, got):
    return parts[0].astype(f32) + (
        got[1].astype(f32) + (got[2].astype(f32) + got[4].astype(f32))
    )


def outer_bits(count):
    bits, bit = [], CUBE
    while bit < count:
        bits.append(bit)
        bit *= 2
    return bits


def outer_gather(own, count):
    pieces = [own[None]]
    for bit in outer_bits(count):
        pieces.append(swap(jnp.concatenate(pieces, axis=0), bit, count))
    return pieces


def outer_pair(shard, count):
    return jnp.concatenate(outer_gather(shard, count), axis=0)


def piece_copies(got, block, me, count):
    outer = got[0].shape[0]
    if block % 16:
        wholes = got | {3: jnp.concatenate([got[3], got[9]]), 7: jnp.concatenate([got[7], got[8]])}
        stacked = jnp.stack([wholes[b] for b in range(CUBE)], axis=1)
        whole = stacked.reshape(count, block, -1)[jnp.arange(count) ^ me]
        return [whole.reshape(1, count * block, -1)], [(0, 0, count * block, None, block)]
    sources, copies = [], []
    for b in range(CUBE + 2):
        first = outer // 2 if b >= 8 else 0
        offset = {8: 7, 9: 3}.get(b, b)
        for j in range(got[b].shape[0]):
            copies.append((b, j, block, 8 * (first + j) + offset, block))
        sources.append(got[b])
    return sources, copies


def lay_rows(copies, sources, targets, sems, me):
    started = []
    for number, (source, entry, rows, offset, block) in enumerate(copies):
        row = 0 if offset is None else pl.multiple_of((me ^ offset) * block, 16)
        column = 0
        for k, target in enumerate(targets):
            cols = target.shape[1]
            copy = pltpu.make_async_copy(
                sources[source].at[entry, :, pl.ds(column, cols)],
                target.at[pl.ds(row, rows)],
                sems.at[len(targets) * number + k],
            )
            copy.start()
            started.append(copy)
            column += cols
    for copy in started:
        copy.wait()


def part_order(count):
    outer = count // CUBE
    return [(b, (0, outer)) for b in range(7)] + [(7, span) for span in halves(outer)]


def part_shapes(count, block, width):
    if block % 16:
        return [jax.ShapeDtypeStruct((count * block, width), bf16)]
    return [
        jax.ShapeDtypeStruct((span[1] - span[0], block, width), bf16)
        for _, span in part_order(count)
    ]


def store_parts(whole, parts, me, block, at):
    cols = pl.ds(at, whole.shape[1])
    if len(parts) == 1:
        parts[0][:, cols] = whole[...].astype(bf16)
        return
    for part, (offset, span) in zip(parts, part_order(whole.shape[0] // block)):
        for j in range(part.shape[0]):
            row = pl.multiple_of((me ^ (8 * (span[0] + j) + offset)) * block, 16)
            part[j, :, cols] = whole[pl.ds(row, block)].astype(bf16)


def spread_parts(parts, me, count):
    if len(parts) > 1:
        return dict(enumerate(parts))
    blocks = parts[0].reshape(count, parts[0].shape[0] // count, -1)
    return {
        k: blocks[(offset + CUBE * jnp.arange(*span)) ^ me]
        for k, (offset, span) in enumerate(part_order(count))
    }


def outer_sum(total, count):
    for bit in reversed(outer_bits(count)):
        half = total.shape[0] // 2
        total = total[:half] + swap(total[half:].astype(bf16), bit, count).astype(f32)
    return total[0]


def vmem_call(kernel, out_shapes, scratch, args, name, smem=(), flops=0):
    spaces = {0: pltpu.VMEM, 1: pltpu.SMEM, 2: pl.ANY}
    moved = sum(math.prod(o.shape) * o.dtype.itemsize for o in out_shapes)
    moved += sum(math.prod(a.shape) * a.dtype.itemsize for a, _ in args)
    return pl.pallas_call(
        kernel,
        out_shape=out_shapes,
        in_specs=[pl.BlockSpec(memory_space=spaces[space]) for _, space in args],
        out_specs=[pl.BlockSpec(memory_space=pltpu.VMEM)] * len(out_shapes),
        scratch_shapes=scratch,
        compiler_params=pltpu.CompilerParams(vmem_limit_bytes=60 * 1024 * 1024),
        cost_estimate=FREE if name in LIGHT else BRIEF,
        name=name,
    )(*[a for a, _ in args])


def turn(values, cosine, sine):
    return values * cosine + pltpu.roll(values, values.shape[1] // 2, 1) * sine


def masks(seg_col, seg_row, splits):
    out = []
    for low, high in splits:
        shape = (high - low, high)
        query_at = lax.broadcasted_iota(jnp.int32, shape, 0) + low
        key_at = lax.broadcasted_iota(jnp.int32, shape, 1)
        allowed = (seg_col[low:high] == seg_row[:, :high]) & (key_at <= query_at)
        out.append(jnp.where(allowed, 0.0, -1e30))
    return out


def row_splits(length):
    return [(at, at + length // 2) for at in (0, length // 2)]


def attend_kernel(
    copies, sizes, at_ref, own_ref, other_ref, seg_col, seg_row, cos_ref, sin_ref, *refs
):
    heads, kv_heads, sources = sizes
    pieces = refs[:sources]
    hid, normed, qs, ks, vs, mixed, lse, weights, small, out_weights, gains = refs[sources:-3]
    own, other, sems = refs[-3:]
    me, core = at_ref[0], at_ref[1]
    rows = own_ref.shape[0]
    length = 2 * rows
    hid[pl.ds(pl.multiple_of(core * rows, rows), rows)] = own_ref[...]
    hid[pl.ds(pl.multiple_of((1 - core) * rows, rows), rows)] = other_ref[...]
    lay_rows(copies, pieces, (weights, small, out_weights), sems, me)
    gains[...] = jnp.transpose(small[...].astype(f32))[: gains.shape[0]]
    value = hid[...].astype(f32)
    root = lax.rsqrt(jnp.mean(value * value, axis=1, keepdims=True) + epsilon)
    normed[...] = (value * root * gains[GAIN_A : GAIN_A + 1]).astype(bf16)
    qkv = lax.dot_general(normed[...], weights[...], NN, preferred_element_type=f32)
    cosine, sine = cos_ref[...], sin_ref[...]
    for head in range(heads):
        at = slice(head * HD, (head + 1) * HD)
        qs[:, at] = turn(qkv[:, at], cosine, sine).astype(bf16)
    for head in range(kv_heads):
        at = slice(head * HD, (head + 1) * HD)
        ks[:, at] = turn(qkv[:, heads * HD :][:, at], cosine, sine).astype(bf16)
    vs[...] = qkv[:, (heads + kv_heads) * HD :].astype(bf16)
    splits = row_splits(length)
    scale = 1.0 / math.sqrt(HD)
    for (low, high), mask in zip(splits, masks(seg_col[...], seg_row[...], splits)):
        for head in range(heads):
            at = slice(head * HD, (head + 1) * HD)
            kv = head // (heads // kv_heads)
            kv = slice(kv * HD, (kv + 1) * HD)
            scores = lax.dot_general(
                qs[low:high, at], ks[:high, kv], NT, preferred_element_type=f32
            )
            scores = scores * scale + mask
            peak = jnp.max(scores, axis=1, keepdims=True)
            expo = jnp.exp(scores - peak)
            total = jnp.sum(expo, axis=1, keepdims=True)
            lse[low:high, head : head + 1] = peak + jnp.log(total)
            probs = (expo * (1.0 / total)).astype(bf16)
            mixed[low:high, at] = lax.dot_general(
                probs, vs[:high, kv], NN, preferred_element_type=f32
            ).astype(bf16)
    for target, half in ((other, 1 - core), (own, core)):
        part = mixed[pl.ds(pl.multiple_of(half * rows, rows), rows)]
        target[...] = lax.dot_general(
            part, out_weights[...], NT, preferred_element_type=f32
        ).astype(target.dtype)


def middle_kernel(hidden, own, other, gains, middle, normed):
    value = hidden[...].astype(f32) + own[...] + other[...].astype(f32)
    middle[...] = value
    root = lax.rsqrt(jnp.mean(value * value, axis=1, keepdims=True) + epsilon)
    normed[...] = (value * root * gains[GAIN_F : GAIN_F + 1]).astype(bf16)


def middle_back_kernel(
    middle, normed, grad_out, code, router, gains, own, *refs
):
    others, (grad_middle, grad_round, small) = refs[:-3], refs[-3:]
    width = middle.shape[1]
    total = own[...].astype(f32)
    for other in others:
        total += other[...].astype(f32)
    routed = code[...].astype(f32) > 0.5
    logits = lax.dot_general(normed[...], router[...], NN, preferred_element_type=f32)
    logits = jnp.where(routed, logits, -1e30)
    expo = jnp.where(routed, jnp.exp(logits - jnp.max(logits, axis=1, keepdims=True)), 0.0)
    gates = expo / jnp.sum(expo, axis=1, keepdims=True)
    grad_gates = total[:, width:]
    grad_logits = gates * (grad_gates - jnp.sum(gates * grad_gates, axis=1, keepdims=True))
    high = grad_logits.astype(bf16)
    low = (grad_logits - high.astype(f32)).astype(bf16)
    grad_normed = total[:, :width]
    router_grad = jnp.zeros(small.shape, f32)
    for part in (high, low):
        grad_normed += lax.dot_general(part, router[...], NT, preferred_element_type=f32)
        router_grad += lax.dot_general(normed[...], part, TN, preferred_element_type=f32)
    value = middle[...]
    root = lax.rsqrt(jnp.mean(value * value, axis=1, keepdims=True) + epsilon)
    scaled = value * root
    column = jnp.sum(grad_normed * scaled, axis=0, keepdims=True)
    column = jnp.transpose(jnp.broadcast_to(column, (EXTRA, width)))
    lanes = lax.broadcasted_iota(jnp.int32, small.shape, 1)
    small[...] = jnp.where(lanes == GAIN_F, column, router_grad)
    grad_scaled = grad_normed * gains[GAIN_F : GAIN_F + 1]
    inner = jnp.mean(grad_scaled * scaled, axis=1, keepdims=True)
    result = grad_out[...].astype(f32) + root * (grad_scaled - scaled * inner)
    grad_middle[...] = result
    grad_round[...] = result.astype(bf16)


def attend_back_kernel(
    block,
    sizes,
    at_ref,
    own_ref,
    other_ref,
    mixed,
    out_weights,
    small_ref,
    qs,
    ks,
    vs,
    lse,
    seg_col,
    seg_row,
    cos_ref,
    sin_ref,
    hid,
    normed,
    weights,
    *refs,
):
    heads, kv_heads = sizes
    own, other, parts = refs[0], refs[1], refs[2:-6]
    acc, small, grads, whole, grad_mixed, out_acc = refs[-6:]
    me, core = at_ref[0], at_ref[1]
    length, width = hid.shape
    rows = own.shape[0]
    cols = grads.shape[1]
    whole[pl.ds(pl.multiple_of(core * rows, rows), rows)] = own_ref[...]
    whole[pl.ds(pl.multiple_of((1 - core) * rows, rows), rows)] = other_ref[...]
    grad_mixed[...] = lax.dot_general(
        whole[...], out_weights[...], NN, preferred_element_type=f32
    ).astype(bf16)
    out_acc[...] = lax.dot_general(whole[...], mixed[...], TN, preferred_element_type=f32)
    store_parts(out_acc, parts, me, block, cols + EXTRA)
    cosine, sine = cos_ref[...], -sin_ref[...]
    splits = row_splits(length)
    scale = 1.0 / math.sqrt(HD)
    per_group = heads // kv_heads
    bias = masks(seg_col[...], seg_row[...], splits)
    for kv_head in range(kv_heads):
        kv = slice(kv_head * HD, (kv_head + 1) * HD)
        grad_key = jnp.zeros((length, HD), f32)
        grad_value = jnp.zeros((length, HD), f32)
        for (low, high), mask in zip(splits, bias):
            key_sum = jnp.zeros((high, HD), f32)
            value_sum = jnp.zeros((high, HD), f32)
            for head in range(kv_head * per_group, (kv_head + 1) * per_group):
                at = slice(head * HD, (head + 1) * HD)
                query, grad = qs[low:high, at], grad_mixed[low:high, at]
                scores = lax.dot_general(query, ks[:high, kv], NT, preferred_element_type=f32)
                probs = jnp.exp(scores * scale + mask - lse[low:high, head : head + 1])
                grad_probs = lax.dot_general(
                    grad, vs[:high, kv], NT, preferred_element_type=f32
                )
                inner = jnp.sum(grad_probs * probs, axis=1, keepdims=True)
                grad_scores = (probs * (grad_probs - inner)).astype(bf16)
                grad_query = lax.dot_general(
                    grad_scores, ks[:high, kv], NN, preferred_element_type=f32
                )
                grads[low:high, at] = turn(
                    grad_query * scale, cosine[low:high], sine[low:high]
                ).astype(bf16)
                key_sum += lax.dot_general(grad_scores, query, TN, preferred_element_type=f32)
                value_sum += lax.dot_general(
                    probs.astype(bf16), grad, TN, preferred_element_type=f32
                )
            if high < length:
                pad = jnp.zeros((length - high, HD), f32)
                key_sum = jnp.concatenate([key_sum, pad], axis=0)
                value_sum = jnp.concatenate([value_sum, pad], axis=0)
            grad_key += key_sum
            grad_value += value_sum
        at = (heads + kv_head) * HD
        grads[:, at : at + HD] = turn(grad_key * scale, cosine, sine).astype(bf16)
        at += kv_heads * HD
        grads[:, at : at + HD] = grad_value.astype(bf16)
    acc[...] = lax.dot_general(normed[...], grads[...], TN, preferred_element_type=f32)
    store_parts(acc, parts, me, block, 0)
    value = hid[...].astype(f32)
    root = lax.rsqrt(jnp.mean(value * value, axis=1, keepdims=True) + epsilon)
    column = jnp.zeros((1, width), f32)
    for target, half in ((other, 1 - core), (own, core)):
        at = pl.ds(pl.multiple_of(half * rows, rows), rows)
        part = lax.dot_general(grads[at], weights[...], NT, preferred_element_type=f32)
        target[...] = part.astype(target.dtype)
        half_value = hid[at].astype(f32)
        half_root = lax.rsqrt(jnp.mean(half_value * half_value, axis=1, keepdims=True) + epsilon)
        column += jnp.sum(part * (half_value * half_root), axis=0, keepdims=True)
    lanes = lax.broadcasted_iota(jnp.int32, small.shape, 1)
    column = jnp.transpose(jnp.broadcast_to(column, (EXTRA, width)))
    small[...] = jnp.where(lanes == GAIN_A, column, small_ref[...])
    store_parts(small, parts, me, block, cols)


def slots_kernel(parts, at_ref, order_col, order_row, own, other, code, *refs):
    picks, rows_out, whole = refs[: len(parts)], refs[-2], refs[-1]
    core = at_ref[1]
    rows = own.shape[0]
    width = own.shape[1]
    whole[pl.ds(pl.multiple_of(core * rows, rows), rows), :width] = own[...]
    whole[pl.ds(pl.multiple_of((1 - core) * rows, rows), rows), :width] = other[...]
    whole[:, width:] = code[...]
    none = order_row.shape[0] // 2 * order_row.shape[1]
    first = core * sum(parts)
    for expert in range(order_row.shape[0]):
        row = order_row[expert : expert + 1, :]
        ahead = (order_col[:, expert : expert + 1] < row).astype(f32)
        position = jnp.sum(ahead, axis=0, keepdims=True).astype(jnp.int32)
        position = jnp.where(row < none, position, -1)
        low = first
        for pick, count in zip(picks, parts):
            slot = lax.broadcasted_iota(jnp.int32, (count, row.shape[1]), 0) + low
            pick[expert * count : (expert + 1) * count, :] = (slot == position).astype(bf16)
            low = low + count
    low = 0
    for pick, count in zip(picks, parts):
        taken = lax.dot_general(pick[...], whole[...], NN, preferred_element_type=f32)
        rows_out[:, low : low + count] = taken.astype(bf16).reshape(
            order_row.shape[0], count, whole.shape[1]
        )
        low += count


def take_kernel(at_ref, own, other, *refs):
    count = (len(refs) - 1) // 2
    picks, outs, whole = refs[:count], refs[count:-1], refs[-1]
    core = at_ref[1]
    rows = own.shape[0]
    whole[pl.ds(pl.multiple_of(core * rows, rows), rows)] = own[...]
    whole[pl.ds(pl.multiple_of((1 - core) * rows, rows), rows)] = other[...]
    for pick, out in zip(picks, outs):
        out[...] = lax.dot_general(
            pick[...], whole[...], NN, preferred_element_type=f32
        ).astype(bf16)


def give_kernel(count, at_ref, *refs):
    picks, values, (own, other) = refs[:count], refs[count:-2], refs[-2:]
    rows = own.shape[0]
    if len(values) < count:
        whole, values, low = values[0][...], [], 0
        for pick in picks:
            each = pick.shape[0] // whole.shape[0]
            values.append(whole[:, low : low + each].reshape(pick.shape[0], whole.shape[2]))
            low += each
    for target, half in ((other, 1 - at_ref[1]), (own, at_ref[1])):
        columns = pl.ds(pl.multiple_of(half * rows, rows), rows)
        total = None
        for pick, value in zip(picks, values):
            part = lax.dot_general(
                pick[:, columns], value[...], TN, preferred_element_type=f32
            )
            total = part if total is None else total + part
        target[...] = total.astype(target.dtype)


def gelu_parts(value):
    square = value * value
    inner = value * (0.7978845608028654 + 0.035677408136300125 * square)
    tanh = jnp.tanh(inner)
    half = 0.5 + 0.5 * tanh
    slope = half + 0.5 * value * (1.0 - tanh * tanh) * (
        0.7978845608028654 + 3.0 * 0.035677408136300125 * square
    )
    return value * half, slope


def moe_kernel(plan, at_ref, router_ref, x_in, g_in, *refs):
    copies, hidden, blocks, outer, first, groups = plan
    weight_count = len(set(c[0] for c in copies))
    if first:
        refs = refs[1:]
    sources, outs, refs = refs[:weight_count], refs[weight_count:][:5], refs[weight_count + 5 :]
    weights, xs, gs = refs[:3]
    buffers = refs[3:8]
    weight_sems, in_sems, out_sems = refs[8:]
    branch, gradn, act_all, gp_all, geo_all = buffers
    _, rows, width = xs.shape
    whole = 2 * hidden
    expert = at_ref[0] % CUBE

    weight_copies = []
    block_rows = weights.shape[0] // outer
    for number, (source, entry, low, length, offset, from_col, to_col, cols) in enumerate(copies):
        row = pl.multiple_of(((at_ref[0] // CUBE) ^ offset) * block_rows + low, 16)
        weight_copies.append(
            pltpu.make_async_copy(
                sources[source].at[entry, :, pl.ds(from_col, cols)],
                weights.at[pl.ds(row, length), pl.ds(to_col, cols)],
                weight_sems.at[number],
            )
        )
    weight_order = sorted(range(len(copies)), key=lambda k: copies[k][5] // hidden)
    in_copies = []
    for block in range(blocks):
        span = pl.ds(block * rows, rows)
        for kind, (source, target) in enumerate(((x_in, xs), (g_in, gs))):
            held = (span,)
            if kind == 1:
                held = pl.ds(block * groups, groups), pl.ds(first, rows // groups)
            in_copies.append(
                pltpu.make_async_copy(
                    source.at[held], target.at[block], in_sems.at[2 * block + kind]
                )
            )
    in_copies[0].start()
    for k in weight_order:
        weight_copies[k].start()
    for copy in in_copies[1:]:
        copy.start()
    out_copies = []
    for block in range(blocks):
        in_copies[2 * block].wait()
        x = xs[block]
        logits = lax.dot_general(x, router_ref[...], NN, preferred_element_type=f32)
        if block == 0:
            for k in weight_order:
                if copies[k][5] < 2 * hidden:
                    weight_copies[k].wait()
        pre = lax.dot_general(x, weights[:, : 2 * whole], NN, preferred_element_type=f32)
        in_copies[2 * block + 1].wait()
        both = gs[block].reshape(rows, gs.shape[3])
        routed = both[:, width:].astype(f32) > 0.5
        lanes = lax.broadcasted_iota(jnp.int32, routed.shape, 1)
        logits = jnp.where(routed, logits, -1e30)
        expo = jnp.where(routed, jnp.exp(logits - jnp.max(logits, axis=1, keepdims=True)), 0.0)
        total = jnp.sum(expo, axis=1, keepdims=True)
        gate = jnp.sum(jnp.where(lanes == expert, expo, 0.0), axis=1, keepdims=True)
        gate = gate / jnp.where(total > 0.0, total, 1.0)

        gate_pre, up_pre = pre[:, :whole], pre[:, whole:]
        gelu, slope = gelu_parts(gate_pre)
        act = (gelu * up_pre).astype(bf16)
        act_all[block] = act
        if block == 0:
            for k in weight_order:
                if copies[k][5] == 2 * hidden:
                    weight_copies[k].wait()
        down = weights[:, 2 * whole :]
        expert_out = lax.dot_general(act, down, NT, preferred_element_type=f32)
        branch[block] = (gate * expert_out).astype(bf16).reshape(branch.shape[1:])
        g = both[:, :width].astype(f32)
        grad_gate = jnp.sum(g * expert_out, axis=1, keepdims=True)
        gradn[block, :, width:] = jnp.where(lanes == expert, grad_gate, 0.0).astype(bf16)
        geo = (gate * g).astype(bf16)
        geo_all[block] = geo
        grad_act = lax.dot_general(geo, down, NN, preferred_element_type=f32)
        grad_gate_pre = (grad_act * up_pre * slope).astype(bf16)
        grad_up_pre = (grad_act * gelu).astype(bf16)
        for side in range(2):
            cols = slice(side * hidden, (side + 1) * hidden)
            for kind, part in enumerate((grad_gate_pre, grad_up_pre)):
                at = (2 * side + kind) * hidden
                gp_all[block, :, at : at + hidden] = part[:, cols]
        grad_in = lax.dot_general(
            grad_gate_pre, weights[:, :whole], NT, preferred_element_type=f32
        ) + lax.dot_general(
            grad_up_pre, weights[:, whole : 2 * whole], NT, preferred_element_type=f32
        )
        gradn[block, :, :width] = grad_in.astype(bf16)
        for number, (source, target) in enumerate(zip(buffers, outs)):
            if number == 0:
                held = pl.ds(block * groups, groups), pl.ds(first, rows // groups)
            else:
                held = (pl.ds(block * rows, rows),)
            copy = pltpu.make_async_copy(
                source.at[block], target.at[held], out_sems.at[5 * block + number]
            )
            copy.start()
            out_copies.append(copy)
    for copy in out_copies:
        copy.wait()


def moe(at, x, g, router, pieces, hidden, outer, sequences, capacity, branch=None):
    copies = []
    for source, (array, first, low, side) in enumerate(pieces):
        for entry in range(array.shape[0]):
            for kind in range(3):
                copies.append(
                    (source, entry, low, array.shape[1], first + entry, kind * hidden)
                    + ((2 * kind + side) * hidden, hidden)
                )
    total, width = x.shape
    blocks = 2
    rows = total // blocks
    widths = (width, width + EXTRA, 2 * hidden, 4 * hidden, width)
    each = total // sequences
    first = 0 if branch is None else capacity - each
    args = [x, g] + ([] if branch is None else [branch]) + [p[0] for p in pieces]
    groups = sequences // blocks
    buffers = [(blocks, rows, w) for w in widths]
    buffers[0] = (blocks, groups, each, width)
    return pl.pallas_call(
        functools.partial(moe_kernel, (copies, hidden, blocks, outer, first, groups)),
        out_shape=[jax.ShapeDtypeStruct((sequences, capacity, width), bf16)]
        + [jax.ShapeDtypeStruct((total, w), bf16) for w in widths[1:]],
        in_specs=[pl.BlockSpec(memory_space=pltpu.SMEM), pl.BlockSpec(memory_space=pltpu.VMEM)]
        + [pl.BlockSpec(memory_space=pl.ANY)] * len(args),
        out_specs=[pl.BlockSpec(memory_space=pl.ANY)] * 5,
        scratch_shapes=[
            pltpu.VMEM((width, 6 * hidden), bf16),
            pltpu.VMEM((blocks, rows, width), bf16),
            pltpu.VMEM((blocks, groups, each, width + EXTRA), bf16),
        ]
        + [pltpu.VMEM(dims, bf16) for dims in buffers]
        + [
            pltpu.SemaphoreType.DMA((len(copies),)),
            pltpu.SemaphoreType.DMA((2 * blocks,)),
            pltpu.SemaphoreType.DMA((5 * blocks,)),
        ],
        input_output_aliases={} if branch is None else {4: 0},
        compiler_params=pltpu.CompilerParams(vmem_limit_bytes=60 * 1024 * 1024),
        cost_estimate=BRIEF,
        name="experts",
    )(at, router, *args)


def weight_grads_kernel(calls, at_ref, *refs):
    pairs = []
    for _ in range(2):
        pairs.append((refs[:calls], refs[calls : 2 * calls]))
        refs = refs[2 * calls :]
    own, other, *buffers, sems = refs
    cols = buffers[0].shape[1]
    columns = pl.ds(pl.multiple_of(at_ref[2] * cols, cols), cols)
    copies = []
    for number, (lefts, rights) in enumerate(pairs):
        row = 0
        for left, right in zip(lefts, rights):
            rows = pl.ds(row, left.shape[0])
            for source, target in (
                (left.at[:, columns], buffers[2 * number].at[rows]),
                (right, buffers[2 * number + 1].at[rows]),
            ):
                copies.append(pltpu.make_async_copy(source, target, sems.at[len(copies)]))
                copies[-1].start()
            row += left.shape[0]
    at = 0
    for number in range(2):
        for copy in copies[2 * calls * number : 2 * calls * (number + 1)]:
            copy.wait()
        total = lax.dot_general(
            buffers[2 * number][...],
            buffers[2 * number + 1][...],
            TN,
            preferred_element_type=f32,
        ).astype(bf16)
        width = total.shape[1] // 2
        own[:, at : at + width] = total[:, :width]
        other[:, at : at + width] = total[:, width:]
        at += width


def weight_grads(at, half, pre, down):
    args, scratch, width = [], [], 0
    for pairs in (pre, down):
        args += [p[0] for p in pairs] + [p[1] for p in pairs]
        rows = sum(p[0].shape[0] for p in pairs)
        left, right = pairs[0][0].shape[1] // 2, pairs[0][1].shape[1]
        scratch += [(rows, left), (rows, right)]
        width += right // 2
    return pl.pallas_call(
        functools.partial(weight_grads_kernel, len(pre)),
        out_shape=[jax.ShapeDtypeStruct((left, width), bf16)] * 2,
        in_specs=[pl.BlockSpec(memory_space=pltpu.SMEM)]
        + [pl.BlockSpec(memory_space=pl.ANY)] * len(args),
        out_specs=[pl.BlockSpec(memory_space=pltpu.VMEM)] * 2,
        scratch_shapes=[pltpu.VMEM(dims, bf16) for dims in scratch]
        + [pltpu.SemaphoreType.DMA((len(args),))],
        compiler_params=pltpu.CompilerParams(vmem_limit_bytes=60 * 1024 * 1024),
        cost_estimate=FREE,
        name="weight_grads",
    )(jnp.concatenate([at, half.reshape(1)]), *args)


def per_device(
    count,
    hidden_in,
    segment_ids,
    routes,
    slot_order,
    gain_attn,
    w_query,
    w_key,
    w_value,
    w_out,
    gain_ffn,
    w_router,
    w_gate,
    w_up,
    w_down,
    grad_out,
):
    tok_rows, width = hidden_in.shape
    seq_len = segment_ids.shape[0]
    top_count = routes.shape[1]
    experts, block, hidden = w_gate.shape
    capacity = 9 * seq_len * top_count // (8 * experts)
    me = lax.axis_index("dp").astype(jnp.int32)
    core = lax.axis_index("tensor").astype(jnp.int32)
    at = jnp.stack([me, core])
    groups = [list(range(first, first + CUBE)) for first in range(0, count, CUBE)]
    heads_cols, kv_cols = w_query.shape[1], w_key.shape[1]
    qkv_cols = heads_cols + 2 * kv_cols
    heads, kv_heads = heads_cols // HD, kv_cols // HD

    def shape(rows, cols, dtype=bf16):
        return jax.ShapeDtypeStruct((rows, cols), dtype)

    def near(own):
        return {0: own} | {bit: swap(own, bit, count) for bit in NEAR}

    def far(got):
        spans = halves(got[0].shape[0])
        return got | {
            3: swap(cut(got[2], spans[0], 0), 1, count),
            9: swap(cut(got[1], spans[1], 0), 2, count),
            6: swap(got[4], 2, count),
            5: swap(got[4], 1, count),
        }

    def last(got):
        spans = halves(got[0].shape[0])
        return got | {
            7: swap(cut(got[6], spans[0], 0), 1, count),
            8: swap(cut(got[5], spans[1], 0), 2, count),
        }

    small = jnp.concatenate([w_router, gain_attn[:, None], gain_ffn[:, None]], axis=1)
    small = jnp.pad(small, ((0, 0), (0, EXTRA - small.shape[1])))
    pair = outer_pair(
        jnp.concatenate([w_query, w_key, w_value, small, w_out.T], axis=1), count
    )
    hidden_other = swap_core(hidden_in)

    expert_shard = jnp.concatenate([w_gate, w_up, jnp.swapaxes(w_down, 1, 2)], axis=2)
    expert_rows = lax.all_to_all(
        expert_shard.reshape(experts * block, 3 * hidden),
        "dp",
        0,
        0,
        tiled=True,
        axis_index_groups=groups,
    )

    order = jnp.min(
        jnp.where(
            routes[:, :, None] == jnp.arange(experts, dtype=jnp.int32),
            slot_order[0].reshape(seq_len, top_count)[:, :, None],
            seq_len * top_count,
        ),
        axis=1,
    )
    code = (order < seq_len * top_count).astype(bf16)
    code = jnp.pad(code, ((0, 0), (0, EXTRA - experts)))
    code_own = lax.dynamic_slice_in_dim(code, core * tok_rows, tok_rows, 0)
    first_part = capacity // 4 // 16 * 16
    slot_parts = (first_part, capacity // 2 - first_part)
    grad_other = swap_core(grad_out)
    slots = vmem_call(
        functools.partial(slots_kernel, slot_parts),
        [shape(experts * part, seq_len) for part in slot_parts]
        + [jax.ShapeDtypeStruct((experts, sum(slot_parts), width + EXTRA), bf16)],
        [pltpu.VMEM((seq_len, width + EXTRA), bf16)],
        [(at, 1), (order, 0), (order.T, 0), (grad_out, 0), (grad_other, 0), (code, 0)],
        "slots",
    )
    picks, grad_rows = slots[:2], slots[2]

    def exchange(rows):
        return lax.all_to_all(rows, "dp", 0, 0, tiled=True, axis_index_groups=groups)

    cosine, sine_table = rope_tables(seq_len, HD)
    cosine = jnp.concatenate([cosine, cosine], axis=1)
    sine_table = jnp.concatenate([-sine_table, sine_table], axis=1)
    seg_col, seg_row = segment_ids[:, None], segment_ids[None, :]

    pair, expert_rows = gate([pair, expert_rows], cosine, sine_table, hidden_other, grad_other)
    if count == 2 * CUBE:
        edges = [expert_rows.shape[0] * k // 48 // 16 * 16 for k in (0, 10, 25, 31, 44, 48)]
    else:
        edges = [0] * 5 + [expert_rows.shape[0]]
    pieces = [(expert_rows[None], 0, 0, 0), (swap_core(expert_rows)[None], 0, 0, 1)]

    def outer_chunk(k, *events):
        low, high = edges[k], edges[k + 1]
        if high == low:
            return [], []
        (chunk,) = gate([cut(expert_rows, (low, high), 0)], *events)
        arrays, first, swapped = outer_gather(chunk, count)[1:], 1, []
        for array in arrays:
            swapped.append(swap_core(array))
            pieces.append((array, first, low, 0))
            pieces.append((swapped[-1], first, low, 1))
            first += array.shape[0]
        return arrays, swapped

    with jax.named_scope("weights_near"):
        got = near(pair)
    arrays, swapped = outer_chunk(0, pair)
    got = gate_dict(got, NEAR, grad_rows, arrays, pieces[1][0])
    with jax.named_scope("weights_far"):
        got = far(got)
    arrays, swapped_next = outer_chunk(1, got[1])
    got = gate_dict(got, FAR, arrays, swapped)
    with jax.named_scope("weights_last"):
        got = last(got)
    arrays, swapped = outer_chunk(2, got[3])
    got = gate_dict(got, LAST, arrays, swapped_next)
    sources, copies = piece_copies(got, block, me, count)
    grad_rows, seg_col = gate([grad_rows, seg_col], got[7])
    with jax.named_scope("grads_rows"):
        grad_rows = exchange(grad_rows)
    attended = vmem_call(
        functools.partial(attend_kernel, copies, (heads, kv_heads, len(sources))),
        [
            shape(seq_len, width),
            shape(seq_len, width),
            shape(seq_len, heads_cols),
            shape(seq_len, kv_cols),
            shape(seq_len, kv_cols),
            shape(seq_len, heads_cols),
            shape(seq_len, HD, f32),
            shape(width, qkv_cols),
            shape(width, EXTRA),
            shape(width, heads_cols),
            shape(16, width, f32),
            shape(tok_rows, width, f32),
            shape(tok_rows, width),
        ],
        [pltpu.SemaphoreType.DMA((3 * len(copies),))],
        [(at, 1), (hidden_in, 0), (hidden_other, 0), (seg_col, 0), (seg_row, 0)]
        + [(cosine, 0), (sine_table, 0)]
        + [(piece, 2) for piece in sources],
        "attend",
        flops=2 * seq_len * (width * (qkv_cols + heads_cols) + heads_cols * seq_len),
    )
    hid, normed, qs, ks, vs, mixed, lse, full_qkv, router, out_wt, gains = attended[:-2]
    attn_own, attn_other = attended[-2:]
    arrays, swapped_next = outer_chunk(3, got[7])
    middle, normed2 = vmem_call(
        middle_kernel,
        [shape(tok_rows, width, f32), shape(tok_rows, width)],
        [],
        [(hidden_in, 0), (attn_own, 0), (swap_core(attn_other), 0), (gains, 0)],
        "middle",
    )

    rows = vmem_call(
        take_kernel,
        [shape(experts * part, width) for part in slot_parts],
        [pltpu.VMEM((seq_len, width), bf16)],
        [(at, 1), (normed2, 0), (swap_core(normed2), 0)] + [(pick, 0) for pick in picks],
        "take",
    )
    rows = list(rows)
    rows[0], grad_rows = gate([rows[0], grad_rows], arrays, swapped)
    with jax.named_scope("tokens_rows"):
        x_first = exchange(rows[0])
    arrays, _ = outer_chunk(4, rows[0])
    x_first, rows_second = gate([x_first, rows[1]], arrays, swapped_next)
    with jax.named_scope("tokens_rows"):
        x_second = exchange(rows_second)

    def experts_on(x, g, router, branch=None):
        held = (CUBE, sum(slot_parts))
        return moe(at, x, g, router, pieces, hidden, count // CUBE, *held, branch)

    branch, gradn_first, *first = experts_on(x_first, grad_rows, router)
    with jax.named_scope("gradn_rows"):
        gradn_first = exchange(gradn_first)
    (second_router,) = gate([router], first[0])
    branch, gradn_second, *second = experts_on(x_second, grad_rows, second_router, branch)

    xs = (x_first, x_second)
    pre_pairs = [(x, call[1]) for x, call in zip(xs, (first, second))]
    down_pairs = [(call[2], call[0]) for call in (first, second)]
    bits = outer_bits(count)
    top = (me // bits[-1]) % 2 if bits else jnp.zeros((), jnp.int32)

    def half_grads(half, *events):
        half = gate([half.reshape(1)], *events)[0]
        return weight_grads(at, half, pre_pairs, down_pairs)

    with jax.named_scope("gradn_rows"):
        gradn_second = exchange(gradn_second)
    sent, sent_other = half_grads(1 - top, second[0])
    keep, keep_other = half_grads(top, sent_other)
    with jax.named_scope("expert_scatter"):
        sent = add_round(sent, swap_core(sent_other))
        sent_got = swap(sent, bits[-1], count) if bits else sent

    def give(picks, values, name):
        own, other = vmem_call(
            functools.partial(give_kernel, len(picks)),
            [shape(tok_rows, values[0].shape[-1], f32), shape(tok_rows, values[0].shape[-1])],
            [],
            [(at, 1)] + [(pick, 0) for pick in picks] + [(value, 0) for value in values],
            name,
        )
        return own, swap_core(other)

    gradn_second, gradn_first = gate([gradn_second, gradn_first], sent, keep)
    gradn = list(give(picks, (gradn_first, gradn_second), "give_gradn"))

    grad_middle, grad_mid_r, small_f = vmem_call(
        middle_back_kernel,
        [shape(tok_rows, width, f32), shape(tok_rows, width), shape(width, EXTRA, f32)],
        [],
        [(middle, 0), (normed2, 0), (grad_out, 0), (code_own, 0), (router, 0), (gains, 0)]
        + [(array, 0) for array in gradn],
        "middle_back",
    )

    grad_mid_other = swap_core(grad_mid_r)
    (branch,) = gate([branch], gradn_second)
    with jax.named_scope("branch_rows"):
        branch = exchange(branch)
    normed_own, normed_other, *parts = vmem_call(
        functools.partial(attend_back_kernel, block, (heads, kv_heads)),
        [shape(tok_rows, width, f32), shape(tok_rows, width)]
        + part_shapes(count, block, qkv_cols + EXTRA + heads_cols),
        [
            pltpu.VMEM((width, qkv_cols), f32),
            pltpu.VMEM((width, EXTRA), f32),
            pltpu.VMEM((seq_len, qkv_cols), bf16),
            pltpu.VMEM((seq_len, width), bf16),
            pltpu.VMEM((seq_len, heads_cols), bf16),
            pltpu.VMEM((width, heads_cols), f32),
        ],
        [(at, 1), (grad_mid_r, 0), (grad_mid_other, 0), (mixed, 0), (out_wt, 0)]
        + [(small_f, 0), (qs, 0), (ks, 0), (vs, 0), (lse, 0), (seg_col, 0)]
        + [(seg_row, 0), (cosine, 0), (sine_table, 0), (hid, 0), (normed, 0), (full_qkv, 0)],
        "attend_back",
        flops=4 * seq_len * (width * (qkv_cols + heads_cols) + 2 * heads_cols * seq_len),
    )
    parts = spread_parts(parts, me, count)

    parts = gate_dict(parts, (3,) + LAST)
    with jax.named_scope("attn_last"):
        got = sum_last(parts, count)
    normed_swapped = swap_core(normed_other)
    gated = gate([got[7], got[8], parts[3]], normed_swapped)
    got, parts[3] = dict(zip(LAST, gated)), gated[2]
    with jax.named_scope("attn_far"):
        terms = far_terms(parts, got)
        attn_far = sum_far(parts, terms, count)
    with jax.named_scope("expert_scatter"):
        sent_got, keep = gate([sent_got, keep], terms)
        keep_swapped = swap_core(keep_other)
        if bits:
            total = keep.astype(f32) + keep_swapped.astype(f32) + sent_got.astype(f32)
        else:
            total = jnp.concatenate([add_round(keep, keep_swapped), sent_got]).astype(f32)
        for bit in reversed(bits[:-1]):
            half = total.shape[0] // 2
            high = (me // bit) % 2
            mine = lax.dynamic_slice_in_dim(total, high * half, half, 0)
            other = lax.dynamic_slice_in_dim(total, (1 - high) * half, half, 0)
            total = mine + swap(other.astype(bf16), bit, count).astype(f32)
        total = total.astype(bf16)
    grad_normed = normed_own + normed_swapped.astype(f32)
    gated = gate([attn_far[k] for k in NEAR] + [branch, total])
    attn_far, branch, total = dict(zip(NEAR, gated)), gated[3], gated[4]
    with jax.named_scope("attn_near"):
        attn_near = sum_near(near_terms(parts, attn_far), count)
    branch_own, branch_other = give(picks, (branch,), "give_branch")
    with jax.named_scope("expert_scatter"):
        total = exchange(total)
    attn_near = gate_dict(attn_near, NEAR, branch_own)
    with jax.named_scope("attn_outer"):
        attn_grads = outer_sum(sum_own(parts, attn_near), count)
    layer_out = middle + branch_own + branch_other.astype(f32)

    expert_grads = total.reshape(experts, block, 3 * hidden).astype(f32)
    grad_gate_w = expert_grads[:, :, :hidden]
    grad_up_w = expert_grads[:, :, hidden : 2 * hidden]
    grad_down_w = jnp.swapaxes(expert_grads[:, :, 2 * hidden :], 1, 2)
    scaled_in, root_in = rms_parts(hidden_in.astype(f32))
    grad_in = grad_middle + norm_backward(grad_normed, scaled_in, root_in, gains[GAIN_A])
    smalls = attn_grads[:, qkv_cols : qkv_cols + EXTRA]
    smalls = smalls + swap_core(smalls)
    return (
        layer_out,
        grad_in,
        smalls[:, GAIN_A],
        attn_grads[:, :heads_cols],
        attn_grads[:, heads_cols : heads_cols + kv_cols],
        attn_grads[:, heads_cols + kv_cols : qkv_cols],
        attn_grads[:, qkv_cols + EXTRA :].T,
        smalls[:, GAIN_F],
        smalls[:, :experts],
        grad_gate_w,
        grad_up_w,
        grad_down_w,
    )


def solution(mesh):
    return jax.shard_map(
        functools.partial(per_device, mesh.shape["dp"]),
        mesh=mesh,
        in_specs=(
            P(("dp", "tensor"), None),
            P("dp"),
            P("dp", None),
            P("dp", None),
            P("dp"),
            P("dp", "tensor"),
            P("dp", "tensor"),
            P("dp", "tensor"),
            P("tensor", "dp"),
            P("dp"),
            P("dp", None),
            P(None, "dp", "tensor"),
            P(None, "dp", "tensor"),
            P(None, "tensor", "dp"),
            P(("dp", "tensor"), None),
        ),
        out_specs=(
            P(("dp", "tensor"), None),
            P(("dp", "tensor"), None),
            P("dp"),
            P("dp", "tensor"),
            P("dp", "tensor"),
            P("dp", "tensor"),
            P("tensor", "dp"),
            P("dp"),
            P("dp", None),
            P(None, "dp", "tensor"),
            P(None, "dp", "tensor"),
            P(None, "tensor", "dp"),
        ),
        check_vma=False,
    )
```

```python
import functools
import math

import jax
import jax.numpy as jnp
from jax import lax
from jax.experimental import pallas as pl
from jax.experimental.pallas import tpu as pltpu
from jax.sharding import PartitionSpec as P

HD = 128
EXTRA = 128
GAIN_A, GAIN_F = 8, 9
CUBE = 8
BRIEF = pl.CostEstimate(flops=0, bytes_accessed=3_000_000, transcendentals=0)
LIGHT = ("attend", "middle", "take", "give_gradn", "middle_back", "attend_back")
FREE = pl.CostEstimate(flops=0, bytes_accessed=0, transcendentals=0)
epsilon = 1e-06
highest = lax.Precision.HIGHEST
f32 = jnp.float32
bf16 = jnp.bfloat16
NN = (((1,), (0,)), ((), ()))
NT = (((1,), (1,)), ((), ()))
TN = (((0,), (0,)), ((), ()))


def rms_parts(values):
    inverse_root = lax.rsqrt(jnp.mean(values * values, axis=-1, keepdims=True) + epsilon)
    return (values * inverse_root, inverse_root)


def norm_backward(grad_normed, scaled, inverse_root, gain):
    grad_scaled = grad_normed * gain
    inner = jnp.mean(grad_scaled * scaled, axis=-1, keepdims=True)
    return inverse_root * (grad_scaled - scaled * inner)


def rope_tables(length, size):
    inverse = 10000.0 ** (-jnp.arange(size // 2, dtype=f32) / (size // 2))
    angle = jnp.arange(length, dtype=f32)[:, None] * inverse[None, :]
    return (jnp.cos(angle), jnp.sin(angle))


def swap(values, bit, count):
    return lax.ppermute(values, "dp", [(i, i ^ bit) for i in range(count)])


def swap_core(values):
    return lax.ppermute(values, "tensor", [(0, 1), (1, 0)])


def gate(values, *events):
    values = list(values)
    flat = jax.tree.leaves(events)
    return pl.pallas_call(
        lambda *refs: None,
        out_shape=[jax.ShapeDtypeStruct(v.shape, v.dtype) for v in values],
        in_specs=[pl.BlockSpec(memory_space=pl.ANY)] * (len(values) + len(flat)),
        out_specs=[pl.BlockSpec(memory_space=pl.ANY)] * len(values),
        input_output_aliases={i: i for i in range(len(values))},
        compiler_params=pltpu.CompilerParams(vmem_limit_bytes=60 * 1024 * 1024),
        cost_estimate=BRIEF,
        name="gate",
    )(*values, *flat)


def gate_dict(got, keys, *events):
    return got | dict(zip(keys, gate([got[k] for k in keys], *events)))


def halves(rows):
    part = rows // 2
    return ((0, part), (part, rows))


def cut(values, span, axis):
    return lax.slice_in_dim(values, span[0], span[1], axis=axis)


NEAR, FAR, LAST = (1, 2, 4), (3, 9, 6, 5), (7, 8)


def add_round(left, right):
    return (left.astype(f32) + right.astype(f32)).astype(bf16)


def sum_last(parts, count):
    return {7: swap(parts[7], 1, count), 8: swap(parts[8], 2, count)}


def patch_kernel(first, second, low, high, first_out, second_out):
    first_out[...] = (first[...].astype(f32) + low[...].astype(f32)).astype(bf16)
    second_out[...] = (second[...].astype(f32) + high[...].astype(f32)).astype(bf16)


def patch(first, second, low, high):
    shape = first.shape
    half = low.shape
    if half[1] % 16:
        return (
            jnp.concatenate([add_round(first[: half[0]], low), first[half[0] :]], axis=0),
            jnp.concatenate([second[: half[0]], add_round(second[half[0] :], high)], axis=0),
        )
    top = pl.BlockSpec(half, lambda i: (0, 0, 0))
    bottom = pl.BlockSpec(half, lambda i: (1, 0, 0))
    return pl.pallas_call(
        patch_kernel,
        grid=(1,),
        out_shape=[jax.ShapeDtypeStruct(shape, bf16)] * 2,
        in_specs=[top, bottom, top, top],
        out_specs=[top, bottom],
        input_output_aliases={0: 0, 1: 1},
        compiler_params=pltpu.CompilerParams(vmem_limit_bytes=60 * 1024 * 1024),
        cost_estimate=FREE,
        name="patch",
    )(first, second, low, high)


def far_terms(parts, got):
    return patch(parts[6], parts[5], got[7], got[8])


def sum_far(parts, terms, count):
    first, second = terms
    return {
        6: swap(first, 2, count),
        5: swap(second, 1, count),
        3: swap(parts[3], 1, count),
        9: swap(parts[9], 2, count),
    }


def terms_kernel(one, two, four, six, five, three, nine, one_out, two_out, four_out):
    four_out[...] = (
        four[...].astype(f32) + six[...].astype(f32) + five[...].astype(f32)
    ).astype(bf16)
    first = three.shape[0]
    two_out[:first] = (two[:first].astype(f32) + three[...].astype(f32)).astype(bf16)
    two_out[first:] = two[first:]
    one_out[:first] = one[:first]
    one_out[first:] = (one[first:].astype(f32) + nine[...].astype(f32)).astype(bf16)


def near_terms(parts, got):
    args = [parts[bit] for bit in NEAR] + [got[k] for k in (6, 5, 3, 9)]
    shape = parts[1].shape
    grid = 6 if shape[1] % 96 == 0 else 1

    def spec(dims):
        return pl.BlockSpec((dims[0], dims[1] // grid, dims[2]), lambda i: (0, i, 0))

    outs = pl.pallas_call(
        terms_kernel,
        grid=(grid,),
        out_shape=[jax.ShapeDtypeStruct(shape, bf16)] * 3,
        in_specs=[spec(arg.shape) for arg in args],
        out_specs=[spec(shape)] * 3,
        compiler_params=pltpu.CompilerParams(vmem_limit_bytes=60 * 1024 * 1024),
        cost_estimate=FREE,
        name="terms",
    )(*args)
    return dict(zip(NEAR, outs))


def sum_near(terms, count):
    return {bit: swap(terms[bit], bit, count) for bit in NEAR}


def sum_own(parts, got):
    return parts[0].astype(f32) + (
        got[1].astype(f32) + (got[2].astype(f32) + got[4].astype(f32))
    )


def outer_bits(count):
    bits, bit = [], CUBE
    while bit < count:
        bits.append(bit)
        bit *= 2
    return bits


def outer_gather(own, count):
    pieces = [own[None]]
    for bit in outer_bits(count):
        pieces.append(swap(jnp.concatenate(pieces, axis=0), bit, count))
    return pieces


def outer_pair(shard, count):
    return jnp.concatenate(outer_gather(shard, count), axis=0)


def piece_copies(got, block, me, count):
    outer = got[0].shape[0]
    if block % 16:
        wholes = got | {3: jnp.concatenate([got[3], got[9]]), 7: jnp.concatenate([got[7], got[8]])}
        stacked = jnp.stack([wholes[b] for b in range(CUBE)], axis=1)
        whole = stacked.reshape(count, block, -1)[jnp.arange(count) ^ me]
        return [whole.reshape(1, count * block, -1)], [(0, 0, count * block, None, block)]
    sources, copies = [], []
    for b in range(CUBE + 2):
        first = outer // 2 if b >= 8 else 0
        offset = {8: 7, 9: 3}.get(b, b)
        for j in range(got[b].shape[0]):
            copies.append((b, j, block, 8 * (first + j) + offset, block))
        sources.append(got[b])
    return sources, copies


def lay_rows(copies, sources, targets, sems, me):
    started = []
    for number, (source, entry, rows, offset, block) in enumerate(copies):
        row = 0 if offset is None else pl.multiple_of((me ^ offset) * block, 16)
        column = 0
        for k, target in enumerate(targets):
            cols = target.shape[1]
            copy = pltpu.make_async_copy(
                sources[source].at[entry, :, pl.ds(column, cols)],
                target.at[pl.ds(row, rows)],
                sems.at[len(targets) * number + k],
            )
            copy.start()
            started.append(copy)
            column += cols
    for copy in started:
        copy.wait()


def part_order(count):
    outer = count // CUBE
    first, second = halves(outer)
    offsets = {3: first, 7: first}
    order = [(b, offsets.get(b, (0, outer))) for b in range(CUBE)]
    return order + [(7, second), (3, second)]


def part_shapes(count, block, width):
    if block % 16:
        return [jax.ShapeDtypeStruct((count * block, width), bf16)]
    return [
        jax.ShapeDtypeStruct((span[1] - span[0], block, width), bf16)
        for _, span in part_order(count)
    ]


def store_parts(whole, parts, me, block, at):
    cols = pl.ds(at, whole.shape[1])
    if len(parts) == 1:
        parts[0][:, cols] = whole[...].astype(bf16)
        return
    for part, (offset, span) in zip(parts, part_order(whole.shape[0] // block)):
        for j in range(part.shape[0]):
            row = pl.multiple_of((me ^ (8 * (span[0] + j) + offset)) * block, 16)
            part[j, :, cols] = whole[pl.ds(row, block)].astype(bf16)


def spread_parts(parts, me, count):
    if len(parts) > 1:
        return dict(enumerate(parts))
    blocks = parts[0].reshape(count, parts[0].shape[0] // count, -1)
    return {
        k: blocks[(offset + CUBE * jnp.arange(*span)) ^ me]
        for k, (offset, span) in enumerate(part_order(count))
    }


def outer_sum(total, count):
    for bit in reversed(outer_bits(count)):
        half = total.shape[0] // 2
        total = total[:half] + swap(total[half:].astype(bf16), bit, count).astype(f32)
    return total[0]


def vmem_call(kernel, out_shapes, scratch, args, name, smem=(), flops=0):
    spaces = {0: pltpu.VMEM, 1: pltpu.SMEM, 2: pl.ANY}
    moved = sum(math.prod(o.shape) * o.dtype.itemsize for o in out_shapes)
    moved += sum(math.prod(a.shape) * a.dtype.itemsize for a, _ in args)
    return pl.pallas_call(
        kernel,
        out_shape=out_shapes,
        in_specs=[pl.BlockSpec(memory_space=spaces[space]) for _, space in args],
        out_specs=[pl.BlockSpec(memory_space=pltpu.VMEM)] * len(out_shapes),
        scratch_shapes=scratch,
        compiler_params=pltpu.CompilerParams(vmem_limit_bytes=60 * 1024 * 1024),
        cost_estimate=FREE if name in LIGHT else BRIEF,
        name=name,
    )(*[a for a, _ in args])


def turn(values, cosine, sine):
    return values * cosine + pltpu.roll(values, values.shape[1] // 2, 1) * sine


def masks(seg_col, seg_row, splits):
    out = []
    for low, high in splits:
        shape = (high - low, high)
        query_at = lax.broadcasted_iota(jnp.int32, shape, 0) + low
        key_at = lax.broadcasted_iota(jnp.int32, shape, 1)
        allowed = (seg_col[low:high] == seg_row[:, :high]) & (key_at <= query_at)
        out.append(jnp.where(allowed, 0.0, -1e30))
    return out


def row_splits(length):
    return [(at, at + length // 2) for at in (0, length // 2)]


def attend_kernel(
    copies, sizes, at_ref, own_ref, other_ref, seg_col, seg_row, cos_ref, sin_ref, *refs
):
    heads, kv_heads, sources = sizes
    pieces = refs[:sources]
    hid, normed, qs, ks, vs, mixed, lse, weights, small, out_weights, gains = refs[sources:-3]
    own, other, sems = refs[-3:]
    me, core = at_ref[0], at_ref[1]
    rows = own_ref.shape[0]
    length = 2 * rows
    hid[pl.ds(pl.multiple_of(core * rows, rows), rows)] = own_ref[...]
    hid[pl.ds(pl.multiple_of((1 - core) * rows, rows), rows)] = other_ref[...]
    lay_rows(copies, pieces, (weights, small, out_weights), sems, me)
    gains[...] = jnp.transpose(small[...].astype(f32))[: gains.shape[0]]
    value = hid[...].astype(f32)
    root = lax.rsqrt(jnp.mean(value * value, axis=1, keepdims=True) + epsilon)
    normed[...] = (value * root * gains[GAIN_A : GAIN_A + 1]).astype(bf16)
    qkv = lax.dot_general(normed[...], weights[...], NN, preferred_element_type=f32)
    cosine, sine = cos_ref[...], sin_ref[...]
    for head in range(heads):
        at = slice(head * HD, (head + 1) * HD)
        qs[:, at] = turn(qkv[:, at], cosine, sine).astype(bf16)
    for head in range(kv_heads):
        at = slice(head * HD, (head + 1) * HD)
        ks[:, at] = turn(qkv[:, heads * HD :][:, at], cosine, sine).astype(bf16)
    vs[...] = qkv[:, (heads + kv_heads) * HD :].astype(bf16)
    splits = row_splits(length)
    scale = 1.0 / math.sqrt(HD)
    for (low, high), mask in zip(splits, masks(seg_col[...], seg_row[...], splits)):
        for head in range(heads):
            at = slice(head * HD, (head + 1) * HD)
            kv = head // (heads // kv_heads)
            kv = slice(kv * HD, (kv + 1) * HD)
            scores = lax.dot_general(
                qs[low:high, at], ks[:high, kv], NT, preferred_element_type=f32
            )
            scores = scores * scale + mask
            peak = jnp.max(scores, axis=1, keepdims=True)
            expo = jnp.exp(scores - peak)
            total = jnp.sum(expo, axis=1, keepdims=True)
            lse[low:high, head : head + 1] = peak + jnp.log(total)
            probs = (expo * (1.0 / total)).astype(bf16)
            mixed[low:high, at] = lax.dot_general(
                probs, vs[:high, kv], NN, preferred_element_type=f32
            ).astype(bf16)
    for target, half in ((other, 1 - core), (own, core)):
        part = mixed[pl.ds(pl.multiple_of(half * rows, rows), rows)]
        target[...] = lax.dot_general(
            part, out_weights[...], NT, preferred_element_type=f32
        ).astype(target.dtype)


def middle_kernel(hidden, own, other, gains, middle, normed):
    value = hidden[...].astype(f32) + own[...] + other[...].astype(f32)
    middle[...] = value
    root = lax.rsqrt(jnp.mean(value * value, axis=1, keepdims=True) + epsilon)
    normed[...] = (value * root * gains[GAIN_F : GAIN_F + 1]).astype(bf16)


def middle_back_kernel(
    middle, normed, grad_out, code, router, gains, own, *refs
):
    others, (grad_middle, grad_round, small) = refs[:-3], refs[-3:]
    width = middle.shape[1]
    total = own[...].astype(f32)
    for other in others:
        total += other[...].astype(f32)
    routed = code[...].astype(f32) > 0.5
    logits = lax.dot_general(normed[...], router[...], NN, preferred_element_type=f32)
    logits = jnp.where(routed, logits, -1e30)
    expo = jnp.where(routed, jnp.exp(logits - jnp.max(logits, axis=1, keepdims=True)), 0.0)
    gates = expo / jnp.sum(expo, axis=1, keepdims=True)
    grad_gates = total[:, width:]
    grad_logits = gates * (grad_gates - jnp.sum(gates * grad_gates, axis=1, keepdims=True))
    high = grad_logits.astype(bf16)
    low = (grad_logits - high.astype(f32)).astype(bf16)
    grad_normed = total[:, :width]
    router_grad = jnp.zeros(small.shape, f32)
    for part in (high, low):
        grad_normed += lax.dot_general(part, router[...], NT, preferred_element_type=f32)
        router_grad += lax.dot_general(normed[...], part, TN, preferred_element_type=f32)
    value = middle[...]
    root = lax.rsqrt(jnp.mean(value * value, axis=1, keepdims=True) + epsilon)
    scaled = value * root
    column = jnp.sum(grad_normed * scaled, axis=0, keepdims=True)
    column = jnp.transpose(jnp.broadcast_to(column, (EXTRA, width)))
    lanes = lax.broadcasted_iota(jnp.int32, small.shape, 1)
    small[...] = jnp.where(lanes == GAIN_F, column, router_grad)
    grad_scaled = grad_normed * gains[GAIN_F : GAIN_F + 1]
    inner = jnp.mean(grad_scaled * scaled, axis=1, keepdims=True)
    result = grad_out[...].astype(f32) + root * (grad_scaled - scaled * inner)
    grad_middle[...] = result
    grad_round[...] = result.astype(bf16)


def attend_back_kernel(
    block,
    sizes,
    at_ref,
    own_ref,
    other_ref,
    mixed,
    out_weights,
    small_ref,
    qs,
    ks,
    vs,
    lse,
    seg_col,
    seg_row,
    cos_ref,
    sin_ref,
    hid,
    normed,
    weights,
    *refs,
):
    heads, kv_heads = sizes
    own, other, parts = refs[0], refs[1], refs[2:-6]
    acc, small, grads, whole, grad_mixed, out_acc = refs[-6:]
    me, core = at_ref[0], at_ref[1]
    length, width = hid.shape
    rows = own.shape[0]
    cols = grads.shape[1]
    whole[pl.ds(pl.multiple_of(core * rows, rows), rows)] = own_ref[...]
    whole[pl.ds(pl.multiple_of((1 - core) * rows, rows), rows)] = other_ref[...]
    grad_mixed[...] = lax.dot_general(
        whole[...], out_weights[...], NN, preferred_element_type=f32
    ).astype(bf16)
    out_acc[...] = lax.dot_general(whole[...], mixed[...], TN, preferred_element_type=f32)
    store_parts(out_acc, parts, me, block, cols + EXTRA)
    cosine, sine = cos_ref[...], -sin_ref[...]
    splits = row_splits(length)
    scale = 1.0 / math.sqrt(HD)
    per_group = heads // kv_heads
    bias = masks(seg_col[...], seg_row[...], splits)
    for kv_head in range(kv_heads):
        kv = slice(kv_head * HD, (kv_head + 1) * HD)
        grad_key = jnp.zeros((length, HD), f32)
        grad_value = jnp.zeros((length, HD), f32)
        for (low, high), mask in zip(splits, bias):
            key_sum = jnp.zeros((high, HD), f32)
            value_sum = jnp.zeros((high, HD), f32)
            for head in range(kv_head * per_group, (kv_head + 1) * per_group):
                at = slice(head * HD, (head + 1) * HD)
                query, grad = qs[low:high, at], grad_mixed[low:high, at]
                scores = lax.dot_general(query, ks[:high, kv], NT, preferred_element_type=f32)
                probs = jnp.exp(scores * scale + mask - lse[low:high, head : head + 1])
                grad_probs = lax.dot_general(
                    grad, vs[:high, kv], NT, preferred_element_type=f32
                )
                inner = jnp.sum(grad_probs * probs, axis=1, keepdims=True)
                grad_scores = (probs * (grad_probs - inner)).astype(bf16)
                grad_query = lax.dot_general(
                    grad_scores, ks[:high, kv], NN, preferred_element_type=f32
                )
                grads[low:high, at] = turn(
                    grad_query * scale, cosine[low:high], sine[low:high]
                ).astype(bf16)
                key_sum += lax.dot_general(grad_scores, query, TN, preferred_element_type=f32)
                value_sum += lax.dot_general(
                    probs.astype(bf16), grad, TN, preferred_element_type=f32
                )
            if high < length:
                pad = jnp.zeros((length - high, HD), f32)
                key_sum = jnp.concatenate([key_sum, pad], axis=0)
                value_sum = jnp.concatenate([value_sum, pad], axis=0)
            grad_key += key_sum
            grad_value += value_sum
        at = (heads + kv_head) * HD
        grads[:, at : at + HD] = turn(grad_key * scale, cosine, sine).astype(bf16)
        at += kv_heads * HD
        grads[:, at : at + HD] = grad_value.astype(bf16)
    acc[...] = lax.dot_general(normed[...], grads[...], TN, preferred_element_type=f32)
    store_parts(acc, parts, me, block, 0)
    value = hid[...].astype(f32)
    root = lax.rsqrt(jnp.mean(value * value, axis=1, keepdims=True) + epsilon)
    column = jnp.zeros((1, width), f32)
    for target, half in ((other, 1 - core), (own, core)):
        at = pl.ds(pl.multiple_of(half * rows, rows), rows)
        part = lax.dot_general(grads[at], weights[...], NT, preferred_element_type=f32)
        target[...] = part.astype(target.dtype)
        half_value = hid[at].astype(f32)
        half_root = lax.rsqrt(jnp.mean(half_value * half_value, axis=1, keepdims=True) + epsilon)
        column += jnp.sum(part * (half_value * half_root), axis=0, keepdims=True)
    lanes = lax.broadcasted_iota(jnp.int32, small.shape, 1)
    column = jnp.transpose(jnp.broadcast_to(column, (EXTRA, width)))
    small[...] = jnp.where(lanes == GAIN_A, column, small_ref[...])
    store_parts(small, parts, me, block, cols)


def slots_kernel(parts, at_ref, order_col, order_row, own, other, code, *refs):
    picks, rows_out, whole = refs[: len(parts)], refs[-2], refs[-1]
    core = at_ref[1]
    rows = own.shape[0]
    width = own.shape[1]
    whole[pl.ds(pl.multiple_of(core * rows, rows), rows), :width] = own[...]
    whole[pl.ds(pl.multiple_of((1 - core) * rows, rows), rows), :width] = other[...]
    whole[:, width:] = code[...]
    none = order_row.shape[0] // 2 * order_row.shape[1]
    first = core * sum(parts)
    for expert in range(order_row.shape[0]):
        row = order_row[expert : expert + 1, :]
        ahead = (order_col[:, expert : expert + 1] < row).astype(f32)
        position = jnp.sum(ahead, axis=0, keepdims=True).astype(jnp.int32)
        position = jnp.where(row < none, position, -1)
        low = first
        for pick, count in zip(picks, parts):
            slot = lax.broadcasted_iota(jnp.int32, (count, row.shape[1]), 0) + low
            pick[expert * count : (expert + 1) * count, :] = (slot == position).astype(bf16)
            low = low + count
    low = 0
    for pick, count in zip(picks, parts):
        taken = lax.dot_general(pick[...], whole[...], NN, preferred_element_type=f32)
        rows_out[:, low : low + count] = taken.astype(bf16).reshape(
            order_row.shape[0], count, whole.shape[1]
        )
        low += count


def take_kernel(at_ref, own, other, *refs):
    count = (len(refs) - 1) // 2
    picks, outs, whole = refs[:count], refs[count:-1], refs[-1]
    core = at_ref[1]
    rows = own.shape[0]
    whole[pl.ds(pl.multiple_of(core * rows, rows), rows)] = own[...]
    whole[pl.ds(pl.multiple_of((1 - core) * rows, rows), rows)] = other[...]
    for pick, out in zip(picks, outs):
        out[...] = lax.dot_general(
            pick[...], whole[...], NN, preferred_element_type=f32
        ).astype(bf16)


def give_kernel(count, at_ref, *refs):
    picks, values, (own, other) = refs[:count], refs[count:-2], refs[-2:]
    rows = own.shape[0]
    if len(values) < count:
        whole, values, low = values[0][...], [], 0
        for pick in picks:
            each = pick.shape[0] // whole.shape[0]
            values.append(whole[:, low : low + each].reshape(pick.shape[0], whole.shape[2]))
            low += each
    for target, half in ((other, 1 - at_ref[1]), (own, at_ref[1])):
        columns = pl.ds(pl.multiple_of(half * rows, rows), rows)
        total = None
        for pick, value in zip(picks, values):
            part = lax.dot_general(
                pick[:, columns], value[...], TN, preferred_element_type=f32
            )
            total = part if total is None else total + part
        target[...] = total.astype(target.dtype)


def gelu_parts(value):
    square = value * value
    inner = value * (0.7978845608028654 + 0.035677408136300125 * square)
    tanh = jnp.tanh(inner)
    half = 0.5 + 0.5 * tanh
    slope = half + 0.5 * value * (1.0 - tanh * tanh) * (
        0.7978845608028654 + 3.0 * 0.035677408136300125 * square
    )
    return value * half, slope


def moe_kernel(plan, at_ref, router_ref, x_in, g_in, *refs):
    copies, hidden, blocks, outer, first, groups = plan
    weight_count = len(set(c[0] for c in copies))
    if first:
        refs = refs[1:]
    sources, outs, refs = refs[:weight_count], refs[weight_count:][:5], refs[weight_count + 5 :]
    weights, xs, gs = refs[:3]
    buffers = refs[3:8]
    weight_sems, in_sems, out_sems = refs[8:]
    branch, gradn, act_all, gp_all, geo_all = buffers
    _, rows, width = xs.shape
    whole = 2 * hidden
    expert = at_ref[0] % CUBE

    weight_copies = []
    block_rows = weights.shape[0] // outer
    for number, (source, entry, low, length, offset, from_col, to_col, cols) in enumerate(copies):
        row = pl.multiple_of(((at_ref[0] // CUBE) ^ offset) * block_rows + low, 16)
        weight_copies.append(
            pltpu.make_async_copy(
                sources[source].at[entry, :, pl.ds(from_col, cols)],
                weights.at[pl.ds(row, length), pl.ds(to_col, cols)],
                weight_sems.at[number],
            )
        )
    weight_order = sorted(range(len(copies)), key=lambda k: copies[k][5] // hidden)
    in_copies = []
    for block in range(blocks):
        span = pl.ds(block * rows, rows)
        for kind, (source, target) in enumerate(((x_in, xs), (g_in, gs))):
            held = (span,)
            if kind == 1:
                held = pl.ds(block * groups, groups), pl.ds(first, rows // groups)
            in_copies.append(
                pltpu.make_async_copy(
                    source.at[held], target.at[block], in_sems.at[2 * block + kind]
                )
            )
    in_copies[0].start()
    for k in weight_order:
        weight_copies[k].start()
    for copy in in_copies[1:]:
        copy.start()
    out_copies = []
    for block in range(blocks):
        in_copies[2 * block].wait()
        x = xs[block]
        logits = lax.dot_general(x, router_ref[...], NN, preferred_element_type=f32)
        if block == 0:
            for k in weight_order:
                if copies[k][5] < 2 * hidden:
                    weight_copies[k].wait()
        pre = lax.dot_general(x, weights[:, : 2 * whole], NN, preferred_element_type=f32)
        in_copies[2 * block + 1].wait()
        both = gs[block].reshape(rows, gs.shape[3])
        routed = both[:, width:].astype(f32) > 0.5
        lanes = lax.broadcasted_iota(jnp.int32, routed.shape, 1)
        logits = jnp.where(routed, logits, -1e30)
        expo = jnp.where(routed, jnp.exp(logits - jnp.max(logits, axis=1, keepdims=True)), 0.0)
        total = jnp.sum(expo, axis=1, keepdims=True)
        gate = jnp.sum(jnp.where(lanes == expert, expo, 0.0), axis=1, keepdims=True)
        gate = gate / jnp.where(total > 0.0, total, 1.0)

        gate_pre, up_pre = pre[:, :whole], pre[:, whole:]
        gelu, slope = gelu_parts(gate_pre)
        act = (gelu * up_pre).astype(bf16)
        act_all[block] = act
        if block == 0:
            for k in weight_order:
                if copies[k][5] == 2 * hidden:
                    weight_copies[k].wait()
        down = weights[:, 2 * whole :]
        expert_out = lax.dot_general(act, down, NT, preferred_element_type=f32)
        branch[block] = (gate * expert_out).astype(bf16).reshape(branch.shape[1:])
        g = both[:, :width].astype(f32)
        grad_gate = jnp.sum(g * expert_out, axis=1, keepdims=True)
        gradn[block, :, width:] = jnp.where(lanes == expert, grad_gate, 0.0).astype(bf16)
        geo = (gate * g).astype(bf16)
        geo_all[block] = geo
        grad_act = lax.dot_general(geo, down, NN, preferred_element_type=f32)
        grad_gate_pre = (grad_act * up_pre * slope).astype(bf16)
        grad_up_pre = (grad_act * gelu).astype(bf16)
        for side in range(2):
            cols = slice(side * hidden, (side + 1) * hidden)
            for kind, part in enumerate((grad_gate_pre, grad_up_pre)):
                at = (2 * side + kind) * hidden
                gp_all[block, :, at : at + hidden] = part[:, cols]
        grad_in = lax.dot_general(
            grad_gate_pre, weights[:, :whole], NT, preferred_element_type=f32
        ) + lax.dot_general(
            grad_up_pre, weights[:, whole : 2 * whole], NT, preferred_element_type=f32
        )
        gradn[block, :, :width] = grad_in.astype(bf16)
        for number, (source, target) in enumerate(zip(buffers, outs)):
            if number == 0:
                held = pl.ds(block * groups, groups), pl.ds(first, rows // groups)
            else:
                held = (pl.ds(block * rows, rows),)
            copy = pltpu.make_async_copy(
                source.at[block], target.at[held], out_sems.at[5 * block + number]
            )
            copy.start()
            out_copies.append(copy)
    for copy in out_copies:
        copy.wait()


def moe(at, x, g, router, pieces, hidden, outer, sequences, capacity, branch=None):
    copies = []
    for source, (array, first, low, side) in enumerate(pieces):
        for entry in range(array.shape[0]):
            for kind in range(3):
                copies.append(
                    (source, entry, low, array.shape[1], first + entry, kind * hidden)
                    + ((2 * kind + side) * hidden, hidden)
                )
    total, width = x.shape
    blocks = 2
    rows = total // blocks
    widths = (width, width + EXTRA, 2 * hidden, 4 * hidden, width)
    each = total // sequences
    first = 0 if branch is None else capacity - each
    args = [x, g] + ([] if branch is None else [branch]) + [p[0] for p in pieces]
    groups = sequences // blocks
    buffers = [(blocks, rows, w) for w in widths]
    buffers[0] = (blocks, groups, each, width)
    return pl.pallas_call(
        functools.partial(moe_kernel, (copies, hidden, blocks, outer, first, groups)),
        out_shape=[jax.ShapeDtypeStruct((sequences, capacity, width), bf16)]
        + [jax.ShapeDtypeStruct((total, w), bf16) for w in widths[1:]],
        in_specs=[pl.BlockSpec(memory_space=pltpu.SMEM), pl.BlockSpec(memory_space=pltpu.VMEM)]
        + [pl.BlockSpec(memory_space=pl.ANY)] * len(args),
        out_specs=[pl.BlockSpec(memory_space=pl.ANY)] * 5,
        scratch_shapes=[
            pltpu.VMEM((width, 6 * hidden), bf16),
            pltpu.VMEM((blocks, rows, width), bf16),
            pltpu.VMEM((blocks, groups, each, width + EXTRA), bf16),
        ]
        + [pltpu.VMEM(dims, bf16) for dims in buffers]
        + [
            pltpu.SemaphoreType.DMA((len(copies),)),
            pltpu.SemaphoreType.DMA((2 * blocks,)),
            pltpu.SemaphoreType.DMA((5 * blocks,)),
        ],
        input_output_aliases={} if branch is None else {4: 0},
        compiler_params=pltpu.CompilerParams(vmem_limit_bytes=60 * 1024 * 1024),
        cost_estimate=BRIEF,
        name="experts",
    )(at, router, *args)


def weight_grads_kernel(calls, at_ref, *refs):
    pairs = []
    for _ in range(2):
        pairs.append((refs[:calls], refs[calls : 2 * calls]))
        refs = refs[2 * calls :]
    own, other, *buffers, sems = refs
    cols = buffers[0].shape[1]
    columns = pl.ds(pl.multiple_of(at_ref[2] * cols, cols), cols)
    copies = []
    for number, (lefts, rights) in enumerate(pairs):
        row = 0
        for left, right in zip(lefts, rights):
            rows = pl.ds(row, left.shape[0])
            for source, target in (
                (left.at[:, columns], buffers[2 * number].at[rows]),
                (right, buffers[2 * number + 1].at[rows]),
            ):
                copies.append(pltpu.make_async_copy(source, target, sems.at[len(copies)]))
                copies[-1].start()
            row += left.shape[0]
    at = 0
    for number in range(2):
        for copy in copies[2 * calls * number : 2 * calls * (number + 1)]:
            copy.wait()
        total = lax.dot_general(
            buffers[2 * number][...],
            buffers[2 * number + 1][...],
            TN,
            preferred_element_type=f32,
        ).astype(bf16)
        width = total.shape[1] // 2
        own[:, at : at + width] = total[:, :width]
        other[:, at : at + width] = total[:, width:]
        at += width


def weight_grads(at, half, pre, down):
    args, scratch, width = [], [], 0
    for pairs in (pre, down):
        args += [p[0] for p in pairs] + [p[1] for p in pairs]
        rows = sum(p[0].shape[0] for p in pairs)
        left, right = pairs[0][0].shape[1] // 2, pairs[0][1].shape[1]
        scratch += [(rows, left), (rows, right)]
        width += right // 2
    return pl.pallas_call(
        functools.partial(weight_grads_kernel, len(pre)),
        out_shape=[jax.ShapeDtypeStruct((left, width), bf16)] * 2,
        in_specs=[pl.BlockSpec(memory_space=pltpu.SMEM)]
        + [pl.BlockSpec(memory_space=pl.ANY)] * len(args),
        out_specs=[pl.BlockSpec(memory_space=pltpu.VMEM)] * 2,
        scratch_shapes=[pltpu.VMEM(dims, bf16) for dims in scratch]
        + [pltpu.SemaphoreType.DMA((len(args),))],
        compiler_params=pltpu.CompilerParams(vmem_limit_bytes=60 * 1024 * 1024),
        cost_estimate=FREE,
        name="weight_grads",
    )(jnp.concatenate([at, half.reshape(1)]), *args)


def per_device(
    count,
    hidden_in,
    segment_ids,
    routes,
    slot_order,
    gain_attn,
    w_query,
    w_key,
    w_value,
    w_out,
    gain_ffn,
    w_router,
    w_gate,
    w_up,
    w_down,
    grad_out,
):
    tok_rows, width = hidden_in.shape
    seq_len = segment_ids.shape[0]
    top_count = routes.shape[1]
    experts, block, hidden = w_gate.shape
    capacity = 9 * seq_len * top_count // (8 * experts)
    me = lax.axis_index("dp").astype(jnp.int32)
    core = lax.axis_index("tensor").astype(jnp.int32)
    at = jnp.stack([me, core])
    groups = [list(range(first, first + CUBE)) for first in range(0, count, CUBE)]
    heads_cols, kv_cols = w_query.shape[1], w_key.shape[1]
    qkv_cols = heads_cols + 2 * kv_cols
    heads, kv_heads = heads_cols // HD, kv_cols // HD

    def shape(rows, cols, dtype=bf16):
        return jax.ShapeDtypeStruct((rows, cols), dtype)

    def near(own):
        return {0: own} | {bit: swap(own, bit, count) for bit in NEAR}

    def far(got):
        spans = halves(got[0].shape[0])
        return got | {
            3: swap(cut(got[2], spans[0], 0), 1, count),
            9: swap(cut(got[1], spans[1], 0), 2, count),
            6: swap(got[4], 2, count),
            5: swap(got[4], 1, count),
        }

    def last(got):
        spans = halves(got[0].shape[0])
        return got | {
            7: swap(cut(got[6], spans[0], 0), 1, count),
            8: swap(cut(got[5], spans[1], 0), 2, count),
        }

    small = jnp.concatenate([w_router, gain_attn[:, None], gain_ffn[:, None]], axis=1)
    small = jnp.pad(small, ((0, 0), (0, EXTRA - small.shape[1])))
    pair = outer_pair(
        jnp.concatenate([w_query, w_key, w_value, small, w_out.T], axis=1), count
    )
    hidden_other = swap_core(hidden_in)

    expert_shard = jnp.concatenate([w_gate, w_up, jnp.swapaxes(w_down, 1, 2)], axis=2)
    expert_rows = lax.all_to_all(
        expert_shard.reshape(experts * block, 3 * hidden),
        "dp",
        0,
        0,
        tiled=True,
        axis_index_groups=groups,
    )

    order = jnp.min(
        jnp.where(
            routes[:, :, None] == jnp.arange(experts, dtype=jnp.int32),
            slot_order[0].reshape(seq_len, top_count)[:, :, None],
            seq_len * top_count,
        ),
        axis=1,
    )
    code = (order < seq_len * top_count).astype(bf16)
    code = jnp.pad(code, ((0, 0), (0, EXTRA - experts)))
    code_own = lax.dynamic_slice_in_dim(code, core * tok_rows, tok_rows, 0)
    first_part = capacity // 4 // 16 * 16
    slot_parts = (first_part, capacity // 2 - first_part)
    grad_other = swap_core(grad_out)
    slots = vmem_call(
        functools.partial(slots_kernel, slot_parts),
        [shape(experts * part, seq_len) for part in slot_parts]
        + [jax.ShapeDtypeStruct((experts, sum(slot_parts), width + EXTRA), bf16)],
        [pltpu.VMEM((seq_len, width + EXTRA), bf16)],
        [(at, 1), (order, 0), (order.T, 0), (grad_out, 0), (grad_other, 0), (code, 0)],
        "slots",
    )
    picks, grad_rows = slots[:2], slots[2]

    def exchange(rows):
        return lax.all_to_all(rows, "dp", 0, 0, tiled=True, axis_index_groups=groups)

    cosine, sine_table = rope_tables(seq_len, HD)
    cosine = jnp.concatenate([cosine, cosine], axis=1)
    sine_table = jnp.concatenate([-sine_table, sine_table], axis=1)
    seg_col, seg_row = segment_ids[:, None], segment_ids[None, :]

    pair, expert_rows = gate([pair, expert_rows], cosine, sine_table, hidden_other, grad_other)
    if count == 2 * CUBE:
        edges = [expert_rows.shape[0] * k // 48 // 16 * 16 for k in (0, 10, 26, 26, 34, 48)]
    else:
        edges = [0] * 5 + [expert_rows.shape[0]]
    pieces = [(expert_rows[None], 0, 0, 0), (swap_core(expert_rows)[None], 0, 0, 1)]

    def outer_chunk(k, *events):
        low, high = edges[k], edges[k + 1]
        if high == low:
            return [], []
        (chunk,) = gate([cut(expert_rows, (low, high), 0)], *events)
        arrays, first, swapped = outer_gather(chunk, count)[1:], 1, []
        for array in arrays:
            swapped.append(swap_core(array))
            pieces.append((array, first, low, 0))
            pieces.append((swapped[-1], first, low, 1))
            first += array.shape[0]
        return arrays, swapped

    with jax.named_scope("weights_near"):
        got = near(pair)
    arrays, swapped = outer_chunk(0, pair)
    got = gate_dict(got, NEAR, grad_rows, arrays, pieces[1][0])
    with jax.named_scope("weights_far"):
        got = far(got)
    arrays, swapped_next = outer_chunk(1, got[1])
    got = gate_dict(got, FAR, arrays, swapped)
    with jax.named_scope("weights_last"):
        got = last(got)
    arrays, swapped = outer_chunk(2, got[3])
    got = gate_dict(got, LAST, arrays, swapped_next)
    sources, copies = piece_copies(got, block, me, count)
    grad_rows, seg_col = gate([grad_rows, seg_col], got[7])
    with jax.named_scope("grads_rows"):
        grad_rows = exchange(grad_rows)
    attended = vmem_call(
        functools.partial(attend_kernel, copies, (heads, kv_heads, len(sources))),
        [
            shape(seq_len, width),
            shape(seq_len, width),
            shape(seq_len, heads_cols),
            shape(seq_len, kv_cols),
            shape(seq_len, kv_cols),
            shape(seq_len, heads_cols),
            shape(seq_len, HD, f32),
            shape(width, qkv_cols),
            shape(width, EXTRA),
            shape(width, heads_cols),
            shape(16, width, f32),
            shape(tok_rows, width, f32),
            shape(tok_rows, width),
        ],
        [pltpu.SemaphoreType.DMA((3 * len(copies),))],
        [(at, 1), (hidden_in, 0), (hidden_other, 0), (seg_col, 0), (seg_row, 0)]
        + [(cosine, 0), (sine_table, 0)]
        + [(piece, 2) for piece in sources],
        "attend",
        flops=2 * seq_len * (width * (qkv_cols + heads_cols) + heads_cols * seq_len),
    )
    hid, normed, qs, ks, vs, mixed, lse, full_qkv, router, out_wt, gains = attended[:-2]
    attn_own, attn_other = attended[-2:]
    arrays, swapped_next = outer_chunk(3, got[7])
    middle, normed2 = vmem_call(
        middle_kernel,
        [shape(tok_rows, width, f32), shape(tok_rows, width)],
        [],
        [(hidden_in, 0), (attn_own, 0), (swap_core(attn_other), 0), (gains, 0)],
        "middle",
    )

    rows = vmem_call(
        take_kernel,
        [shape(experts * part, width) for part in slot_parts],
        [pltpu.VMEM((seq_len, width), bf16)],
        [(at, 1), (normed2, 0), (swap_core(normed2), 0)] + [(pick, 0) for pick in picks],
        "take",
    )
    rows = list(rows)
    rows[0], grad_rows = gate([rows[0], grad_rows], arrays, swapped)
    with jax.named_scope("tokens_rows"):
        x_first = exchange(rows[0])
    arrays, _ = outer_chunk(4, rows[0])
    x_first, rows_second = gate([x_first, rows[1]], arrays, swapped_next)
    with jax.named_scope("tokens_rows"):
        x_second = exchange(rows_second)

    def experts_on(x, g, router, branch=None):
        held = (CUBE, sum(slot_parts))
        return moe(at, x, g, router, pieces, hidden, count // CUBE, *held, branch)

    branch, gradn_first, *first = experts_on(x_first, grad_rows, router)
    with jax.named_scope("gradn_rows"):
        gradn_first = exchange(gradn_first)
    (second_router,) = gate([router], first[0])
    branch, gradn_second, *second = experts_on(x_second, grad_rows, second_router, branch)

    xs = (x_first, x_second)
    pre_pairs = [(x, call[1]) for x, call in zip(xs, (first, second))]
    down_pairs = [(call[2], call[0]) for call in (first, second)]
    bits = outer_bits(count)
    top = (me // bits[-1]) % 2 if bits else jnp.zeros((), jnp.int32)

    def half_grads(half, *events):
        half = gate([half.reshape(1)], *events)[0]
        return weight_grads(at, half, pre_pairs, down_pairs)

    with jax.named_scope("gradn_rows"):
        gradn_second = exchange(gradn_second)
    sent, sent_other = half_grads(1 - top, second[0])
    keep, keep_other = half_grads(top, sent_other)
    with jax.named_scope("expert_scatter"):
        sent = add_round(sent, swap_core(sent_other))
        sent_got = swap(sent, bits[-1], count) if bits else sent

    def give(picks, values, name):
        own, other = vmem_call(
            functools.partial(give_kernel, len(picks)),
            [shape(tok_rows, values[0].shape[-1], f32), shape(tok_rows, values[0].shape[-1])],
            [],
            [(at, 1)] + [(pick, 0) for pick in picks] + [(value, 0) for value in values],
            name,
        )
        return own, swap_core(other)

    gradn_second, gradn_first = gate([gradn_second, gradn_first], sent, keep)
    gradn = list(give(picks, (gradn_first, gradn_second), "give_gradn"))

    grad_middle, grad_mid_r, small_f = vmem_call(
        middle_back_kernel,
        [shape(tok_rows, width, f32), shape(tok_rows, width), shape(width, EXTRA, f32)],
        [],
        [(middle, 0), (normed2, 0), (grad_out, 0), (code_own, 0), (router, 0), (gains, 0)]
        + [(array, 0) for array in gradn],
        "middle_back",
    )

    grad_mid_other = swap_core(grad_mid_r)
    (branch,) = gate([branch], gradn_second)
    with jax.named_scope("branch_rows"):
        branch = exchange(branch)
    normed_own, normed_other, *parts = vmem_call(
        functools.partial(attend_back_kernel, block, (heads, kv_heads)),
        [shape(tok_rows, width, f32), shape(tok_rows, width)]
        + part_shapes(count, block, qkv_cols + EXTRA + heads_cols),
        [
            pltpu.VMEM((width, qkv_cols), f32),
            pltpu.VMEM((width, EXTRA), f32),
            pltpu.VMEM((seq_len, qkv_cols), bf16),
            pltpu.VMEM((seq_len, width), bf16),
            pltpu.VMEM((seq_len, heads_cols), bf16),
            pltpu.VMEM((width, heads_cols), f32),
        ],
        [(at, 1), (grad_mid_r, 0), (grad_mid_other, 0), (mixed, 0), (out_wt, 0)]
        + [(small_f, 0), (qs, 0), (ks, 0), (vs, 0), (lse, 0), (seg_col, 0)]
        + [(seg_row, 0), (cosine, 0), (sine_table, 0), (hid, 0), (normed, 0), (full_qkv, 0)],
        "attend_back",
        flops=4 * seq_len * (width * (qkv_cols + heads_cols) + 2 * heads_cols * seq_len),
    )
    parts = spread_parts(parts, me, count)

    keep_swapped = swap_core(keep_other)
    parts = gate_dict(parts, (3, 9) + LAST, keep_swapped)
    with jax.named_scope("attn_last"):
        got = sum_last(parts, count)
    normed_swapped = swap_core(normed_other)
    gated = gate([got[7], got[8], parts[3], parts[9]], normed_swapped)
    got, parts[3], parts[9] = dict(zip(LAST, gated)), gated[2], gated[3]
    with jax.named_scope("attn_far"):
        terms = far_terms(parts, got)
        attn_far = sum_far(parts, terms, count)
    with jax.named_scope("expert_scatter"):
        sent_got, keep = gate([sent_got, keep], terms)
        if bits:
            total = keep.astype(f32) + keep_swapped.astype(f32) + sent_got.astype(f32)
        else:
            total = jnp.concatenate([add_round(keep, keep_swapped), sent_got]).astype(f32)
        for bit in reversed(bits[:-1]):
            half = total.shape[0] // 2
            high = (me // bit) % 2
            mine = lax.dynamic_slice_in_dim(total, high * half, half, 0)
            other = lax.dynamic_slice_in_dim(total, (1 - high) * half, half, 0)
            total = mine + swap(other.astype(bf16), bit, count).astype(f32)
        total = total.astype(bf16)
    grad_normed = normed_own + normed_swapped.astype(f32)
    gated = gate([attn_far[k] for k in FAR] + [branch, total])
    attn_far, branch, total = dict(zip(FAR, gated)), gated[4], gated[5]
    with jax.named_scope("attn_near"):
        attn_near = sum_near(near_terms(parts, attn_far), count)
    branch_own, branch_other = give(picks, (branch,), "give_branch")
    with jax.named_scope("expert_scatter"):
        total = exchange(total)
    attn_near = gate_dict(attn_near, NEAR, branch_own)
    with jax.named_scope("attn_outer"):
        attn_grads = outer_sum(sum_own(parts, attn_near), count)
    layer_out = middle + branch_own + branch_other.astype(f32)

    expert_grads = total.reshape(experts, block, 3 * hidden).astype(f32)
    grad_gate_w = expert_grads[:, :, :hidden]
    grad_up_w = expert_grads[:, :, hidden : 2 * hidden]
    grad_down_w = jnp.swapaxes(expert_grads[:, :, 2 * hidden :], 1, 2)
    scaled_in, root_in = rms_parts(hidden_in.astype(f32))
    grad_in = grad_middle + norm_backward(grad_normed, scaled_in, root_in, gains[GAIN_A])
    smalls = attn_grads[:, qkv_cols : qkv_cols + EXTRA]
    smalls = smalls + swap_core(smalls)
    return (
        layer_out,
        grad_in,
        smalls[:, GAIN_A],
        attn_grads[:, :heads_cols],
        attn_grads[:, heads_cols : heads_cols + kv_cols],
        attn_grads[:, heads_cols + kv_cols : qkv_cols],
        attn_grads[:, qkv_cols + EXTRA :].T,
        smalls[:, GAIN_F],
        smalls[:, :experts],
        grad_gate_w,
        grad_up_w,
        grad_down_w,
    )


def solution(mesh):
    return jax.shard_map(
        functools.partial(per_device, mesh.shape["dp"]),
        mesh=mesh,
        in_specs=(
            P(("dp", "tensor"), None),
            P("dp"),
            P("dp", None),
            P("dp", None),
            P("dp"),
            P("dp", "tensor"),
            P("dp", "tensor"),
            P("dp", "tensor"),
            P("tensor", "dp"),
            P("dp"),
            P("dp", None),
            P(None, "dp", "tensor"),
            P(None, "dp", "tensor"),
            P(None, "tensor", "dp"),
            P(("dp", "tensor"), None),
        ),
        out_specs=(
            P(("dp", "tensor"), None),
            P(("dp", "tensor"), None),
            P("dp"),
            P("dp", "tensor"),
            P("dp", "tensor"),
            P("dp", "tensor"),
            P("tensor", "dp"),
            P("dp"),
            P("dp", None),
            P(None, "dp", "tensor"),
            P(None, "dp", "tensor"),
            P(None, "tensor", "dp"),
        ),
        check_vma=False,
    )
```

```python
import functools
import math

import jax
import jax.numpy as jnp
from jax import lax
from jax.experimental import pallas as pl
from jax.experimental.pallas import tpu as pltpu
from jax.sharding import PartitionSpec as P

HD = 128
EXTRA = 128
GAIN_A, GAIN_F = 8, 9
CUBE = 8
BRIEF = pl.CostEstimate(flops=0, bytes_accessed=3_000_000, transcendentals=0)
LIGHT = ("attend", "middle", "take", "give_gradn", "middle_back", "attend_back")
FREE = pl.CostEstimate(flops=0, bytes_accessed=0, transcendentals=0)
epsilon = 1e-06
highest = lax.Precision.HIGHEST
f32 = jnp.float32
bf16 = jnp.bfloat16
NN = (((1,), (0,)), ((), ()))
NT = (((1,), (1,)), ((), ()))
TN = (((0,), (0,)), ((), ()))


def rms_parts(values):
    inverse_root = lax.rsqrt(jnp.mean(values * values, axis=-1, keepdims=True) + epsilon)
    return (values * inverse_root, inverse_root)


def norm_backward(grad_normed, scaled, inverse_root, gain):
    grad_scaled = grad_normed * gain
    inner = jnp.mean(grad_scaled * scaled, axis=-1, keepdims=True)
    return inverse_root * (grad_scaled - scaled * inner)


def rope_tables(length, size):
    inverse = 10000.0 ** (-jnp.arange(size // 2, dtype=f32) / (size // 2))
    angle = jnp.arange(length, dtype=f32)[:, None] * inverse[None, :]
    return (jnp.cos(angle), jnp.sin(angle))


def swap(values, bit, count):
    return lax.ppermute(values, "dp", [(i, i ^ bit) for i in range(count)])


def swap_core(values):
    return lax.ppermute(values, "tensor", [(0, 1), (1, 0)])


def gate(values, *events):
    values = list(values)
    flat = jax.tree.leaves(events)
    return pl.pallas_call(
        lambda *refs: None,
        out_shape=[jax.ShapeDtypeStruct(v.shape, v.dtype) for v in values],
        in_specs=[pl.BlockSpec(memory_space=pl.ANY)] * (len(values) + len(flat)),
        out_specs=[pl.BlockSpec(memory_space=pl.ANY)] * len(values),
        input_output_aliases={i: i for i in range(len(values))},
        compiler_params=pltpu.CompilerParams(vmem_limit_bytes=60 * 1024 * 1024),
        cost_estimate=BRIEF,
        name="gate",
    )(*values, *flat)


def gate_dict(got, keys, *events):
    return got | dict(zip(keys, gate([got[k] for k in keys], *events)))


def halves(rows):
    part = rows // 2
    return ((0, part), (part, rows))


def cut(values, span, axis):
    return lax.slice_in_dim(values, span[0], span[1], axis=axis)


NEAR, FAR, LAST = (1, 2, 4), (3, 9, 6, 5), (7, 8)


def add_round(left, right):
    return (left.astype(f32) + right.astype(f32)).astype(bf16)


def sum_last(parts, count):
    return {7: swap(parts[7], 1, count), 8: swap(parts[8], 2, count)}


def patch_kernel(first, second, low, high, first_out, second_out):
    first_out[...] = (first[...].astype(f32) + low[...].astype(f32)).astype(bf16)
    second_out[...] = (second[...].astype(f32) + high[...].astype(f32)).astype(bf16)


def patch(first, second, low, high):
    shape = first.shape
    half = low.shape
    if half[1] % 16:
        return (
            jnp.concatenate([add_round(first[: half[0]], low), first[half[0] :]], axis=0),
            jnp.concatenate([second[: half[0]], add_round(second[half[0] :], high)], axis=0),
        )
    top = pl.BlockSpec(half, lambda i: (0, 0, 0))
    bottom = pl.BlockSpec(half, lambda i: (1, 0, 0))
    return pl.pallas_call(
        patch_kernel,
        grid=(1,),
        out_shape=[jax.ShapeDtypeStruct(shape, bf16)] * 2,
        in_specs=[top, bottom, top, top],
        out_specs=[top, bottom],
        input_output_aliases={0: 0, 1: 1},
        compiler_params=pltpu.CompilerParams(vmem_limit_bytes=60 * 1024 * 1024),
        cost_estimate=FREE,
        name="patch",
    )(first, second, low, high)


def far_terms(parts, got):
    return patch(parts[6], parts[5], got[7], got[8])


def sum_far(parts, terms, count):
    first, second = terms
    return {
        6: swap(first, 2, count),
        5: swap(second, 1, count),
        3: swap(parts[3], 1, count),
        9: swap(parts[9], 2, count),
    }


def terms_kernel(one, two, four, six, five, three, nine, one_out, two_out, four_out):
    four_out[...] = (
        four[...].astype(f32) + six[...].astype(f32) + five[...].astype(f32)
    ).astype(bf16)
    first = three.shape[0]
    two_out[:first] = (two[:first].astype(f32) + three[...].astype(f32)).astype(bf16)
    two_out[first:] = two[first:]
    one_out[:first] = one[:first]
    one_out[first:] = (one[first:].astype(f32) + nine[...].astype(f32)).astype(bf16)


def near_terms(parts, got):
    args = [parts[bit] for bit in NEAR] + [got[k] for k in (6, 5, 3, 9)]
    shape = parts[1].shape
    grid = 2 if shape[1] % 32 == 0 else 1

    def spec(dims):
        return pl.BlockSpec((dims[0], dims[1] // grid, dims[2]), lambda i: (0, i, 0))

    outs = pl.pallas_call(
        terms_kernel,
        grid=(grid,),
        out_shape=[jax.ShapeDtypeStruct(shape, bf16)] * 3,
        in_specs=[spec(arg.shape) for arg in args],
        out_specs=[spec(shape)] * 3,
        compiler_params=pltpu.CompilerParams(vmem_limit_bytes=60 * 1024 * 1024),
        cost_estimate=FREE,
        name="terms",
    )(*args)
    return dict(zip(NEAR, outs))


def sum_near(terms, count):
    return {bit: swap(terms[bit], bit, count) for bit in NEAR}


def sum_own(parts, got):
    return parts[0].astype(f32) + (
        got[1].astype(f32) + (got[2].astype(f32) + got[4].astype(f32))
    )


def outer_bits(count):
    bits, bit = [], CUBE
    while bit < count:
        bits.append(bit)
        bit *= 2
    return bits


def outer_gather(own, count):
    pieces = [own[None]]
    for bit in outer_bits(count):
        pieces.append(swap(jnp.concatenate(pieces, axis=0), bit, count))
    return pieces


def outer_pair(shard, count):
    return jnp.concatenate(outer_gather(shard, count), axis=0)


def piece_copies(got, block, me, count):
    outer = got[0].shape[0]
    if block % 16:
        wholes = got | {3: jnp.concatenate([got[3], got[9]]), 7: jnp.concatenate([got[7], got[8]])}
        stacked = jnp.stack([wholes[b] for b in range(CUBE)], axis=1)
        whole = stacked.reshape(count, block, -1)[jnp.arange(count) ^ me]
        return [whole.reshape(1, count * block, -1)], [(0, 0, count * block, None, block)]
    sources, copies = [], []
    for b in range(CUBE + 2):
        first = outer // 2 if b >= 8 else 0
        offset = {8: 7, 9: 3}.get(b, b)
        for j in range(got[b].shape[0]):
            copies.append((b, j, block, 8 * (first + j) + offset, block))
        sources.append(got[b])
    return sources, copies


def lay_rows(copies, sources, targets, sems, me):
    started = []
    for number, (source, entry, rows, offset, block) in enumerate(copies):
        row = 0 if offset is None else pl.multiple_of((me ^ offset) * block, 16)
        column = 0
        for k, target in enumerate(targets):
            cols = target.shape[1]
            copy = pltpu.make_async_copy(
                sources[source].at[entry, :, pl.ds(column, cols)],
                target.at[pl.ds(row, rows)],
                sems.at[len(targets) * number + k],
            )
            copy.start()
            started.append(copy)
            column += cols
    for copy in started:
        copy.wait()


def part_order(count):
    outer = count // CUBE
    first, second = halves(outer)
    offsets = {3: first, 7: first}
    order = [(b, offsets.get(b, (0, outer))) for b in range(CUBE)]
    return order + [(7, second), (3, second)]


def part_shapes(count, block, width):
    if block % 16:
        return [jax.ShapeDtypeStruct((count * block, width), bf16)]
    return [
        jax.ShapeDtypeStruct((span[1] - span[0], block, width), bf16)
        for _, span in part_order(count)
    ]


def store_parts(whole, parts, me, block, at):
    cols = pl.ds(at, whole.shape[1])
    if len(parts) == 1:
        parts[0][:, cols] = whole[...].astype(bf16)
        return
    for part, (offset, span) in zip(parts, part_order(whole.shape[0] // block)):
        for j in range(part.shape[0]):
            row = pl.multiple_of((me ^ (8 * (span[0] + j) + offset)) * block, 16)
            part[j, :, cols] = whole[pl.ds(row, block)].astype(bf16)


def spread_parts(parts, me, count):
    if len(parts) > 1:
        return dict(enumerate(parts))
    blocks = parts[0].reshape(count, parts[0].shape[0] // count, -1)
    return {
        k: blocks[(offset + CUBE * jnp.arange(*span)) ^ me]
        for k, (offset, span) in enumerate(part_order(count))
    }


def outer_sum(total, count):
    for bit in reversed(outer_bits(count)):
        half = total.shape[0] // 2
        total = total[:half] + swap(total[half:].astype(bf16), bit, count).astype(f32)
    return total[0]


def vmem_call(kernel, out_shapes, scratch, args, name, smem=(), flops=0):
    spaces = {0: pltpu.VMEM, 1: pltpu.SMEM, 2: pl.ANY}
    moved = sum(math.prod(o.shape) * o.dtype.itemsize for o in out_shapes)
    moved += sum(math.prod(a.shape) * a.dtype.itemsize for a, _ in args)
    return pl.pallas_call(
        kernel,
        out_shape=out_shapes,
        in_specs=[pl.BlockSpec(memory_space=spaces[space]) for _, space in args],
        out_specs=[pl.BlockSpec(memory_space=pltpu.VMEM)] * len(out_shapes),
        scratch_shapes=scratch,
        compiler_params=pltpu.CompilerParams(vmem_limit_bytes=60 * 1024 * 1024),
        cost_estimate=FREE if name in LIGHT else BRIEF,
        name=name,
    )(*[a for a, _ in args])


def turn(values, cosine, sine):
    return values * cosine + pltpu.roll(values, values.shape[1] // 2, 1) * sine


def masks(seg_col, seg_row, splits):
    out = []
    for low, high in splits:
        shape = (high - low, high)
        query_at = lax.broadcasted_iota(jnp.int32, shape, 0) + low
        key_at = lax.broadcasted_iota(jnp.int32, shape, 1)
        allowed = (seg_col[low:high] == seg_row[:, :high]) & (key_at <= query_at)
        out.append(jnp.where(allowed, 0.0, -1e30))
    return out


def row_splits(length):
    return [(at, at + length // 2) for at in (0, length // 2)]


def attend_kernel(
    copies, sizes, at_ref, own_ref, other_ref, seg_col, seg_row, cos_ref, sin_ref, *refs
):
    heads, kv_heads, sources = sizes
    pieces = refs[:sources]
    hid, normed, qs, ks, vs, mixed, lse, weights, small, out_weights, gains = refs[sources:-3]
    own, other, sems = refs[-3:]
    me, core = at_ref[0], at_ref[1]
    rows = own_ref.shape[0]
    length = 2 * rows
    hid[pl.ds(pl.multiple_of(core * rows, rows), rows)] = own_ref[...]
    hid[pl.ds(pl.multiple_of((1 - core) * rows, rows), rows)] = other_ref[...]
    lay_rows(copies, pieces, (weights, small, out_weights), sems, me)
    gains[...] = jnp.transpose(small[...].astype(f32))[: gains.shape[0]]
    value = hid[...].astype(f32)
    root = lax.rsqrt(jnp.mean(value * value, axis=1, keepdims=True) + epsilon)
    normed[...] = (value * root * gains[GAIN_A : GAIN_A + 1]).astype(bf16)
    qkv = lax.dot_general(normed[...], weights[...], NN, preferred_element_type=f32)
    cosine, sine = cos_ref[...], sin_ref[...]
    for head in range(heads):
        at = slice(head * HD, (head + 1) * HD)
        qs[:, at] = turn(qkv[:, at], cosine, sine).astype(bf16)
    for head in range(kv_heads):
        at = slice(head * HD, (head + 1) * HD)
        ks[:, at] = turn(qkv[:, heads * HD :][:, at], cosine, sine).astype(bf16)
    vs[...] = qkv[:, (heads + kv_heads) * HD :].astype(bf16)
    splits = row_splits(length)
    scale = 1.0 / math.sqrt(HD)
    for (low, high), mask in zip(splits, masks(seg_col[...], seg_row[...], splits)):
        for head in range(heads):
            at = slice(head * HD, (head + 1) * HD)
            kv = head // (heads // kv_heads)
            kv = slice(kv * HD, (kv + 1) * HD)
            scores = lax.dot_general(
                qs[low:high, at], ks[:high, kv], NT, preferred_element_type=f32
            )
            scores = scores * scale + mask
            peak = jnp.max(scores, axis=1, keepdims=True)
            expo = jnp.exp(scores - peak)
            total = jnp.sum(expo, axis=1, keepdims=True)
            lse[low:high, head : head + 1] = peak + jnp.log(total)
            probs = (expo * (1.0 / total)).astype(bf16)
            mixed[low:high, at] = lax.dot_general(
                probs, vs[:high, kv], NN, preferred_element_type=f32
            ).astype(bf16)
    for target, half in ((other, 1 - core), (own, core)):
        part = mixed[pl.ds(pl.multiple_of(half * rows, rows), rows)]
        target[...] = lax.dot_general(
            part, out_weights[...], NT, preferred_element_type=f32
        ).astype(target.dtype)


def middle_kernel(hidden, own, other, gains, middle, normed):
    value = hidden[...].astype(f32) + own[...] + other[...].astype(f32)
    middle[...] = value
    root = lax.rsqrt(jnp.mean(value * value, axis=1, keepdims=True) + epsilon)
    normed[...] = (value * root * gains[GAIN_F : GAIN_F + 1]).astype(bf16)


def middle_back_kernel(
    middle, normed, grad_out, code, router, gains, own, *refs
):
    others, (grad_middle, grad_round, small) = refs[:-3], refs[-3:]
    width = middle.shape[1]
    total = own[...].astype(f32)
    for other in others:
        total += other[...].astype(f32)
    routed = code[...].astype(f32) > 0.5
    logits = lax.dot_general(normed[...], router[...], NN, preferred_element_type=f32)
    logits = jnp.where(routed, logits, -1e30)
    expo = jnp.where(routed, jnp.exp(logits - jnp.max(logits, axis=1, keepdims=True)), 0.0)
    gates = expo / jnp.sum(expo, axis=1, keepdims=True)
    grad_gates = total[:, width:]
    grad_logits = gates * (grad_gates - jnp.sum(gates * grad_gates, axis=1, keepdims=True))
    high = grad_logits.astype(bf16)
    low = (grad_logits - high.astype(f32)).astype(bf16)
    grad_normed = total[:, :width]
    router_grad = jnp.zeros(small.shape, f32)
    for part in (high, low):
        grad_normed += lax.dot_general(part, router[...], NT, preferred_element_type=f32)
        router_grad += lax.dot_general(normed[...], part, TN, preferred_element_type=f32)
    value = middle[...]
    root = lax.rsqrt(jnp.mean(value * value, axis=1, keepdims=True) + epsilon)
    scaled = value * root
    column = jnp.sum(grad_normed * scaled, axis=0, keepdims=True)
    column = jnp.transpose(jnp.broadcast_to(column, (EXTRA, width)))
    lanes = lax.broadcasted_iota(jnp.int32, small.shape, 1)
    small[...] = jnp.where(lanes == GAIN_F, column, router_grad)
    grad_scaled = grad_normed * gains[GAIN_F : GAIN_F + 1]
    inner = jnp.mean(grad_scaled * scaled, axis=1, keepdims=True)
    result = grad_out[...].astype(f32) + root * (grad_scaled - scaled * inner)
    grad_middle[...] = result
    grad_round[...] = result.astype(bf16)


def attend_back_kernel(
    block,
    sizes,
    at_ref,
    own_ref,
    other_ref,
    mixed,
    out_weights,
    small_ref,
    qs,
    ks,
    vs,
    lse,
    seg_col,
    seg_row,
    cos_ref,
    sin_ref,
    hid,
    normed,
    weights,
    *refs,
):
    heads, kv_heads = sizes
    own, other, parts = refs[0], refs[1], refs[2:-6]
    acc, small, grads, whole, grad_mixed, out_acc = refs[-6:]
    me, core = at_ref[0], at_ref[1]
    length, width = hid.shape
    rows = own.shape[0]
    cols = grads.shape[1]
    whole[pl.ds(pl.multiple_of(core * rows, rows), rows)] = own_ref[...]
    whole[pl.ds(pl.multiple_of((1 - core) * rows, rows), rows)] = other_ref[...]
    grad_mixed[...] = lax.dot_general(
        whole[...], out_weights[...], NN, preferred_element_type=f32
    ).astype(bf16)
    out_acc[...] = lax.dot_general(whole[...], mixed[...], TN, preferred_element_type=f32)
    store_parts(out_acc, parts, me, block, cols + EXTRA)
    cosine, sine = cos_ref[...], -sin_ref[...]
    splits = row_splits(length)
    scale = 1.0 / math.sqrt(HD)
    per_group = heads // kv_heads
    bias = masks(seg_col[...], seg_row[...], splits)
    for kv_head in range(kv_heads):
        kv = slice(kv_head * HD, (kv_head + 1) * HD)
        grad_key = jnp.zeros((length, HD), f32)
        grad_value = jnp.zeros((length, HD), f32)
        for (low, high), mask in zip(splits, bias):
            key_sum = jnp.zeros((high, HD), f32)
            value_sum = jnp.zeros((high, HD), f32)
            for head in range(kv_head * per_group, (kv_head + 1) * per_group):
                at = slice(head * HD, (head + 1) * HD)
                query, grad = qs[low:high, at], grad_mixed[low:high, at]
                scores = lax.dot_general(query, ks[:high, kv], NT, preferred_element_type=f32)
                probs = jnp.exp(scores * scale + mask - lse[low:high, head : head + 1])
                grad_probs = lax.dot_general(
                    grad, vs[:high, kv], NT, preferred_element_type=f32
                )
                inner = jnp.sum(grad_probs * probs, axis=1, keepdims=True)
                grad_scores = (probs * (grad_probs - inner)).astype(bf16)
                grad_query = lax.dot_general(
                    grad_scores, ks[:high, kv], NN, preferred_element_type=f32
                )
                grads[low:high, at] = turn(
                    grad_query * scale, cosine[low:high], sine[low:high]
                ).astype(bf16)
                key_sum += lax.dot_general(grad_scores, query, TN, preferred_element_type=f32)
                value_sum += lax.dot_general(
                    probs.astype(bf16), grad, TN, preferred_element_type=f32
                )
            if high < length:
                pad = jnp.zeros((length - high, HD), f32)
                key_sum = jnp.concatenate([key_sum, pad], axis=0)
                value_sum = jnp.concatenate([value_sum, pad], axis=0)
            grad_key += key_sum
            grad_value += value_sum
        at = (heads + kv_head) * HD
        grads[:, at : at + HD] = turn(grad_key * scale, cosine, sine).astype(bf16)
        at += kv_heads * HD
        grads[:, at : at + HD] = grad_value.astype(bf16)
    acc[...] = lax.dot_general(normed[...], grads[...], TN, preferred_element_type=f32)
    store_parts(acc, parts, me, block, 0)
    value = hid[...].astype(f32)
    root = lax.rsqrt(jnp.mean(value * value, axis=1, keepdims=True) + epsilon)
    column = jnp.zeros((1, width), f32)
    for target, half in ((other, 1 - core), (own, core)):
        at = pl.ds(pl.multiple_of(half * rows, rows), rows)
        part = lax.dot_general(grads[at], weights[...], NT, preferred_element_type=f32)
        target[...] = part.astype(target.dtype)
        half_value = hid[at].astype(f32)
        half_root = lax.rsqrt(jnp.mean(half_value * half_value, axis=1, keepdims=True) + epsilon)
        column += jnp.sum(part * (half_value * half_root), axis=0, keepdims=True)
    lanes = lax.broadcasted_iota(jnp.int32, small.shape, 1)
    column = jnp.transpose(jnp.broadcast_to(column, (EXTRA, width)))
    small[...] = jnp.where(lanes == GAIN_A, column, small_ref[...])
    store_parts(small, parts, me, block, cols)


def slots_kernel(parts, at_ref, order_col, order_row, own, other, code, *refs):
    picks, rows_out, whole = refs[: len(parts)], refs[-2], refs[-1]
    core = at_ref[1]
    rows = own.shape[0]
    width = own.shape[1]
    whole[pl.ds(pl.multiple_of(core * rows, rows), rows), :width] = own[...]
    whole[pl.ds(pl.multiple_of((1 - core) * rows, rows), rows), :width] = other[...]
    whole[:, width:] = code[...]
    none = order_row.shape[0] // 2 * order_row.shape[1]
    first = core * sum(parts)
    for expert in range(order_row.shape[0]):
        row = order_row[expert : expert + 1, :]
        ahead = (order_col[:, expert : expert + 1] < row).astype(f32)
        position = jnp.sum(ahead, axis=0, keepdims=True).astype(jnp.int32)
        position = jnp.where(row < none, position, -1)
        low = first
        for pick, count in zip(picks, parts):
            slot = lax.broadcasted_iota(jnp.int32, (count, row.shape[1]), 0) + low
            pick[expert * count : (expert + 1) * count, :] = (slot == position).astype(bf16)
            low = low + count
    low = 0
    for pick, count in zip(picks, parts):
        taken = lax.dot_general(pick[...], whole[...], NN, preferred_element_type=f32)
        rows_out[:, low : low + count] = taken.astype(bf16).reshape(
            order_row.shape[0], count, whole.shape[1]
        )
        low += count


def take_kernel(at_ref, own, other, *refs):
    count = (len(refs) - 1) // 2
    picks, outs, whole = refs[:count], refs[count:-1], refs[-1]
    core = at_ref[1]
    rows = own.shape[0]
    whole[pl.ds(pl.multiple_of(core * rows, rows), rows)] = own[...]
    whole[pl.ds(pl.multiple_of((1 - core) * rows, rows), rows)] = other[...]
    for pick, out in zip(picks, outs):
        out[...] = lax.dot_general(
            pick[...], whole[...], NN, preferred_element_type=f32
        ).astype(bf16)


def give_kernel(count, at_ref, *refs):
    picks, values, (own, other) = refs[:count], refs[count:-2], refs[-2:]
    rows = own.shape[0]
    if len(values) < count:
        whole, values, low = values[0][...], [], 0
        for pick in picks:
            each = pick.shape[0] // whole.shape[0]
            values.append(whole[:, low : low + each].reshape(pick.shape[0], whole.shape[2]))
            low += each
    for target, half in ((other, 1 - at_ref[1]), (own, at_ref[1])):
        columns = pl.ds(pl.multiple_of(half * rows, rows), rows)
        total = None
        for pick, value in zip(picks, values):
            part = lax.dot_general(
                pick[:, columns], value[...], TN, preferred_element_type=f32
            )
            total = part if total is None else total + part
        target[...] = total.astype(target.dtype)


def gelu_parts(value):
    square = value * value
    inner = value * (0.7978845608028654 + 0.035677408136300125 * square)
    tanh = jnp.tanh(inner)
    half = 0.5 + 0.5 * tanh
    slope = half + 0.5 * value * (1.0 - tanh * tanh) * (
        0.7978845608028654 + 3.0 * 0.035677408136300125 * square
    )
    return value * half, slope


def moe_kernel(plan, at_ref, router_ref, x_in, g_in, *refs):
    copies, hidden, blocks, outer, first, groups = plan
    weight_count = len(set(c[0] for c in copies))
    if first:
        refs = refs[1:]
    sources, outs, refs = refs[:weight_count], refs[weight_count:][:5], refs[weight_count + 5 :]
    weights, xs, gs = refs[:3]
    buffers = refs[3:8]
    weight_sems, in_sems, out_sems = refs[8:]
    branch, gradn, act_all, gp_all, geo_all = buffers
    _, rows, width = xs.shape
    whole = 2 * hidden
    expert = at_ref[0] % CUBE

    weight_copies = []
    block_rows = weights.shape[0] // outer
    for number, (source, entry, low, length, offset, from_col, to_col, cols) in enumerate(copies):
        row = pl.multiple_of(((at_ref[0] // CUBE) ^ offset) * block_rows + low, 16)
        weight_copies.append(
            pltpu.make_async_copy(
                sources[source].at[entry, :, pl.ds(from_col, cols)],
                weights.at[pl.ds(row, length), pl.ds(to_col, cols)],
                weight_sems.at[number],
            )
        )
    weight_order = sorted(range(len(copies)), key=lambda k: copies[k][5] // hidden)
    in_copies = []
    for block in range(blocks):
        span = pl.ds(block * rows, rows)
        for kind, (source, target) in enumerate(((x_in, xs), (g_in, gs))):
            held = (span,)
            if kind == 1:
                held = pl.ds(block * groups, groups), pl.ds(first, rows // groups)
            in_copies.append(
                pltpu.make_async_copy(
                    source.at[held], target.at[block], in_sems.at[2 * block + kind]
                )
            )
    in_copies[0].start()
    for k in weight_order:
        weight_copies[k].start()
    for copy in in_copies[1:]:
        copy.start()
    out_copies = []
    for block in range(blocks):
        in_copies[2 * block].wait()
        x = xs[block]
        logits = lax.dot_general(x, router_ref[...], NN, preferred_element_type=f32)
        if block == 0:
            for k in weight_order:
                if copies[k][5] < 2 * hidden:
                    weight_copies[k].wait()
        pre = lax.dot_general(x, weights[:, : 2 * whole], NN, preferred_element_type=f32)
        in_copies[2 * block + 1].wait()
        both = gs[block].reshape(rows, gs.shape[3])
        routed = both[:, width:].astype(f32) > 0.5
        lanes = lax.broadcasted_iota(jnp.int32, routed.shape, 1)
        logits = jnp.where(routed, logits, -1e30)
        expo = jnp.where(routed, jnp.exp(logits - jnp.max(logits, axis=1, keepdims=True)), 0.0)
        total = jnp.sum(expo, axis=1, keepdims=True)
        gate = jnp.sum(jnp.where(lanes == expert, expo, 0.0), axis=1, keepdims=True)
        gate = gate / jnp.where(total > 0.0, total, 1.0)

        gate_pre, up_pre = pre[:, :whole], pre[:, whole:]
        gelu, slope = gelu_parts(gate_pre)
        act = (gelu * up_pre).astype(bf16)
        act_all[block] = act
        if block == 0:
            for k in weight_order:
                if copies[k][5] == 2 * hidden:
                    weight_copies[k].wait()
        down = weights[:, 2 * whole :]
        expert_out = lax.dot_general(act, down, NT, preferred_element_type=f32)
        branch[block] = (gate * expert_out).astype(bf16).reshape(branch.shape[1:])
        g = both[:, :width].astype(f32)
        grad_gate = jnp.sum(g * expert_out, axis=1, keepdims=True)
        gradn[block, :, width:] = jnp.where(lanes == expert, grad_gate, 0.0).astype(bf16)
        geo = (gate * g).astype(bf16)
        geo_all[block] = geo
        grad_act = lax.dot_general(geo, down, NN, preferred_element_type=f32)
        grad_gate_pre = (grad_act * up_pre * slope).astype(bf16)
        grad_up_pre = (grad_act * gelu).astype(bf16)
        for side in range(2):
            cols = slice(side * hidden, (side + 1) * hidden)
            for kind, part in enumerate((grad_gate_pre, grad_up_pre)):
                at = (2 * side + kind) * hidden
                gp_all[block, :, at : at + hidden] = part[:, cols]
        grad_in = lax.dot_general(
            grad_gate_pre, weights[:, :whole], NT, preferred_element_type=f32
        ) + lax.dot_general(
            grad_up_pre, weights[:, whole : 2 * whole], NT, preferred_element_type=f32
        )
        gradn[block, :, :width] = grad_in.astype(bf16)
        for number, (source, target) in enumerate(zip(buffers, outs)):
            if number == 0:
                held = pl.ds(block * groups, groups), pl.ds(first, rows // groups)
            else:
                held = (pl.ds(block * rows, rows),)
            copy = pltpu.make_async_copy(
                source.at[block], target.at[held], out_sems.at[5 * block + number]
            )
            copy.start()
            out_copies.append(copy)
    for copy in out_copies:
        copy.wait()


def moe(at, x, g, router, pieces, hidden, outer, sequences, capacity, branch=None):
    copies = []
    for source, (array, first, low, side) in enumerate(pieces):
        for entry in range(array.shape[0]):
            for kind in range(3):
                copies.append(
                    (source, entry, low, array.shape[1], first + entry, kind * hidden)
                    + ((2 * kind + side) * hidden, hidden)
                )
    total, width = x.shape
    blocks = 2
    rows = total // blocks
    widths = (width, width + EXTRA, 2 * hidden, 4 * hidden, width)
    each = total // sequences
    first = 0 if branch is None else capacity - each
    args = [x, g] + ([] if branch is None else [branch]) + [p[0] for p in pieces]
    groups = sequences // blocks
    buffers = [(blocks, rows, w) for w in widths]
    buffers[0] = (blocks, groups, each, width)
    return pl.pallas_call(
        functools.partial(moe_kernel, (copies, hidden, blocks, outer, first, groups)),
        out_shape=[jax.ShapeDtypeStruct((sequences, capacity, width), bf16)]
        + [jax.ShapeDtypeStruct((total, w), bf16) for w in widths[1:]],
        in_specs=[pl.BlockSpec(memory_space=pltpu.SMEM), pl.BlockSpec(memory_space=pltpu.VMEM)]
        + [pl.BlockSpec(memory_space=pl.ANY)] * len(args),
        out_specs=[pl.BlockSpec(memory_space=pl.ANY)] * 5,
        scratch_shapes=[
            pltpu.VMEM((width, 6 * hidden), bf16),
            pltpu.VMEM((blocks, rows, width), bf16),
            pltpu.VMEM((blocks, groups, each, width + EXTRA), bf16),
        ]
        + [pltpu.VMEM(dims, bf16) for dims in buffers]
        + [
            pltpu.SemaphoreType.DMA((len(copies),)),
            pltpu.SemaphoreType.DMA((2 * blocks,)),
            pltpu.SemaphoreType.DMA((5 * blocks,)),
        ],
        input_output_aliases={} if branch is None else {4: 0},
        compiler_params=pltpu.CompilerParams(vmem_limit_bytes=60 * 1024 * 1024),
        cost_estimate=BRIEF,
        name="experts",
    )(at, router, *args)


def weight_grads_kernel(calls, at_ref, *refs):
    pairs = []
    for _ in range(2):
        pairs.append((refs[:calls], refs[calls : 2 * calls]))
        refs = refs[2 * calls :]
    own, other, *buffers, sems = refs
    cols = buffers[0].shape[1]
    columns = pl.ds(pl.multiple_of(at_ref[2] * cols, cols), cols)
    copies = []
    for number, (lefts, rights) in enumerate(pairs):
        row = 0
        for left, right in zip(lefts, rights):
            rows = pl.ds(row, left.shape[0])
            for source, target in (
                (left.at[:, columns], buffers[2 * number].at[rows]),
                (right, buffers[2 * number + 1].at[rows]),
            ):
                copies.append(pltpu.make_async_copy(source, target, sems.at[len(copies)]))
                copies[-1].start()
            row += left.shape[0]
    at = 0
    for number in range(2):
        for copy in copies[2 * calls * number : 2 * calls * (number + 1)]:
            copy.wait()
        total = lax.dot_general(
            buffers[2 * number][...],
            buffers[2 * number + 1][...],
            TN,
            preferred_element_type=f32,
        ).astype(bf16)
        width = total.shape[1] // 2
        own[:, at : at + width] = total[:, :width]
        other[:, at : at + width] = total[:, width:]
        at += width


def weight_grads(at, half, pre, down):
    args, scratch, width = [], [], 0
    for pairs in (pre, down):
        args += [p[0] for p in pairs] + [p[1] for p in pairs]
        rows = sum(p[0].shape[0] for p in pairs)
        left, right = pairs[0][0].shape[1] // 2, pairs[0][1].shape[1]
        scratch += [(rows, left), (rows, right)]
        width += right // 2
    return pl.pallas_call(
        functools.partial(weight_grads_kernel, len(pre)),
        out_shape=[jax.ShapeDtypeStruct((left, width), bf16)] * 2,
        in_specs=[pl.BlockSpec(memory_space=pltpu.SMEM)]
        + [pl.BlockSpec(memory_space=pl.ANY)] * len(args),
        out_specs=[pl.BlockSpec(memory_space=pltpu.VMEM)] * 2,
        scratch_shapes=[pltpu.VMEM(dims, bf16) for dims in scratch]
        + [pltpu.SemaphoreType.DMA((len(args),))],
        compiler_params=pltpu.CompilerParams(vmem_limit_bytes=60 * 1024 * 1024),
        cost_estimate=FREE,
        name="weight_grads",
    )(jnp.concatenate([at, half.reshape(1)]), *args)


def per_device(
    count,
    hidden_in,
    segment_ids,
    routes,
    slot_order,
    gain_attn,
    w_query,
    w_key,
    w_value,
    w_out,
    gain_ffn,
    w_router,
    w_gate,
    w_up,
    w_down,
    grad_out,
):
    tok_rows, width = hidden_in.shape
    seq_len = segment_ids.shape[0]
    top_count = routes.shape[1]
    experts, block, hidden = w_gate.shape
    capacity = 9 * seq_len * top_count // (8 * experts)
    me = lax.axis_index("dp").astype(jnp.int32)
    core = lax.axis_index("tensor").astype(jnp.int32)
    at = jnp.stack([me, core])
    groups = [list(range(first, first + CUBE)) for first in range(0, count, CUBE)]
    heads_cols, kv_cols = w_query.shape[1], w_key.shape[1]
    qkv_cols = heads_cols + 2 * kv_cols
    heads, kv_heads = heads_cols // HD, kv_cols // HD

    def shape(rows, cols, dtype=bf16):
        return jax.ShapeDtypeStruct((rows, cols), dtype)

    def near(own):
        return {0: own} | {bit: swap(own, bit, count) for bit in NEAR}

    def far(got):
        spans = halves(got[0].shape[0])
        return got | {
            3: swap(cut(got[2], spans[0], 0), 1, count),
            9: swap(cut(got[1], spans[1], 0), 2, count),
            6: swap(got[4], 2, count),
            5: swap(got[4], 1, count),
        }

    def last(got):
        spans = halves(got[0].shape[0])
        return got | {
            7: swap(cut(got[6], spans[0], 0), 1, count),
            8: swap(cut(got[5], spans[1], 0), 2, count),
        }

    small = jnp.concatenate([w_router, gain_attn[:, None], gain_ffn[:, None]], axis=1)
    small = jnp.pad(small, ((0, 0), (0, EXTRA - small.shape[1])))
    pair = outer_pair(
        jnp.concatenate([w_query, w_key, w_value, small, w_out.T], axis=1), count
    )
    hidden_other = swap_core(hidden_in)

    expert_shard = jnp.concatenate([w_gate, w_up, jnp.swapaxes(w_down, 1, 2)], axis=2)
    expert_rows = lax.all_to_all(
        expert_shard.reshape(experts * block, 3 * hidden),
        "dp",
        0,
        0,
        tiled=True,
        axis_index_groups=groups,
    )

    order = jnp.min(
        jnp.where(
            routes[:, :, None] == jnp.arange(experts, dtype=jnp.int32),
            slot_order[0].reshape(seq_len, top_count)[:, :, None],
            seq_len * top_count,
        ),
        axis=1,
    )
    code = (order < seq_len * top_count).astype(bf16)
    code = jnp.pad(code, ((0, 0), (0, EXTRA - experts)))
    code_own = lax.dynamic_slice_in_dim(code, core * tok_rows, tok_rows, 0)
    first_part = capacity // 4 // 16 * 16
    slot_parts = (first_part, capacity // 2 - first_part)
    grad_other = swap_core(grad_out)
    slots = vmem_call(
        functools.partial(slots_kernel, slot_parts),
        [shape(experts * part, seq_len) for part in slot_parts]
        + [jax.ShapeDtypeStruct((experts, sum(slot_parts), width + EXTRA), bf16)],
        [pltpu.VMEM((seq_len, width + EXTRA), bf16)],
        [(at, 1), (order, 0), (order.T, 0), (grad_out, 0), (grad_other, 0), (code, 0)],
        "slots",
    )
    picks, grad_rows = slots[:2], slots[2]

    def exchange(rows):
        return lax.all_to_all(rows, "dp", 0, 0, tiled=True, axis_index_groups=groups)

    cosine, sine_table = rope_tables(seq_len, HD)
    cosine = jnp.concatenate([cosine, cosine], axis=1)
    sine_table = jnp.concatenate([-sine_table, sine_table], axis=1)
    seg_col, seg_row = segment_ids[:, None], segment_ids[None, :]

    pair, expert_rows, code_own = gate(
        [pair, expert_rows, code_own], cosine, sine_table, hidden_other, grad_other
    )
    if count == 2 * CUBE:
        edges = [expert_rows.shape[0] * k // 48 // 16 * 16 for k in (0, 10, 26, 26, 37, 48)]
    else:
        edges = [0] * 5 + [expert_rows.shape[0]]
    pieces = [(expert_rows[None], 0, 0, 0), (swap_core(expert_rows)[None], 0, 0, 1)]

    def outer_chunk(k, *events):
        low, high = edges[k], edges[k + 1]
        if high == low:
            return [], []
        (chunk,) = gate([cut(expert_rows, (low, high), 0)], *events)
        arrays, first, swapped = outer_gather(chunk, count)[1:], 1, []
        for array in arrays:
            swapped.append(swap_core(array))
            pieces.append((array, first, low, 0))
            pieces.append((swapped[-1], first, low, 1))
            first += array.shape[0]
        return arrays, swapped

    with jax.named_scope("weights_near"):
        got = near(pair)
    arrays, swapped = outer_chunk(0, pair)
    got = gate_dict(got, NEAR, grad_rows, arrays, pieces[1][0])
    with jax.named_scope("weights_far"):
        got = far(got)
    arrays, swapped_next = outer_chunk(1, got[1])
    got = gate_dict(got, FAR, arrays, swapped)
    with jax.named_scope("weights_last"):
        got = last(got)
    arrays, swapped = outer_chunk(2, got[3])
    got = gate_dict(got, LAST, arrays, swapped_next)
    sources, copies = piece_copies(got, block, me, count)
    grad_rows, seg_col = gate([grad_rows, seg_col], got[7])
    with jax.named_scope("grads_rows"):
        grad_rows = exchange(grad_rows)
    attended = vmem_call(
        functools.partial(attend_kernel, copies, (heads, kv_heads, len(sources))),
        [
            shape(seq_len, width),
            shape(seq_len, width),
            shape(seq_len, heads_cols),
            shape(seq_len, kv_cols),
            shape(seq_len, kv_cols),
            shape(seq_len, heads_cols),
            shape(seq_len, HD, f32),
            shape(width, qkv_cols),
            shape(width, EXTRA),
            shape(width, heads_cols),
            shape(16, width, f32),
            shape(tok_rows, width, f32),
            shape(tok_rows, width),
        ],
        [pltpu.SemaphoreType.DMA((3 * len(copies),))],
        [(at, 1), (hidden_in, 0), (hidden_other, 0), (seg_col, 0), (seg_row, 0)]
        + [(cosine, 0), (sine_table, 0)]
        + [(piece, 2) for piece in sources],
        "attend",
        flops=2 * seq_len * (width * (qkv_cols + heads_cols) + heads_cols * seq_len),
    )
    hid, normed, qs, ks, vs, mixed, lse, full_qkv, router, out_wt, gains = attended[:-2]
    attn_own, attn_other = attended[-2:]
    arrays, swapped_next = outer_chunk(3, got[7])
    middle, normed2 = vmem_call(
        middle_kernel,
        [shape(tok_rows, width, f32), shape(tok_rows, width)],
        [],
        [(hidden_in, 0), (attn_own, 0), (swap_core(attn_other), 0), (gains, 0)],
        "middle",
    )

    rows = vmem_call(
        take_kernel,
        [shape(experts * part, width) for part in slot_parts],
        [pltpu.VMEM((seq_len, width), bf16)],
        [(at, 1), (normed2, 0), (swap_core(normed2), 0)] + [(pick, 0) for pick in picks],
        "take",
    )
    rows = list(rows)
    rows[0], grad_rows = gate([rows[0], grad_rows], arrays, swapped)
    with jax.named_scope("tokens_rows"):
        x_first = exchange(rows[0])
    arrays, _ = outer_chunk(4, rows[0])
    x_first, rows_second = gate([x_first, rows[1]], arrays, swapped_next)
    with jax.named_scope("tokens_rows"):
        x_second = exchange(rows_second)

    def experts_on(x, g, router, branch=None):
        held = (CUBE, sum(slot_parts))
        return moe(at, x, g, router, pieces, hidden, count // CUBE, *held, branch)

    branch, gradn_first, *first = experts_on(x_first, grad_rows, router)
    with jax.named_scope("gradn_rows"):
        gradn_first = exchange(gradn_first)
    (second_router,) = gate([router], first[0])
    branch, gradn_second, *second = experts_on(x_second, grad_rows, second_router, branch)

    xs = (x_first, x_second)
    pre_pairs = [(x, call[1]) for x, call in zip(xs, (first, second))]
    down_pairs = [(call[2], call[0]) for call in (first, second)]
    bits = outer_bits(count)
    top = (me // bits[-1]) % 2 if bits else jnp.zeros((), jnp.int32)

    def half_grads(half, *events):
        half = gate([half.reshape(1)], *events)[0]
        return weight_grads(at, half, pre_pairs, down_pairs)

    with jax.named_scope("gradn_rows"):
        gradn_second = exchange(gradn_second)
    sent, sent_other = half_grads(1 - top, second[0])
    keep, keep_other = half_grads(top, sent_other)
    with jax.named_scope("expert_scatter"):
        sent = add_round(sent, swap_core(sent_other))
        sent_got = swap(sent, bits[-1], count) if bits else sent

    def give(picks, values, name):
        own, other = vmem_call(
            functools.partial(give_kernel, len(picks)),
            [shape(tok_rows, values[0].shape[-1], f32), shape(tok_rows, values[0].shape[-1])],
            [],
            [(at, 1)] + [(pick, 0) for pick in picks] + [(value, 0) for value in values],
            name,
        )
        return own, swap_core(other)

    gradn_second, gradn_first = gate([gradn_second, gradn_first], sent, keep)
    gradn = list(give(picks, (gradn_first, gradn_second), "give_gradn"))

    grad_middle, grad_mid_r, small_f = vmem_call(
        middle_back_kernel,
        [shape(tok_rows, width, f32), shape(tok_rows, width), shape(width, EXTRA, f32)],
        [],
        [(middle, 0), (normed2, 0), (grad_out, 0), (code_own, 0), (router, 0), (gains, 0)]
        + [(array, 0) for array in gradn],
        "middle_back",
    )

    grad_mid_other = swap_core(grad_mid_r)
    (branch,) = gate([branch], gradn_second)
    with jax.named_scope("branch_rows"):
        branch = exchange(branch)
    normed_own, normed_other, *parts = vmem_call(
        functools.partial(attend_back_kernel, block, (heads, kv_heads)),
        [shape(tok_rows, width, f32), shape(tok_rows, width)]
        + part_shapes(count, block, qkv_cols + EXTRA + heads_cols),
        [
            pltpu.VMEM((width, qkv_cols), f32),
            pltpu.VMEM((width, EXTRA), f32),
            pltpu.VMEM((seq_len, qkv_cols), bf16),
            pltpu.VMEM((seq_len, width), bf16),
            pltpu.VMEM((seq_len, heads_cols), bf16),
            pltpu.VMEM((width, heads_cols), f32),
        ],
        [(at, 1), (grad_mid_r, 0), (grad_mid_other, 0), (mixed, 0), (out_wt, 0)]
        + [(small_f, 0), (qs, 0), (ks, 0), (vs, 0), (lse, 0), (seg_col, 0)]
        + [(seg_row, 0), (cosine, 0), (sine_table, 0), (hid, 0), (normed, 0), (full_qkv, 0)],
        "attend_back",
        flops=4 * seq_len * (width * (qkv_cols + heads_cols) + 2 * heads_cols * seq_len),
    )
    parts = spread_parts(parts, me, count)

    keep_swapped = swap_core(keep_other)
    parts = gate_dict(parts, (3, 9) + LAST, keep_swapped)
    with jax.named_scope("attn_last"):
        got = sum_last(parts, count)
    normed_swapped = swap_core(normed_other)
    gated = gate([got[7], got[8], parts[3], parts[9]], normed_swapped)
    got, parts[3], parts[9] = dict(zip(LAST, gated)), gated[2], gated[3]
    with jax.named_scope("attn_far"):
        terms = far_terms(parts, got)
        attn_far = sum_far(parts, terms, count)
    with jax.named_scope("expert_scatter"):
        sent_got, keep = gate([sent_got, keep], terms)
        if bits:
            total = keep.astype(f32) + keep_swapped.astype(f32) + sent_got.astype(f32)
        else:
            total = jnp.concatenate([add_round(keep, keep_swapped), sent_got]).astype(f32)
        for bit in reversed(bits[:-1]):
            half = total.shape[0] // 2
            high = (me // bit) % 2
            mine = lax.dynamic_slice_in_dim(total, high * half, half, 0)
            other = lax.dynamic_slice_in_dim(total, (1 - high) * half, half, 0)
            total = mine + swap(other.astype(bf16), bit, count).astype(f32)
        total = total.astype(bf16)
    grad_normed = normed_own + normed_swapped.astype(f32)
    gated = gate([attn_far[k] for k in FAR] + [branch, total])
    attn_far, branch, total = dict(zip(FAR, gated)), gated[4], gated[5]
    with jax.named_scope("attn_near"):
        attn_near = sum_near(near_terms(parts, attn_far), count)
    branch_own, branch_other = give(picks, (branch,), "give_branch")
    with jax.named_scope("expert_scatter"):
        total = exchange(total)
    attn_near = gate_dict(attn_near, NEAR, branch_own)
    with jax.named_scope("attn_outer"):
        attn_grads = outer_sum(sum_own(parts, attn_near), count)
    layer_out = middle + branch_own + branch_other.astype(f32)

    expert_grads = total.reshape(experts, block, 3 * hidden).astype(f32)
    grad_gate_w = expert_grads[:, :, :hidden]
    grad_up_w = expert_grads[:, :, hidden : 2 * hidden]
    grad_down_w = jnp.swapaxes(expert_grads[:, :, 2 * hidden :], 1, 2)
    scaled_in, root_in = rms_parts(hidden_in.astype(f32))
    grad_in = grad_middle + norm_backward(grad_normed, scaled_in, root_in, gains[GAIN_A])
    smalls = attn_grads[:, qkv_cols : qkv_cols + EXTRA]
    smalls = smalls + swap_core(smalls)
    return (
        layer_out,
        grad_in,
        smalls[:, GAIN_A],
        attn_grads[:, :heads_cols],
        attn_grads[:, heads_cols : heads_cols + kv_cols],
        attn_grads[:, heads_cols + kv_cols : qkv_cols],
        attn_grads[:, qkv_cols + EXTRA :].T,
        smalls[:, GAIN_F],
        smalls[:, :experts],
        grad_gate_w,
        grad_up_w,
        grad_down_w,
    )


def solution(mesh):
    return jax.shard_map(
        functools.partial(per_device, mesh.shape["dp"]),
        mesh=mesh,
        in_specs=(
            P(("dp", "tensor"), None),
            P("dp"),
            P("dp", None),
            P("dp", None),
            P("dp"),
            P("dp", "tensor"),
            P("dp", "tensor"),
            P("dp", "tensor"),
            P("tensor", "dp"),
            P("dp"),
            P("dp", None),
            P(None, "dp", "tensor"),
            P(None, "dp", "tensor"),
            P(None, "tensor", "dp"),
            P(("dp", "tensor"), None),
        ),
        out_specs=(
            P(("dp", "tensor"), None),
            P(("dp", "tensor"), None),
            P("dp"),
            P("dp", "tensor"),
            P("dp", "tensor"),
            P("dp", "tensor"),
            P("tensor", "dp"),
            P("dp"),
            P("dp", None),
            P(None, "dp", "tensor"),
            P(None, "dp", "tensor"),
            P(None, "tensor", "dp"),
        ),
        check_vma=False,
    )
```

```python
import functools
import math

import jax
import jax.numpy as jnp
from jax import lax
from jax.experimental import pallas as pl
from jax.experimental.pallas import tpu as pltpu
from jax.sharding import PartitionSpec as P

HD = 128
EXTRA = 128
GAIN_A, GAIN_F = 8, 9
CUBE = 8
BRIEF = pl.CostEstimate(flops=0, bytes_accessed=3_000_000, transcendentals=0)
LIGHT = ("attend", "middle", "take", "give_gradn", "middle_back", "attend_back")
FREE = pl.CostEstimate(flops=0, bytes_accessed=0, transcendentals=0)
epsilon = 1e-06
highest = lax.Precision.HIGHEST
f32 = jnp.float32
bf16 = jnp.bfloat16
NN = (((1,), (0,)), ((), ()))
NT = (((1,), (1,)), ((), ()))
TN = (((0,), (0,)), ((), ()))


def rms_parts(values):
    inverse_root = lax.rsqrt(jnp.mean(values * values, axis=-1, keepdims=True) + epsilon)
    return (values * inverse_root, inverse_root)


def norm_backward(grad_normed, scaled, inverse_root, gain):
    grad_scaled = grad_normed * gain
    inner = jnp.mean(grad_scaled * scaled, axis=-1, keepdims=True)
    return inverse_root * (grad_scaled - scaled * inner)


def rope_tables(length, size):
    inverse = 10000.0 ** (-jnp.arange(size // 2, dtype=f32) / (size // 2))
    angle = jnp.arange(length, dtype=f32)[:, None] * inverse[None, :]
    return (jnp.cos(angle), jnp.sin(angle))


def swap(values, bit, count):
    return lax.ppermute(values, "dp", [(i, i ^ bit) for i in range(count)])


def swap_core(values):
    return lax.ppermute(values, "tensor", [(0, 1), (1, 0)])


def gate(values, *events):
    values = list(values)
    flat = jax.tree.leaves(events)
    return pl.pallas_call(
        lambda *refs: None,
        out_shape=[jax.ShapeDtypeStruct(v.shape, v.dtype) for v in values],
        in_specs=[pl.BlockSpec(memory_space=pl.ANY)] * (len(values) + len(flat)),
        out_specs=[pl.BlockSpec(memory_space=pl.ANY)] * len(values),
        input_output_aliases={i: i for i in range(len(values))},
        compiler_params=pltpu.CompilerParams(vmem_limit_bytes=60 * 1024 * 1024),
        cost_estimate=BRIEF,
        name="gate",
    )(*values, *flat)


def gate_dict(got, keys, *events):
    return got | dict(zip(keys, gate([got[k] for k in keys], *events)))


def halves(rows):
    part = rows // 2
    return ((0, part), (part, rows))


def cut(values, span, axis):
    return lax.slice_in_dim(values, span[0], span[1], axis=axis)


NEAR, FAR, LAST = (1, 2, 4), (3, 9, 6, 5), (7, 8)


def add_round(left, right):
    return (left.astype(f32) + right.astype(f32)).astype(bf16)


def sum_last(parts, count):
    return {7: swap(parts[7], 1, count), 8: swap(parts[8], 2, count)}


def patch_kernel(first, second, low, high, first_out, second_out):
    first_out[...] = (first[...].astype(f32) + low[...].astype(f32)).astype(bf16)
    second_out[...] = (second[...].astype(f32) + high[...].astype(f32)).astype(bf16)


def patch(first, second, low, high):
    shape = first.shape
    half = low.shape
    if half[1] % 16:
        return (
            jnp.concatenate([add_round(first[: half[0]], low), first[half[0] :]], axis=0),
            jnp.concatenate([second[: half[0]], add_round(second[half[0] :], high)], axis=0),
        )
    top = pl.BlockSpec(half, lambda i: (0, 0, 0))
    bottom = pl.BlockSpec(half, lambda i: (1, 0, 0))
    return pl.pallas_call(
        patch_kernel,
        grid=(1,),
        out_shape=[jax.ShapeDtypeStruct(shape, bf16)] * 2,
        in_specs=[top, bottom, top, top],
        out_specs=[top, bottom],
        input_output_aliases={0: 0, 1: 1},
        compiler_params=pltpu.CompilerParams(vmem_limit_bytes=60 * 1024 * 1024),
        cost_estimate=FREE,
        name="patch",
    )(first, second, low, high)


def far_terms(parts, got):
    return patch(parts[6], parts[5], got[7], got[8])


def sum_far(parts, terms, count):
    first, second = terms
    return {
        6: swap(first, 2, count),
        5: swap(second, 1, count),
        3: swap(parts[3], 1, count),
        9: swap(parts[9], 2, count),
    }


def terms_kernel(one, two, four, six, five, three, nine, one_out, two_out, four_out):
    four_out[...] = (
        four[...].astype(f32) + six[...].astype(f32) + five[...].astype(f32)
    ).astype(bf16)
    first = three.shape[0]
    two_out[:first] = (two[:first].astype(f32) + three[...].astype(f32)).astype(bf16)
    two_out[first:] = two[first:]
    one_out[:first] = one[:first]
    one_out[first:] = (one[first:].astype(f32) + nine[...].astype(f32)).astype(bf16)


def near_terms(parts, got):
    args = [parts[bit] for bit in NEAR] + [got[k] for k in (6, 5, 3, 9)]
    shape = parts[1].shape
    grid = 2 if shape[1] % 32 == 0 else 1

    def spec(dims):
        return pl.BlockSpec((dims[0], dims[1] // grid, dims[2]), lambda i: (0, i, 0))

    outs = pl.pallas_call(
        terms_kernel,
        grid=(grid,),
        out_shape=[jax.ShapeDtypeStruct(shape, bf16)] * 3,
        in_specs=[spec(arg.shape) for arg in args],
        out_specs=[spec(shape)] * 3,
        compiler_params=pltpu.CompilerParams(vmem_limit_bytes=60 * 1024 * 1024),
        cost_estimate=FREE,
        name="terms",
    )(*args)
    return dict(zip(NEAR, outs))


def sum_near(terms, count):
    return {bit: swap(terms[bit], bit, count) for bit in NEAR}


def sum_own(parts, got):
    return parts[0].astype(f32) + (
        got[1].astype(f32) + (got[2].astype(f32) + got[4].astype(f32))
    )


def outer_bits(count):
    bits, bit = [], CUBE
    while bit < count:
        bits.append(bit)
        bit *= 2
    return bits


def outer_gather(own, count):
    pieces = [own[None]]
    for bit in outer_bits(count):
        pieces.append(swap(jnp.concatenate(pieces, axis=0), bit, count))
    return pieces


def outer_pair(shard, count):
    return jnp.concatenate(outer_gather(shard, count), axis=0)


def piece_copies(got, block, me, count):
    outer = got[0].shape[0]
    if block % 16:
        wholes = got | {3: jnp.concatenate([got[3], got[9]]), 7: jnp.concatenate([got[7], got[8]])}
        stacked = jnp.stack([wholes[b] for b in range(CUBE)], axis=1)
        whole = stacked.reshape(count, block, -1)[jnp.arange(count) ^ me]
        return [whole.reshape(1, count * block, -1)], [(0, 0, count * block, None, block)]
    sources, copies = [], []
    for b in range(CUBE + 2):
        first = outer // 2 if b >= 8 else 0
        offset = {8: 7, 9: 3}.get(b, b)
        for j in range(got[b].shape[0]):
            copies.append((b, j, block, 8 * (first + j) + offset, block))
        sources.append(got[b])
    return sources, copies


def lay_rows(copies, sources, targets, sems, me):
    started = []
    for number, (source, entry, rows, offset, block) in enumerate(copies):
        row = 0 if offset is None else pl.multiple_of((me ^ offset) * block, 16)
        column = 0
        for k, target in enumerate(targets):
            cols = target.shape[1]
            copy = pltpu.make_async_copy(
                sources[source].at[entry, :, pl.ds(column, cols)],
                target.at[pl.ds(row, rows)],
                sems.at[len(targets) * number + k],
            )
            copy.start()
            started.append(copy)
            column += cols
    for copy in started:
        copy.wait()


def part_order(count):
    outer = count // CUBE
    first, second = halves(outer)
    offsets = {3: first, 7: first}
    order = [(b, offsets.get(b, (0, outer))) for b in range(CUBE)]
    return order + [(7, second), (3, second)]


def part_shapes(count, block, width):
    if block % 16:
        return [jax.ShapeDtypeStruct((count * block, width), bf16)]
    return [
        jax.ShapeDtypeStruct((span[1] - span[0], block, width), bf16)
        for _, span in part_order(count)
    ]


def store_parts(whole, parts, me, block, at):
    cols = pl.ds(at, whole.shape[1])
    if len(parts) == 1:
        parts[0][:, cols] = whole[...].astype(bf16)
        return
    for part, (offset, span) in zip(parts, part_order(whole.shape[0] // block)):
        for j in range(part.shape[0]):
            row = pl.multiple_of((me ^ (8 * (span[0] + j) + offset)) * block, 16)
            part[j, :, cols] = whole[pl.ds(row, block)].astype(bf16)


def spread_parts(parts, me, count):
    if len(parts) > 1:
        return dict(enumerate(parts))
    blocks = parts[0].reshape(count, parts[0].shape[0] // count, -1)
    return {
        k: blocks[(offset + CUBE * jnp.arange(*span)) ^ me]
        for k, (offset, span) in enumerate(part_order(count))
    }


def outer_sum(total, count):
    for bit in reversed(outer_bits(count)):
        half = total.shape[0] // 2
        total = total[:half] + swap(total[half:].astype(bf16), bit, count).astype(f32)
    return total[0]


def vmem_call(kernel, out_shapes, scratch, args, name, smem=(), flops=0):
    spaces = {0: pltpu.VMEM, 1: pltpu.SMEM, 2: pl.ANY}
    moved = sum(math.prod(o.shape) * o.dtype.itemsize for o in out_shapes)
    moved += sum(math.prod(a.shape) * a.dtype.itemsize for a, _ in args)
    return pl.pallas_call(
        kernel,
        out_shape=out_shapes,
        in_specs=[pl.BlockSpec(memory_space=spaces[space]) for _, space in args],
        out_specs=[pl.BlockSpec(memory_space=pltpu.VMEM)] * len(out_shapes),
        scratch_shapes=scratch,
        compiler_params=pltpu.CompilerParams(vmem_limit_bytes=60 * 1024 * 1024),
        cost_estimate=FREE if name in LIGHT else BRIEF,
        name=name,
    )(*[a for a, _ in args])


def turn(values, cosine, sine):
    return values * cosine + pltpu.roll(values, values.shape[1] // 2, 1) * sine


def masks(seg_col, seg_row, splits):
    out = []
    for low, high in splits:
        shape = (high - low, high)
        query_at = lax.broadcasted_iota(jnp.int32, shape, 0) + low
        key_at = lax.broadcasted_iota(jnp.int32, shape, 1)
        allowed = (seg_col[low:high] == seg_row[:, :high]) & (key_at <= query_at)
        out.append(jnp.where(allowed, 0.0, -1e30))
    return out


def row_splits(length):
    return [(at, at + length // 2) for at in (0, length // 2)]


def attend_kernel(
    copies, sizes, at_ref, own_ref, other_ref, seg_col, seg_row, cos_ref, sin_ref, *refs
):
    heads, kv_heads, sources = sizes
    pieces = refs[:sources]
    hid, normed, qs, ks, vs, mixed, lse, weights, small, out_weights, gains = refs[sources:-3]
    own, other, sems = refs[-3:]
    me, core = at_ref[0], at_ref[1]
    rows = own_ref.shape[0]
    length = 2 * rows
    hid[pl.ds(pl.multiple_of(core * rows, rows), rows)] = own_ref[...]
    hid[pl.ds(pl.multiple_of((1 - core) * rows, rows), rows)] = other_ref[...]
    lay_rows(copies, pieces, (weights, small, out_weights), sems, me)
    gains[...] = jnp.transpose(small[...].astype(f32))[: gains.shape[0]]
    value = hid[...].astype(f32)
    root = lax.rsqrt(jnp.mean(value * value, axis=1, keepdims=True) + epsilon)
    normed[...] = (value * root * gains[GAIN_A : GAIN_A + 1]).astype(bf16)
    qkv = lax.dot_general(normed[...], weights[...], NN, preferred_element_type=f32)
    cosine, sine = cos_ref[...], sin_ref[...]
    for head in range(heads):
        at = slice(head * HD, (head + 1) * HD)
        qs[:, at] = turn(qkv[:, at], cosine, sine).astype(bf16)
    for head in range(kv_heads):
        at = slice(head * HD, (head + 1) * HD)
        ks[:, at] = turn(qkv[:, heads * HD :][:, at], cosine, sine).astype(bf16)
    vs[...] = qkv[:, (heads + kv_heads) * HD :].astype(bf16)
    splits = row_splits(length)
    scale = 1.0 / math.sqrt(HD)
    for (low, high), mask in zip(splits, masks(seg_col[...], seg_row[...], splits)):
        for head in range(heads):
            at = slice(head * HD, (head + 1) * HD)
            kv = head // (heads // kv_heads)
            kv = slice(kv * HD, (kv + 1) * HD)
            scores = lax.dot_general(
                qs[low:high, at], ks[:high, kv], NT, preferred_element_type=f32
            )
            scores = scores * scale + mask
            peak = jnp.max(scores, axis=1, keepdims=True)
            expo = jnp.exp(scores - peak)
            total = jnp.sum(expo, axis=1, keepdims=True)
            lse[low:high, head : head + 1] = peak + jnp.log(total)
            probs = (expo * (1.0 / total)).astype(bf16)
            mixed[low:high, at] = lax.dot_general(
                probs, vs[:high, kv], NN, preferred_element_type=f32
            ).astype(bf16)
    for target, half in ((other, 1 - core), (own, core)):
        part = mixed[pl.ds(pl.multiple_of(half * rows, rows), rows)]
        target[...] = lax.dot_general(
            part, out_weights[...], NT, preferred_element_type=f32
        ).astype(target.dtype)


def middle_kernel(hidden, own, other, gains, middle, normed):
    value = hidden[...].astype(f32) + own[...] + other[...].astype(f32)
    middle[...] = value
    root = lax.rsqrt(jnp.mean(value * value, axis=1, keepdims=True) + epsilon)
    normed[...] = (value * root * gains[GAIN_F : GAIN_F + 1]).astype(bf16)


def middle_back_kernel(
    middle, normed, grad_out, code, router, gains, own, *refs
):
    others, (grad_middle, grad_round, small) = refs[:-3], refs[-3:]
    width = middle.shape[1]
    total = own[...].astype(f32)
    for other in others:
        total += other[...].astype(f32)
    routed = code[...].astype(f32) > 0.5
    logits = lax.dot_general(normed[...], router[...], NN, preferred_element_type=f32)
    logits = jnp.where(routed, logits, -1e30)
    expo = jnp.where(routed, jnp.exp(logits - jnp.max(logits, axis=1, keepdims=True)), 0.0)
    gates = expo / jnp.sum(expo, axis=1, keepdims=True)
    grad_gates = total[:, width:]
    grad_logits = gates * (grad_gates - jnp.sum(gates * grad_gates, axis=1, keepdims=True))
    high = grad_logits.astype(bf16)
    low = (grad_logits - high.astype(f32)).astype(bf16)
    grad_normed = total[:, :width]
    router_grad = jnp.zeros(small.shape, f32)
    for part in (high, low):
        grad_normed += lax.dot_general(part, router[...], NT, preferred_element_type=f32)
        router_grad += lax.dot_general(normed[...], part, TN, preferred_element_type=f32)
    value = middle[...]
    root = lax.rsqrt(jnp.mean(value * value, axis=1, keepdims=True) + epsilon)
    scaled = value * root
    column = jnp.sum(grad_normed * scaled, axis=0, keepdims=True)
    column = jnp.transpose(jnp.broadcast_to(column, (EXTRA, width)))
    lanes = lax.broadcasted_iota(jnp.int32, small.shape, 1)
    small[...] = jnp.where(lanes == GAIN_F, column, router_grad)
    grad_scaled = grad_normed * gains[GAIN_F : GAIN_F + 1]
    inner = jnp.mean(grad_scaled * scaled, axis=1, keepdims=True)
    result = grad_out[...].astype(f32) + root * (grad_scaled - scaled * inner)
    grad_middle[...] = result
    grad_round[...] = result.astype(bf16)


def attend_back_kernel(
    block,
    sizes,
    at_ref,
    own_ref,
    other_ref,
    mixed,
    out_weights,
    small_ref,
    qs,
    ks,
    vs,
    lse,
    seg_col,
    seg_row,
    cos_ref,
    sin_ref,
    hid,
    normed,
    weights,
    *refs,
):
    heads, kv_heads = sizes
    own, other, parts = refs[0], refs[1], refs[2:-6]
    acc, small, grads, whole, grad_mixed, out_acc = refs[-6:]
    me, core = at_ref[0], at_ref[1]
    length, width = hid.shape
    rows = own.shape[0]
    cols = grads.shape[1]
    whole[pl.ds(pl.multiple_of(core * rows, rows), rows)] = own_ref[...]
    whole[pl.ds(pl.multiple_of((1 - core) * rows, rows), rows)] = other_ref[...]
    grad_mixed[...] = lax.dot_general(
        whole[...], out_weights[...], NN, preferred_element_type=f32
    ).astype(bf16)
    out_acc[...] = lax.dot_general(whole[...], mixed[...], TN, preferred_element_type=f32)
    store_parts(out_acc, parts, me, block, cols + EXTRA)
    cosine, sine = cos_ref[...], -sin_ref[...]
    splits = row_splits(length)
    scale = 1.0 / math.sqrt(HD)
    per_group = heads // kv_heads
    bias = masks(seg_col[...], seg_row[...], splits)
    for kv_head in range(kv_heads):
        kv = slice(kv_head * HD, (kv_head + 1) * HD)
        grad_key = jnp.zeros((length, HD), f32)
        grad_value = jnp.zeros((length, HD), f32)
        for (low, high), mask in zip(splits, bias):
            key_sum = jnp.zeros((high, HD), f32)
            value_sum = jnp.zeros((high, HD), f32)
            for head in range(kv_head * per_group, (kv_head + 1) * per_group):
                at = slice(head * HD, (head + 1) * HD)
                query, grad = qs[low:high, at], grad_mixed[low:high, at]
                scores = lax.dot_general(query, ks[:high, kv], NT, preferred_element_type=f32)
                probs = jnp.exp(scores * scale + mask - lse[low:high, head : head + 1])
                grad_probs = lax.dot_general(
                    grad, vs[:high, kv], NT, preferred_element_type=f32
                )
                inner = jnp.sum(grad_probs * probs, axis=1, keepdims=True)
                grad_scores = (probs * (grad_probs - inner)).astype(bf16)
                grad_query = lax.dot_general(
                    grad_scores, ks[:high, kv], NN, preferred_element_type=f32
                )
                grads[low:high, at] = turn(
                    grad_query * scale, cosine[low:high], sine[low:high]
                ).astype(bf16)
                key_sum += lax.dot_general(grad_scores, query, TN, preferred_element_type=f32)
                value_sum += lax.dot_general(
                    probs.astype(bf16), grad, TN, preferred_element_type=f32
                )
            if high < length:
                pad = jnp.zeros((length - high, HD), f32)
                key_sum = jnp.concatenate([key_sum, pad], axis=0)
                value_sum = jnp.concatenate([value_sum, pad], axis=0)
            grad_key += key_sum
            grad_value += value_sum
        at = (heads + kv_head) * HD
        grads[:, at : at + HD] = turn(grad_key * scale, cosine, sine).astype(bf16)
        at += kv_heads * HD
        grads[:, at : at + HD] = grad_value.astype(bf16)
    acc[...] = lax.dot_general(normed[...], grads[...], TN, preferred_element_type=f32)
    store_parts(acc, parts, me, block, 0)
    value = hid[...].astype(f32)
    root = lax.rsqrt(jnp.mean(value * value, axis=1, keepdims=True) + epsilon)
    column = jnp.zeros((1, width), f32)
    for target, half in ((other, 1 - core), (own, core)):
        at = pl.ds(pl.multiple_of(half * rows, rows), rows)
        part = lax.dot_general(grads[at], weights[...], NT, preferred_element_type=f32)
        target[...] = part.astype(target.dtype)
        half_value = hid[at].astype(f32)
        half_root = lax.rsqrt(jnp.mean(half_value * half_value, axis=1, keepdims=True) + epsilon)
        column += jnp.sum(part * (half_value * half_root), axis=0, keepdims=True)
    lanes = lax.broadcasted_iota(jnp.int32, small.shape, 1)
    column = jnp.transpose(jnp.broadcast_to(column, (EXTRA, width)))
    small[...] = jnp.where(lanes == GAIN_A, column, small_ref[...])
    store_parts(small, parts, me, block, cols)


def slots_kernel(parts, at_ref, order_col, order_row, own, other, code, *refs):
    picks, rows_out, whole = refs[: len(parts)], refs[-2], refs[-1]
    core = at_ref[1]
    rows = own.shape[0]
    width = own.shape[1]
    whole[pl.ds(pl.multiple_of(core * rows, rows), rows), :width] = own[...]
    whole[pl.ds(pl.multiple_of((1 - core) * rows, rows), rows), :width] = other[...]
    whole[:, width:] = code[...]
    none = order_row.shape[0] // 2 * order_row.shape[1]
    first = core * sum(parts)
    for expert in range(order_row.shape[0]):
        row = order_row[expert : expert + 1, :]
        ahead = (order_col[:, expert : expert + 1] < row).astype(f32)
        position = jnp.sum(ahead, axis=0, keepdims=True).astype(jnp.int32)
        position = jnp.where(row < none, position, -1)
        low = first
        for pick, count in zip(picks, parts):
            slot = lax.broadcasted_iota(jnp.int32, (count, row.shape[1]), 0) + low
            pick[expert * count : (expert + 1) * count, :] = (slot == position).astype(bf16)
            low = low + count
    low = 0
    for pick, count in zip(picks, parts):
        taken = lax.dot_general(pick[...], whole[...], NN, preferred_element_type=f32)
        rows_out[:, low : low + count] = taken.astype(bf16).reshape(
            order_row.shape[0], count, whole.shape[1]
        )
        low += count


def take_kernel(at_ref, own, other, *refs):
    count = (len(refs) - 1) // 2
    picks, outs, whole = refs[:count], refs[count:-1], refs[-1]
    core = at_ref[1]
    rows = own.shape[0]
    whole[pl.ds(pl.multiple_of(core * rows, rows), rows)] = own[...]
    whole[pl.ds(pl.multiple_of((1 - core) * rows, rows), rows)] = other[...]
    for pick, out in zip(picks, outs):
        out[...] = lax.dot_general(
            pick[...], whole[...], NN, preferred_element_type=f32
        ).astype(bf16)


def give_kernel(count, at_ref, *refs):
    picks, values, (own, other) = refs[:count], refs[count:-2], refs[-2:]
    rows = own.shape[0]
    if len(values) < count:
        whole, values, low = values[0][...], [], 0
        for pick in picks:
            each = pick.shape[0] // whole.shape[0]
            values.append(whole[:, low : low + each].reshape(pick.shape[0], whole.shape[2]))
            low += each
    for target, half in ((other, 1 - at_ref[1]), (own, at_ref[1])):
        columns = pl.ds(pl.multiple_of(half * rows, rows), rows)
        total = None
        for pick, value in zip(picks, values):
            part = lax.dot_general(
                pick[:, columns], value[...], TN, preferred_element_type=f32
            )
            total = part if total is None else total + part
        target[...] = total.astype(target.dtype)


def gelu_parts(value):
    square = value * value
    inner = value * (0.7978845608028654 + 0.035677408136300125 * square)
    tanh = jnp.tanh(inner)
    half = 0.5 + 0.5 * tanh
    slope = half + 0.5 * value * (1.0 - tanh * tanh) * (
        0.7978845608028654 + 3.0 * 0.035677408136300125 * square
    )
    return value * half, slope


def moe_kernel(plan, at_ref, router_ref, x_in, g_in, *refs):
    copies, hidden, blocks, outer, first, groups = plan
    weight_count = len(set(c[0] for c in copies))
    if first:
        refs = refs[1:]
    sources, outs, refs = refs[:weight_count], refs[weight_count:][:5], refs[weight_count + 5 :]
    weights, xs, gs = refs[:3]
    buffers = refs[3:8]
    weight_sems, in_sems, out_sems = refs[8:]
    branch, gradn, act_all, gp_all, geo_all = buffers
    _, rows, width = xs.shape
    whole = 2 * hidden
    expert = at_ref[0] % CUBE

    weight_copies = []
    block_rows = weights.shape[0] // outer
    for number, (source, entry, low, length, offset, from_col, to_col, cols) in enumerate(copies):
        row = pl.multiple_of(((at_ref[0] // CUBE) ^ offset) * block_rows + low, 16)
        weight_copies.append(
            pltpu.make_async_copy(
                sources[source].at[entry, :, pl.ds(from_col, cols)],
                weights.at[pl.ds(row, length), pl.ds(to_col, cols)],
                weight_sems.at[number],
            )
        )
    weight_order = sorted(range(len(copies)), key=lambda k: copies[k][5] // hidden)
    in_copies = []
    for block in range(blocks):
        span = pl.ds(block * rows, rows)
        for kind, (source, target) in enumerate(((x_in, xs), (g_in, gs))):
            held = (span,)
            if kind == 1:
                held = pl.ds(block * groups, groups), pl.ds(first, rows // groups)
            in_copies.append(
                pltpu.make_async_copy(
                    source.at[held], target.at[block], in_sems.at[2 * block + kind]
                )
            )
    in_copies[0].start()
    for k in weight_order:
        weight_copies[k].start()
    for copy in in_copies[1:]:
        copy.start()
    out_copies = []
    for block in range(blocks):
        if block == 0:
            for copy in in_copies:
                copy.wait()
        x = xs[block]
        logits = lax.dot_general(x, router_ref[...], NN, preferred_element_type=f32)
        if block == 0:
            for k in weight_order:
                weight_copies[k].wait()
        pre = lax.dot_general(x, weights[:, : 2 * whole], NN, preferred_element_type=f32)
        both = gs[block].reshape(rows, gs.shape[3])
        routed = both[:, width:].astype(f32) > 0.5
        lanes = lax.broadcasted_iota(jnp.int32, routed.shape, 1)
        logits = jnp.where(routed, logits, -1e30)
        expo = jnp.where(routed, jnp.exp(logits - jnp.max(logits, axis=1, keepdims=True)), 0.0)
        total = jnp.sum(expo, axis=1, keepdims=True)
        gate = jnp.sum(jnp.where(lanes == expert, expo, 0.0), axis=1, keepdims=True)
        gate = gate / jnp.where(total > 0.0, total, 1.0)

        gate_pre, up_pre = pre[:, :whole], pre[:, whole:]
        gelu, slope = gelu_parts(gate_pre)
        act = (gelu * up_pre).astype(bf16)
        act_all[block] = act
        down = weights[:, 2 * whole :]
        expert_out = lax.dot_general(act, down, NT, preferred_element_type=f32)
        branch[block] = (gate * expert_out).astype(bf16).reshape(branch.shape[1:])
        g = both[:, :width].astype(f32)
        grad_gate = jnp.sum(g * expert_out, axis=1, keepdims=True)
        gradn[block, :, width:] = jnp.where(lanes == expert, grad_gate, 0.0).astype(bf16)
        geo = (gate * g).astype(bf16)
        geo_all[block] = geo
        grad_act = lax.dot_general(geo, down, NN, preferred_element_type=f32)
        grad_gate_pre = (grad_act * up_pre * slope).astype(bf16)
        grad_up_pre = (grad_act * gelu).astype(bf16)
        for side in range(2):
            cols = slice(side * hidden, (side + 1) * hidden)
            for kind, part in enumerate((grad_gate_pre, grad_up_pre)):
                at = (2 * side + kind) * hidden
                gp_all[block, :, at : at + hidden] = part[:, cols]
        grad_in = lax.dot_general(
            grad_gate_pre, weights[:, :whole], NT, preferred_element_type=f32
        ) + lax.dot_general(
            grad_up_pre, weights[:, whole : 2 * whole], NT, preferred_element_type=f32
        )
        gradn[block, :, :width] = grad_in.astype(bf16)
        for number, (source, target) in enumerate(zip(buffers, outs)):
            if number == 0:
                held = pl.ds(block * groups, groups), pl.ds(first, rows // groups)
            else:
                held = (pl.ds(block * rows, rows),)
            copy = pltpu.make_async_copy(
                source.at[block], target.at[held], out_sems.at[5 * block + number]
            )
            copy.start()
            out_copies.append(copy)
    for copy in out_copies:
        copy.wait()


def moe(at, x, g, router, pieces, hidden, outer, sequences, capacity, branch=None):
    copies = []
    for source, (array, first, low, side) in enumerate(pieces):
        for entry in range(array.shape[0]):
            for kind in range(3):
                copies.append(
                    (source, entry, low, array.shape[1], first + entry, kind * hidden)
                    + ((2 * kind + side) * hidden, hidden)
                )
    total, width = x.shape
    blocks = 2
    rows = total // blocks
    widths = (width, width + EXTRA, 2 * hidden, 4 * hidden, width)
    each = total // sequences
    first = 0 if branch is None else capacity - each
    args = [x, g] + ([] if branch is None else [branch]) + [p[0] for p in pieces]
    groups = sequences // blocks
    buffers = [(blocks, rows, w) for w in widths]
    buffers[0] = (blocks, groups, each, width)
    return pl.pallas_call(
        functools.partial(moe_kernel, (copies, hidden, blocks, outer, first, groups)),
        out_shape=[jax.ShapeDtypeStruct((sequences, capacity, width), bf16)]
        + [jax.ShapeDtypeStruct((total, w), bf16) for w in widths[1:]],
        in_specs=[pl.BlockSpec(memory_space=pltpu.SMEM), pl.BlockSpec(memory_space=pltpu.VMEM)]
        + [pl.BlockSpec(memory_space=pl.ANY)] * len(args),
        out_specs=[pl.BlockSpec(memory_space=pl.ANY)] * 5,
        scratch_shapes=[
            pltpu.VMEM((width, 6 * hidden), bf16),
            pltpu.VMEM((blocks, rows, width), bf16),
            pltpu.VMEM((blocks, groups, each, width + EXTRA), bf16),
        ]
        + [pltpu.VMEM(dims, bf16) for dims in buffers]
        + [
            pltpu.SemaphoreType.DMA((len(copies),)),
            pltpu.SemaphoreType.DMA((2 * blocks,)),
            pltpu.SemaphoreType.DMA((5 * blocks,)),
        ],
        input_output_aliases={} if branch is None else {4: 0},
        compiler_params=pltpu.CompilerParams(vmem_limit_bytes=60 * 1024 * 1024),
        cost_estimate=BRIEF,
        name="experts",
    )(at, router, *args)


def weight_grads_kernel(calls, at_ref, *refs):
    pairs = []
    for _ in range(2):
        pairs.append((refs[:calls], refs[calls : 2 * calls]))
        refs = refs[2 * calls :]
    own, other, *buffers, sems = refs
    cols = buffers[0].shape[1]
    columns = pl.ds(pl.multiple_of(at_ref[2] * cols, cols), cols)
    copies = []
    for number, (lefts, rights) in enumerate(pairs):
        row = 0
        for left, right in zip(lefts, rights):
            rows = pl.ds(row, left.shape[0])
            for source, target in (
                (left.at[:, columns], buffers[2 * number].at[rows]),
                (right, buffers[2 * number + 1].at[rows]),
            ):
                copies.append(pltpu.make_async_copy(source, target, sems.at[len(copies)]))
                copies[-1].start()
            row += left.shape[0]
    at = 0
    for number in range(2):
        for copy in copies[2 * calls * number : 2 * calls * (number + 1)]:
            copy.wait()
        total = lax.dot_general(
            buffers[2 * number][...],
            buffers[2 * number + 1][...],
            TN,
            preferred_element_type=f32,
        ).astype(bf16)
        width = total.shape[1] // 2
        own[:, at : at + width] = total[:, :width]
        other[:, at : at + width] = total[:, width:]
        at += width


def weight_grads(at, half, pre, down):
    args, scratch, width = [], [], 0
    for pairs in (pre, down):
        args += [p[0] for p in pairs] + [p[1] for p in pairs]
        rows = sum(p[0].shape[0] for p in pairs)
        left, right = pairs[0][0].shape[1] // 2, pairs[0][1].shape[1]
        scratch += [(rows, left), (rows, right)]
        width += right // 2
    return pl.pallas_call(
        functools.partial(weight_grads_kernel, len(pre)),
        out_shape=[jax.ShapeDtypeStruct((left, width), bf16)] * 2,
        in_specs=[pl.BlockSpec(memory_space=pltpu.SMEM)]
        + [pl.BlockSpec(memory_space=pl.ANY)] * len(args),
        out_specs=[pl.BlockSpec(memory_space=pltpu.VMEM)] * 2,
        scratch_shapes=[pltpu.VMEM(dims, bf16) for dims in scratch]
        + [pltpu.SemaphoreType.DMA((len(args),))],
        compiler_params=pltpu.CompilerParams(vmem_limit_bytes=60 * 1024 * 1024),
        cost_estimate=FREE,
        name="weight_grads",
    )(jnp.concatenate([at, half.reshape(1)]), *args)


def per_device(
    count,
    hidden_in,
    segment_ids,
    routes,
    slot_order,
    gain_attn,
    w_query,
    w_key,
    w_value,
    w_out,
    gain_ffn,
    w_router,
    w_gate,
    w_up,
    w_down,
    grad_out,
):
    tok_rows, width = hidden_in.shape
    seq_len = segment_ids.shape[0]
    top_count = routes.shape[1]
    experts, block, hidden = w_gate.shape
    capacity = 9 * seq_len * top_count // (8 * experts)
    me = lax.axis_index("dp").astype(jnp.int32)
    core = lax.axis_index("tensor").astype(jnp.int32)
    at = jnp.stack([me, core])
    groups = [list(range(first, first + CUBE)) for first in range(0, count, CUBE)]
    heads_cols, kv_cols = w_query.shape[1], w_key.shape[1]
    qkv_cols = heads_cols + 2 * kv_cols
    heads, kv_heads = heads_cols // HD, kv_cols // HD

    def shape(rows, cols, dtype=bf16):
        return jax.ShapeDtypeStruct((rows, cols), dtype)

    def near(own):
        return {0: own} | {bit: swap(own, bit, count) for bit in NEAR}

    def far(got):
        spans = halves(got[0].shape[0])
        return got | {
            3: swap(cut(got[2], spans[0], 0), 1, count),
            9: swap(cut(got[1], spans[1], 0), 2, count),
            6: swap(got[4], 2, count),
            5: swap(got[4], 1, count),
        }

    def last(got):
        spans = halves(got[0].shape[0])
        return got | {
            7: swap(cut(got[6], spans[0], 0), 1, count),
            8: swap(cut(got[5], spans[1], 0), 2, count),
        }

    small = jnp.concatenate([w_router, gain_attn[:, None], gain_ffn[:, None]], axis=1)
    small = jnp.pad(small, ((0, 0), (0, EXTRA - small.shape[1])))
    pair = outer_pair(
        jnp.concatenate([w_query, w_key, w_value, small, w_out.T], axis=1), count
    )
    hidden_other = swap_core(hidden_in)

    expert_shard = jnp.concatenate([w_gate, w_up, jnp.swapaxes(w_down, 1, 2)], axis=2)
    expert_rows = lax.all_to_all(
        expert_shard.reshape(experts * block, 3 * hidden),
        "dp",
        0,
        0,
        tiled=True,
        axis_index_groups=groups,
    )

    order = jnp.min(
        jnp.where(
            routes[:, :, None] == jnp.arange(experts, dtype=jnp.int32),
            slot_order[0].reshape(seq_len, top_count)[:, :, None],
            seq_len * top_count,
        ),
        axis=1,
    )
    code = (order < seq_len * top_count).astype(bf16)
    code = jnp.pad(code, ((0, 0), (0, EXTRA - experts)))
    code_own = lax.dynamic_slice_in_dim(code, core * tok_rows, tok_rows, 0)
    first_part = capacity // 4 // 16 * 16
    slot_parts = (first_part, capacity // 2 - first_part)
    grad_other = swap_core(grad_out)
    slots = vmem_call(
        functools.partial(slots_kernel, slot_parts),
        [shape(experts * part, seq_len) for part in slot_parts]
        + [jax.ShapeDtypeStruct((experts, sum(slot_parts), width + EXTRA), bf16)],
        [pltpu.VMEM((seq_len, width + EXTRA), bf16)],
        [(at, 1), (order, 0), (order.T, 0), (grad_out, 0), (grad_other, 0), (code, 0)],
        "slots",
    )
    picks, grad_rows = slots[:2], slots[2]

    def exchange(rows):
        return lax.all_to_all(rows, "dp", 0, 0, tiled=True, axis_index_groups=groups)

    cosine, sine_table = rope_tables(seq_len, HD)
    cosine = jnp.concatenate([cosine, cosine], axis=1)
    sine_table = jnp.concatenate([-sine_table, sine_table], axis=1)
    seg_col, seg_row = segment_ids[:, None], segment_ids[None, :]

    pair, expert_rows, code_own = gate(
        [pair, expert_rows, code_own], cosine, sine_table, hidden_other, grad_other
    )
    if count == 2 * CUBE:
        edges = [expert_rows.shape[0] * k // 48 // 16 * 16 for k in (0, 10, 26, 26, 37, 48)]
    else:
        edges = [0] * 5 + [expert_rows.shape[0]]
    pieces = [(expert_rows[None], 0, 0, 0), (swap_core(expert_rows)[None], 0, 0, 1)]

    def outer_chunk(k, *events):
        low, high = edges[k], edges[k + 1]
        if high == low:
            return [], []
        (chunk,) = gate([cut(expert_rows, (low, high), 0)], *events)
        arrays, first, swapped = outer_gather(chunk, count)[1:], 1, []
        for array in arrays:
            swapped.append(swap_core(array))
            pieces.append((array, first, low, 0))
            pieces.append((swapped[-1], first, low, 1))
            first += array.shape[0]
        return arrays, swapped

    with jax.named_scope("weights_near"):
        got = near(pair)
    arrays, swapped = outer_chunk(0, pair)
    got = gate_dict(got, NEAR, grad_rows, arrays, pieces[1][0])
    with jax.named_scope("weights_far"):
        got = far(got)
    arrays, swapped_next = outer_chunk(1, got[1])
    got = gate_dict(got, FAR, arrays, swapped)
    with jax.named_scope("weights_last"):
        got = last(got)
    arrays, swapped = outer_chunk(2, got[3])
    got = gate_dict(got, LAST, arrays, swapped_next)
    sources, copies = piece_copies(got, block, me, count)
    grad_rows, seg_col = gate([grad_rows, seg_col], got[7])
    with jax.named_scope("grads_rows"):
        grad_rows = exchange(grad_rows)
    attended = vmem_call(
        functools.partial(attend_kernel, copies, (heads, kv_heads, len(sources))),
        [
            shape(seq_len, width),
            shape(seq_len, width),
            shape(seq_len, heads_cols),
            shape(seq_len, kv_cols),
            shape(seq_len, kv_cols),
            shape(seq_len, heads_cols),
            shape(seq_len, HD, f32),
            shape(width, qkv_cols),
            shape(width, EXTRA),
            shape(width, heads_cols),
            shape(16, width, f32),
            shape(tok_rows, width, f32),
            shape(tok_rows, width),
        ],
        [pltpu.SemaphoreType.DMA((3 * len(copies),))],
        [(at, 1), (hidden_in, 0), (hidden_other, 0), (seg_col, 0), (seg_row, 0)]
        + [(cosine, 0), (sine_table, 0)]
        + [(piece, 2) for piece in sources],
        "attend",
        flops=2 * seq_len * (width * (qkv_cols + heads_cols) + heads_cols * seq_len),
    )
    hid, normed, qs, ks, vs, mixed, lse, full_qkv, router, out_wt, gains = attended[:-2]
    attn_own, attn_other = attended[-2:]
    arrays, swapped_next = outer_chunk(3, got[7])
    middle, normed2 = vmem_call(
        middle_kernel,
        [shape(tok_rows, width, f32), shape(tok_rows, width)],
        [],
        [(hidden_in, 0), (attn_own, 0), (swap_core(attn_other), 0), (gains, 0)],
        "middle",
    )

    rows = vmem_call(
        take_kernel,
        [shape(experts * part, width) for part in slot_parts],
        [pltpu.VMEM((seq_len, width), bf16)],
        [(at, 1), (normed2, 0), (swap_core(normed2), 0)] + [(pick, 0) for pick in picks],
        "take",
    )
    rows = list(rows)
    rows[0], grad_rows = gate([rows[0], grad_rows], arrays, swapped)
    with jax.named_scope("tokens_rows"):
        x_first = exchange(rows[0])
    arrays, _ = outer_chunk(4, rows[0])
    x_first, rows_second = gate([x_first, rows[1]], arrays, swapped_next)
    with jax.named_scope("tokens_rows"):
        x_second = exchange(rows_second)

    def experts_on(x, g, router, branch=None):
        held = (CUBE, sum(slot_parts))
        return moe(at, x, g, router, pieces, hidden, count // CUBE, *held, branch)

    branch, gradn_first, *first = experts_on(x_first, grad_rows, router)
    with jax.named_scope("gradn_rows"):
        gradn_first = exchange(gradn_first)
    (second_router,) = gate([router], first[0])
    branch, gradn_second, *second = experts_on(x_second, grad_rows, second_router, branch)

    xs = (x_first, x_second)
    pre_pairs = [(x, call[1]) for x, call in zip(xs, (first, second))]
    down_pairs = [(call[2], call[0]) for call in (first, second)]
    bits = outer_bits(count)
    top = (me // bits[-1]) % 2 if bits else jnp.zeros((), jnp.int32)

    def half_grads(half, *events):
        half = gate([half.reshape(1)], *events)[0]
        return weight_grads(at, half, pre_pairs, down_pairs)

    with jax.named_scope("gradn_rows"):
        gradn_second = exchange(gradn_second)
    sent, sent_other = half_grads(1 - top, second[0])
    keep, keep_other = half_grads(top, sent_other)
    with jax.named_scope("expert_scatter"):
        sent = add_round(sent, swap_core(sent_other))
        sent_got = swap(sent, bits[-1], count) if bits else sent

    def give(picks, values, name):
        own, other = vmem_call(
            functools.partial(give_kernel, len(picks)),
            [shape(tok_rows, values[0].shape[-1], f32), shape(tok_rows, values[0].shape[-1])],
            [],
            [(at, 1)] + [(pick, 0) for pick in picks] + [(value, 0) for value in values],
            name,
        )
        return own, swap_core(other)

    gradn_second, gradn_first = gate([gradn_second, gradn_first], sent, keep)
    gradn = list(give(picks, (gradn_first, gradn_second), "give_gradn"))

    grad_middle, grad_mid_r, small_f = vmem_call(
        middle_back_kernel,
        [shape(tok_rows, width, f32), shape(tok_rows, width), shape(width, EXTRA, f32)],
        [],
        [(middle, 0), (normed2, 0), (grad_out, 0), (code_own, 0), (router, 0), (gains, 0)]
        + [(array, 0) for array in gradn],
        "middle_back",
    )

    grad_mid_other = swap_core(grad_mid_r)
    (branch,) = gate([branch], gradn_second)
    with jax.named_scope("branch_rows"):
        branch = exchange(branch)
    normed_own, normed_other, *parts = vmem_call(
        functools.partial(attend_back_kernel, block, (heads, kv_heads)),
        [shape(tok_rows, width, f32), shape(tok_rows, width)]
        + part_shapes(count, block, qkv_cols + EXTRA + heads_cols),
        [
            pltpu.VMEM((width, qkv_cols), f32),
            pltpu.VMEM((width, EXTRA), f32),
            pltpu.VMEM((seq_len, qkv_cols), bf16),
            pltpu.VMEM((seq_len, width), bf16),
            pltpu.VMEM((seq_len, heads_cols), bf16),
            pltpu.VMEM((width, heads_cols), f32),
        ],
        [(at, 1), (grad_mid_r, 0), (grad_mid_other, 0), (mixed, 0), (out_wt, 0)]
        + [(small_f, 0), (qs, 0), (ks, 0), (vs, 0), (lse, 0), (seg_col, 0)]
        + [(seg_row, 0), (cosine, 0), (sine_table, 0), (hid, 0), (normed, 0), (full_qkv, 0)],
        "attend_back",
        flops=4 * seq_len * (width * (qkv_cols + heads_cols) + 2 * heads_cols * seq_len),
    )
    parts = spread_parts(parts, me, count)

    keep_swapped = swap_core(keep_other)
    parts = gate_dict(parts, (3, 9) + LAST, keep_swapped)
    with jax.named_scope("attn_last"):
        got = sum_last(parts, count)
    normed_swapped = swap_core(normed_other)
    gated = gate([got[7], got[8], parts[3], parts[9]], normed_swapped)
    got, parts[3], parts[9] = dict(zip(LAST, gated)), gated[2], gated[3]
    with jax.named_scope("attn_far"):
        terms = far_terms(parts, got)
        attn_far = sum_far(parts, terms, count)
    with jax.named_scope("expert_scatter"):
        sent_got, keep = gate([sent_got, keep], terms)
        if bits:
            total = keep.astype(f32) + keep_swapped.astype(f32) + sent_got.astype(f32)
        else:
            total = jnp.concatenate([add_round(keep, keep_swapped), sent_got]).astype(f32)
        for bit in reversed(bits[:-1]):
            half = total.shape[0] // 2
            high = (me // bit) % 2
            mine = lax.dynamic_slice_in_dim(total, high * half, half, 0)
            other = lax.dynamic_slice_in_dim(total, (1 - high) * half, half, 0)
            total = mine + swap(other.astype(bf16), bit, count).astype(f32)
        total = total.astype(bf16)
    grad_normed = normed_own + normed_swapped.astype(f32)
    gated = gate([attn_far[k] for k in FAR] + [branch, total])
    attn_far, branch, total = dict(zip(FAR, gated)), gated[4], gated[5]
    with jax.named_scope("attn_near"):
        attn_near = sum_near(near_terms(parts, attn_far), count)
    branch_own, branch_other = give(picks, (branch,), "give_branch")
    with jax.named_scope("expert_scatter"):
        total = exchange(total)
    attn_near = gate_dict(attn_near, NEAR, branch_own)
    with jax.named_scope("attn_outer"):
        attn_grads = outer_sum(sum_own(parts, attn_near), count)
    layer_out = middle + branch_own + branch_other.astype(f32)

    expert_grads = total.reshape(experts, block, 3 * hidden).astype(f32)
    grad_gate_w = expert_grads[:, :, :hidden]
    grad_up_w = expert_grads[:, :, hidden : 2 * hidden]
    grad_down_w = jnp.swapaxes(expert_grads[:, :, 2 * hidden :], 1, 2)
    scaled_in, root_in = rms_parts(hidden_in.astype(f32))
    grad_in = grad_middle + norm_backward(grad_normed, scaled_in, root_in, gains[GAIN_A])
    smalls = attn_grads[:, qkv_cols : qkv_cols + EXTRA]
    smalls = smalls + swap_core(smalls)
    return (
        layer_out,
        grad_in,
        smalls[:, GAIN_A],
        attn_grads[:, :heads_cols],
        attn_grads[:, heads_cols : heads_cols + kv_cols],
        attn_grads[:, heads_cols + kv_cols : qkv_cols],
        attn_grads[:, qkv_cols + EXTRA :].T,
        smalls[:, GAIN_F],
        smalls[:, :experts],
        grad_gate_w,
        grad_up_w,
        grad_down_w,
    )


def solution(mesh):
    return jax.shard_map(
        functools.partial(per_device, mesh.shape["dp"]),
        mesh=mesh,
        in_specs=(
            P(("dp", "tensor"), None),
            P("dp"),
            P("dp", None),
            P("dp", None),
            P("dp"),
            P("dp", "tensor"),
            P("dp", "tensor"),
            P("dp", "tensor"),
            P("tensor", "dp"),
            P("dp"),
            P("dp", None),
            P(None, "dp", "tensor"),
            P(None, "dp", "tensor"),
            P(None, "tensor", "dp"),
            P(("dp", "tensor"), None),
        ),
        out_specs=(
            P(("dp", "tensor"), None),
            P(("dp", "tensor"), None),
            P("dp"),
            P("dp", "tensor"),
            P("dp", "tensor"),
            P("dp", "tensor"),
            P("tensor", "dp"),
            P("dp"),
            P("dp", None),
            P(None, "dp", "tensor"),
            P(None, "dp", "tensor"),
            P(None, "tensor", "dp"),
        ),
        check_vma=False,
    )
```
